256 devices in a mesh: pipe: 4 (over y), row: 16 (over z, core), col: 4 (over x).
Axes of the slice: x: 4, y: 4, z: 8, core: 2. Of those that a mesh axis runs over, the one named last changes fastest.
Arguments:
- activations: bfloat16 [4, 128, 64, 512], P('pipe', 'row', 'col'), may hold values from -6 to 6
- qkv_weight: bfloat16 [4, 512, 1536], P('pipe'), may hold values from -9 to 9
- out_weight: bfloat16 [4, 512, 512], P('pipe'), may hold values from -0.25 to 0.25
- cotangent: float32 [128, 64, 512], P('row', 'col'), may hold values from -6 to 6
Outputs:
- input_grads: float32 [4, 128, 64, 512], P('pipe', 'row', 'col')
- qkv_grads: float32 [4, 512, 1536], P('pipe', ('row', 'col'))
- out_grads: float32 [4, 512, 512], P('pipe', ('row', 'col'))
The draws below stay inside these ranges and needn't reach their ends.
All inputs are finite; a program needn't handle non-finite values.
Results may differ from the reference program's by a relative error of at most 0.015.
Values may be sent and summed in bfloat16 or wider, within the bound.
No kernel may reach another device: no remote copies, remote signals or barrier semaphores. Data moves between devices by JAX's collectives and lax.ppermute only.
A program may use at most 128 MiB of HBM per device.

```python
import jax
import jax.numpy as jnp
from jax import lax

D = 512
H = 8
SECTIONS = 4
GR = 128
GC = 64
TOKENS = 8192


def draw_qkv_weight(key, part):
    key = jax.random.fold_in(key, 11)
    base_key = jax.random.fold_in(key, 0)
    base = jnp.clip(jax.random.normal(base_key, (SECTIONS, D, 3 * D), jnp.float32), -5.0, 5.0) * D ** (-0.5)
    return jnp.clip(base, -8.5, 8.5).astype(jnp.bfloat16)


def level_of(key, dims, pieces, low, high):
    loudness, own = 1.0, jax.random.fold_in(key, 6)
    for axis_at, blocks in pieces:
        heights = jnp.exp(jax.random.uniform(jax.random.fold_in(own, axis_at), (blocks,), jnp.float32, low / len(pieces), high / len(pieces)))
        loudness = loudness * jnp.repeat(heights, dims[axis_at] // blocks).reshape([-1 if axis == axis_at else 1 for axis in range(len(dims))])
    return loudness


def bell_draw(own_key, shape, width, most, pieces=(), held_as=jnp.bfloat16):
    level = level_of(own_key, shape, pieces, -0.22, 0.18) if pieces else 1.0
    result = jax.random.normal(own_key, shape, jnp.float32) * width * level
    return jnp.minimum(jnp.maximum(result, -most), most).astype(held_as)


def setup_inputs(seed: int = 0) -> dict:
    arg_keys = jax.random.split(jax.random.key(seed), 5)
    return {
        "activations": bell_draw(arg_keys[0], (SECTIONS, GR, GC, D), 1.0, 6.0, ((0, 4), (1, 16), (2, 4))),
        "qkv_weight": draw_qkv_weight(jax.random.fold_in(arg_keys[4], 71), 0),
        "out_weight": bell_draw(arg_keys[2], (SECTIONS, D, D), D ** -0.5, 0.25, ((0, 4),)),
        "cotangent": bell_draw(arg_keys[3], (GR, GC, D), 1.0, 6.0, ((0, 16), (1, 4)), jnp.float32),
    }


def product(form, left, right):
    return jnp.einsum(form, left.astype(jnp.float32), right.astype(jnp.float32))

def split_tiles(source, head_count):
    height, breadth, features = source.shape
    head_size = features // head_count
    shaped = source.reshape(height // 8, 8, breadth // 16, 16, head_count, head_size)
    return shaped.transpose(0, 2, 4, 1, 3, 5).reshape(height // 8, breadth // 16, head_count, 128, head_size)

def join_tiles(tiled_array, height, breadth):
    head_count = tiled_array.shape[2]
    head_size = tiled_array.shape[4]
    shaped = tiled_array.reshape(height // 8, breadth // 16, head_count, 8, 16, head_size)
    return shaped.transpose(0, 3, 1, 4, 2, 5).reshape(height, breadth, head_count * head_size)

def split_stats(stats):
    height, breadth, head_count = stats.shape
    shaped = stats.reshape(height // 8, 8, breadth // 16, 16, head_count)
    return shaped.transpose(0, 2, 4, 1, 3).reshape(height // 8, breadth // 16, head_count, 128)

def join_stats(tiled_array, height, breadth):
    head_count = tiled_array.shape[2]
    shaped = tiled_array.reshape(height // 8, breadth // 16, head_count, 8, 16)
    return shaped.transpose(0, 3, 1, 4, 2).reshape(height, breadth, head_count)

def regions(padded):
    height, breadth, features = padded.shape
    row_tiles = (height - 16) // 8
    col_tiles = (breadth - 16) // 16
    blocks = padded.reshape(row_tiles + 2, 8, breadth, features)
    stacked = jnp.concatenate([blocks[:row_tiles], blocks[1:row_tiles + 1], blocks[2:]], axis=1)
    strips = stacked.reshape(row_tiles, 24, col_tiles + 1, 16, features)
    spread = jnp.concatenate([strips[:, :, :col_tiles], strips[:, :, 1:]], axis=3)
    return spread.transpose(0, 2, 1, 3, 4).reshape(row_tiles, col_tiles, 768, features)

def window_mask(row_tiles, col_tiles, row_start, col_start, row_total, col_total, keys_inside):
    inside = jnp.arange(128, dtype=jnp.int32)
    region_pos = jnp.arange(768, dtype=jnp.int32)
    tile_row = inside // 16
    tile_col = inside % 16
    region_row = region_pos // 32 - 8
    region_col = region_pos % 32 - 8
    if keys_inside:
        step_row = tile_row[:, None] - region_row[None, :]
        step_col = tile_col[:, None] - region_col[None, :]
    else:
        step_row = region_row[None, :] - tile_row[:, None]
        step_col = region_col[None, :] - tile_col[:, None]
    within = (step_row >= -8) & (step_row <= 7) & (step_col >= -8) & (step_col <= 7)
    base_row = row_start + 8 * jnp.arange(row_tiles, dtype=jnp.int32)
    base_col = col_start + 16 * jnp.arange(col_tiles, dtype=jnp.int32)
    grid_row = base_row[:, None] + region_row[None, :]
    grid_col = base_col[:, None] + region_col[None, :]
    row_valid = (grid_row >= 0) & (grid_row < row_total)
    col_valid = (grid_col >= 0) & (grid_col < col_total)
    return within[None, None, None] & row_valid[:, None, None, None, :] & col_valid[None, :, None, None, :]

def attend(queries, key_value_rim, query_mask, head_count):
    height, breadth, features = queries.shape
    head_size = features // head_count
    scaling = head_size ** (-0.5)
    tile_query = split_tiles(queries, head_count)
    row_tiles, col_tiles = (tile_query.shape[0], tile_query.shape[1])
    region_all = regions(key_value_rim)
    key_part = region_all[..., :features].reshape(row_tiles, col_tiles, 768, head_count, head_size)
    value_part = region_all[..., features:].reshape(row_tiles, col_tiles, 768, head_count, head_size)
    scores = product('abhqe,abkhe->abhqk', tile_query, key_part) * scaling
    scores = jnp.where(query_mask, scores, -1e+30)
    highest = lax.optimization_barrier(jnp.max(scores, axis=-1, keepdims=True))
    summed = lax.optimization_barrier(jnp.sum(jnp.where(query_mask, jnp.exp(scores - highest), 0.0), axis=-1, keepdims=True))
    log_total = highest + jnp.log(summed)
    weights = jnp.where(query_mask, jnp.exp(scores - log_total), 0.0).astype(jnp.bfloat16)
    mixed = product('abhqk,abkhe->abhqe', weights, value_part).astype(jnp.bfloat16)
    return (join_tiles(mixed, height, breadth), join_stats(log_total[..., 0], height, breadth))

def query_grads(queries, d_mixed, log_total, row_delta, key_value_rim, query_mask, head_count):
    height, breadth, features = queries.shape
    head_size = features // head_count
    scaling = head_size ** (-0.5)
    tile_query = split_tiles(queries, head_count)
    tile_grad = split_tiles(d_mixed, head_count)
    row_tiles, col_tiles = (tile_query.shape[0], tile_query.shape[1])
    region_all = regions(key_value_rim)
    key_part = region_all[..., :features].reshape(row_tiles, col_tiles, 768, head_count, head_size)
    value_part = region_all[..., features:].reshape(row_tiles, col_tiles, 768, head_count, head_size)
    scores = product('abhqe,abkhe->abhqk', tile_query, key_part) * scaling
    weights = jnp.where(query_mask, jnp.exp(scores - split_stats(log_total)[..., None]), 0.0)
    pressure = product('abhqe,abkhe->abhqk', tile_grad, value_part)
    slopes = (weights * (pressure - split_stats(row_delta)[..., None])).astype(jnp.bfloat16)
    d_query = scaling * product('abhqk,abkhe->abhqe', slopes, key_part)
    return join_tiles(d_query, height, breadth)

def key_grads(key_part, value_part, query_rim, grad_rim, stat_rim, key_mask, head_count):
    height, breadth, features = key_part.shape
    head_size = features // head_count
    scaling = head_size ** (-0.5)
    tile_key = split_tiles(key_part, head_count)
    tile_value = split_tiles(value_part, head_count)
    row_tiles, col_tiles = (tile_key.shape[0], tile_key.shape[1])
    reach_query = regions(query_rim).reshape(row_tiles, col_tiles, 768, head_count, head_size)
    reach_grad = regions(grad_rim).reshape(row_tiles, col_tiles, 768, head_count, head_size)
    reach_stats = regions(stat_rim).transpose(0, 1, 3, 2)
    reach_total = reach_stats[:, :, :head_count][:, :, :, None, :]
    reach_delta = reach_stats[:, :, head_count:][:, :, :, None, :]
    scores = product('abhke,abqhe->abhkq', tile_key, reach_query) * scaling
    weights = jnp.where(key_mask, jnp.exp(scores - reach_total), 0.0)
    pressure = product('abhke,abqhe->abhkq', tile_value, reach_grad)
    slopes = (weights * (pressure - reach_delta)).astype(jnp.bfloat16)
    d_value = product('abhkq,abqhe->abhke', weights.astype(jnp.bfloat16), reach_grad)
    d_key = scaling * product('abhkq,abqhe->abhke', slopes, reach_query)
    return (join_tiles(d_key, height, breadth), join_tiles(d_value, height, breadth))

def section_backward(source, weight_in, weight_back, gradient):
    height, breadth, features = source.shape
    head_count = H
    row_tiles, col_tiles = (height // 8, breadth // 16)
    query_mask = window_mask(row_tiles, col_tiles, 0, 0, height, breadth, False)
    key_mask = window_mask(row_tiles, col_tiles, 0, 0, height, breadth, True)
    floated = source.astype(jnp.float32)
    inverse = lax.rsqrt(lax.optimization_barrier(jnp.mean(floated * floated, axis=-1, keepdims=True)) + 1e-06)
    normed = floated * inverse
    normed_low = normed.astype(jnp.bfloat16)
    projected = jnp.dot(normed_low.reshape(-1, features), weight_in, preferred_element_type=jnp.float32).astype(jnp.bfloat16).reshape(height, breadth, 3 * features)
    padded = jnp.pad(projected, ((8, 8), (8, 8), (0, 0)))
    mixed, log_total = attend(projected[:, :, :features], padded[:, :, features:], query_mask, head_count)
    grad_low = gradient.astype(jnp.bfloat16)
    d_mixed = jnp.dot(grad_low.reshape(-1, features), weight_back.T, preferred_element_type=jnp.float32).astype(jnp.bfloat16).reshape(height, breadth, features)
    row_delta = lax.optimization_barrier(jnp.sum((d_mixed.astype(jnp.float32) * mixed.astype(jnp.float32)).reshape(height, breadth, head_count, -1), axis=-1))
    grad_rim = jnp.pad(d_mixed, ((8, 8), (8, 8), (0, 0)))
    stat_rim = jnp.pad(jnp.concatenate([log_total, row_delta], axis=-1), ((8, 8), (8, 8), (0, 0)))
    d_query = query_grads(projected[:, :, :features], d_mixed, log_total, row_delta, padded[:, :, features:], query_mask, head_count)
    d_key, d_value = key_grads(projected[:, :, features:2 * features], projected[:, :, 2 * features:], padded[:, :, :features], grad_rim, stat_rim, key_mask, head_count)
    d_projected = jnp.concatenate([d_query, d_key, d_value], axis=-1).astype(jnp.bfloat16)
    d_normed = jnp.dot(d_projected.reshape(-1, 3 * features), weight_in.T, preferred_element_type=jnp.float32).reshape(height, breadth, features)
    inner = lax.optimization_barrier(jnp.mean(d_normed * normed, axis=-1, keepdims=True))
    d_input = gradient + inverse * (d_normed - normed * inner)
    qkv_part = jnp.dot(normed_low.reshape(-1, features).T, d_projected.reshape(-1, 3 * features), preferred_element_type=jnp.float32)
    out_part = jnp.dot(mixed.reshape(-1, features).T, grad_low.reshape(-1, features), preferred_element_type=jnp.float32)
    return (d_input, qkv_part, out_part)

def reference(activations, qkv_weight, out_weight, cotangent):
    gradient = cotangent
    input_list = []
    qkv_list = []
    out_list = []
    for section in range(SECTIONS - 1, -1, -1):
        d_input, qkv_part, out_part = section_backward(activations[section], qkv_weight[section], out_weight[section], gradient)
        input_list.insert(0, d_input)
        qkv_list.insert(0, qkv_part)
        out_list.insert(0, out_part)
        gradient = d_input
    scaling = TOKENS ** (-0.5)
    return (jnp.stack(input_list), jnp.stack(qkv_list) * scaling, jnp.stack(out_list) * scaling)
```

```python
import functools

import jax
import jax.numpy as jnp
import numpy as np
from jax import lax
from jax.experimental import pallas as pl
from jax.experimental.pallas import tpu as pltpu
from jax.sharding import Mesh
from jax.sharding import PartitionSpec as P

F32 = jnp.float32
BF16 = jnp.bfloat16
AXES = ("pipe", "z", "core", "col")
D = 512
PAIRS = 4
TOK = 128
OWN = 256
REGION = 768
VMEM_LIMIT = 40 * 1024 * 1024


def nn(a, b):
    return lax.dot_general(a, b, (((1,), (0,)), ((), ())), preferred_element_type=F32)


def nt(a, b):
    return lax.dot_general(a, b, (((1,), (1,)), ((), ())), preferred_element_type=F32)


def tn(a, b):
    return lax.dot_general(a, b, (((0,), (0,)), ((), ())), preferred_element_type=F32)


def two_heads(block):
    lane = lax.broadcasted_iota(jnp.int32, block.shape, 1)
    zero = jnp.zeros_like(block)
    return jnp.concatenate(
        [jnp.where(lane < 64, block, zero), jnp.where(lane < 64, zero, block)], axis=0
    )


def one_block(stacked):
    half = stacked.shape[0] // 2
    lane = lax.broadcasted_iota(jnp.int32, (half, 128), 1)
    return jnp.where(lane < 64, stacked[:half], stacked[half:])


def place(index, core):
    piece = index >> 8
    inner = index & 255
    side = inner - 128
    is_centre = inner < 128
    row = jnp.where(is_centre, inner >> 4, (side & 63) >> 3)
    col = jnp.where(is_centre, inner & 15, jnp.where(side < 64, (side & 7) - 8, (side & 7) + 16))
    mate = jnp.where(core == 0, 8, -8)
    row = row + jnp.where(piece == 1, mate, jnp.where(piece == 2, -mate, 0))
    return row, col


def window(where_ref, keys_own):
    row0, col0, core, rows, cols = (where_ref[i] for i in range(5))
    own = lax.broadcasted_iota(jnp.int32, (TOK, REGION), 0)
    reach_row, reach_col = place(lax.broadcasted_iota(jnp.int32, (TOK, REGION), 1), core)
    step_row, step_col = reach_row - (own >> 4), reach_col - (own & 15)
    if keys_own:
        step_row, step_col = -step_row, -step_col
    ok = (step_row >= -8) & (step_row <= 7) & (step_col >= -8) & (step_col <= 7)
    grid_row, grid_col = row0 + reach_row, col0 + reach_col
    return ok & (grid_row >= 0) & (grid_row < rows) & (grid_col >= 0) & (grid_col < cols)


def forward_kernel(where_ref, x0, x1, x2, w_ref, proj_ref, prob_ref, pack_ref, nlow_ref):
    for piece, x_ref in enumerate((x0, x1, x2)):
        x = x_ref[...].astype(F32)
        inverse = lax.rsqrt(jnp.mean(x * x, axis=-1, keepdims=True) + 1e-06)
        low = (x * inverse).astype(BF16)
        if piece < 2:
            nlow_ref[piece * TOK : (piece + 1) * TOK] = low[:TOK]
        proj_ref[piece * OWN : (piece + 1) * OWN] = nn(low, w_ref[...]).astype(BF16)
    ok = window(where_ref, False)
    ok2 = jnp.concatenate([ok, ok], axis=0)
    lane = lax.broadcasted_iota(jnp.int32, (TOK, 128), 1)
    stats = jnp.zeros((TOK, 128), F32)
    for pair in range(PAIRS):
        at = slice(128 * pair, 128 * pair + 128)
        query = two_heads(proj_ref[:TOK, at])
        scores = nt(query, proj_ref[:, D + 128 * pair : D + 128 * pair + 128]) * 0.125
        scores = jnp.where(ok2, scores, -1e30)
        highest = jnp.max(scores, axis=-1, keepdims=True)
        grown = jnp.exp(scores - highest)
        total = jnp.sum(grown, axis=-1, keepdims=True)
        probs = (grown * (1.0 / total)).astype(BF16)
        prob_ref[pair] = probs
        value = proj_ref[:, 2 * D + 128 * pair : 2 * D + 128 * pair + 128]
        pack_ref[:, at] = one_block(nn(probs, value)).astype(BF16)
        log_total = highest + jnp.log(total)
        rest = log_total
        for part in range(3):
            piece = rest.astype(BF16).astype(F32)
            rest = rest - piece
            for head in range(2):
                chosen = lane == 8 * part + 2 * pair + head
                stats = jnp.where(chosen, piece[TOK * head : TOK * head + TOK], stats)
    pack_ref[:, D:] = stats.astype(BF16)


def key_probs_kernel(where_ref, p0, p1, p2, proj_ref, prob_ref):
    head = lax.broadcasted_iota(jnp.int32, (8, 128), 0)
    lane = lax.broadcasted_iota(jnp.int32, (8, 128), 1)
    chosen = ((lane & 7) == head) & (lane < 24)
    pick = jnp.where(chosen, 1.0, 0.0).astype(BF16)
    stats = jnp.concatenate([p[:, D:] for p in (p0, p1, p2)], axis=0)
    log_total = nt(pick, stats)
    ok = window(where_ref, True)
    for pair in range(PAIRS):
        key = two_heads(proj_ref[:TOK, D + 128 * pair : D + 128 * pair + 128])
        scores = nt(key, proj_ref[:, 128 * pair : 128 * pair + 128]) * 0.125
        for side in range(2):
            at = 2 * pair + side
            part = scores[TOK * side : TOK * side + TOK] - log_total[at : at + 1]
            probs = jnp.exp(jnp.where(ok, part, -1e30))
            prob_ref[pair, TOK * side : TOK * side + TOK] = probs.astype(BF16)


def query_kernel(where_ref, g_ref, w_ref, pack_ref, proj_ref, prob_ref, dq_ref, *, turn):
    @pl.when(where_ref[5] == turn)
    def _():
        d_mixed = nt(g_ref[...].astype(BF16), w_ref[...]).astype(BF16)
        lane = lax.broadcasted_iota(jnp.int32, (TOK, 128), 1)
        for pair in range(PAIRS):
            at = slice(128 * pair, 128 * pair + 128)
            grad = d_mixed[:, at]
            prod = grad.astype(F32) * pack_ref[:, at].astype(F32)
            delta = jnp.concatenate(
                [
                    jnp.sum(jnp.where(lane < 64, prod, 0.0), axis=-1, keepdims=True),
                    jnp.sum(jnp.where(lane < 64, 0.0, prod), axis=-1, keepdims=True),
                ],
                axis=0,
            )
            value = proj_ref[:, 2 * D + 128 * pair : 2 * D + 128 * pair + 128]
            pressure = nt(two_heads(grad), value)
            slopes = (prob_ref[pair].astype(F32) * (pressure - delta)).astype(BF16)
            key = proj_ref[:, D + 128 * pair : D + 128 * pair + 128]
            dq_ref[:, at] = (one_block(nn(slopes, key)) * 0.125).astype(BF16)


def key_kernel(
    where_ref, g_ref, g0, g1, g2, wo_ref, p0, p1, p2, proj_ref, prob_ref, dq_ref, wq_ref, x_ref,
    in_prev, dp_prev, gl_prev,
    left_ref, right_ref, low_ref, in_ref, dp_ref, gl_ref, dm_ref, *, turn,
):
    active = where_ref[5] == turn

    @pl.when(jnp.logical_not(active))
    def _():
        in_ref[...] = in_prev[...]
        dp_ref[...] = dp_prev[...]
        gl_ref[...] = gl_prev[...]

    @pl.when(active)
    def _():
        head = lax.broadcasted_iota(jnp.int32, (8, D), 0)
        lane = lax.broadcasted_iota(jnp.int32, (8, D), 1)
        pick = jnp.where((lane >> 6) == head, 1.0, 0.0).astype(BF16)
        deltas = []
        for piece, (g, p) in enumerate(((g0, p0), (g1, p1), (g2, p2))):
            d_mixed = nt(g[...], wo_ref[...]).astype(BF16)
            dm_ref[piece * OWN : (piece + 1) * OWN] = d_mixed
            prod = d_mixed.astype(F32) * p[:, :D].astype(F32)
            high = prod.astype(BF16)
            rest = (prod - high.astype(F32)).astype(BF16)
            deltas.append(nt(pick, high) + nt(pick, rest))
        delta = jnp.concatenate(deltas, axis=1)
        dp_ref[:, :D] = dq_ref[...]
        for pair in range(PAIRS):
            at = slice(128 * pair, 128 * pair + 128)
            value = two_heads(proj_ref[:TOK, 2 * D + 128 * pair : 2 * D + 128 * pair + 128])
            grad = dm_ref[:, at]
            pressure = nt(value, grad)
            probs = prob_ref[pair]
            d_value = nn(probs, grad)
            slopes = []
            for side in range(2):
                h = 2 * pair + side
                rows = slice(TOK * side, TOK * side + TOK)
                slopes.append(
                    (probs[rows].astype(F32) * (pressure[rows] - delta[h : h + 1])).astype(BF16)
                )
            d_key = nn(jnp.concatenate(slopes, axis=0), proj_ref[:, at])
            dp_ref[:, D + 128 * pair : D + 128 * pair + 128] = (one_block(d_key) * 0.125).astype(BF16)
            dp_ref[:, 2 * D + 128 * pair : 2 * D + 128 * pair + 128] = one_block(d_value).astype(BF16)
        d_normed = nt(dp_ref[...], wq_ref[...])
        x = x_ref[...].astype(F32)
        inverse = lax.rsqrt(jnp.mean(x * x, axis=-1, keepdims=True) + 1e-06)
        normed = x * inverse
        inner = jnp.mean(d_normed * normed, axis=-1, keepdims=True)
        gradient = g_ref[...].astype(F32)
        out = gradient + inverse * (d_normed - normed * inner)
        in_ref[...] = out
        gl_ref[...] = g_ref[...].astype(BF16)
        low_ref[...] = out.astype(BF16)
        sides = out.reshape(8, 2, 8, D)
        left_ref[...] = sides[:, 0].reshape(64, D).astype(BF16)
        right_ref[...] = sides[:, 1].reshape(64, D).astype(BF16)


def weight_kernel(where_ref, n_ref, d0, d1, m0, m1, g0, g1, out_ref, full_ref):
    core = where_ref[2]
    full_ref[:, : 3 * D] = tn(n_ref[:TOK], d0[...]) + tn(n_ref[TOK:], d1[...])
    full_ref[:, 3 * D :] = tn(m0[...], g0[...]) + tn(m1[...], g1[...])
    chips, cols = out_ref.shape[1] // 8, out_ref.shape[0]
    for col in range(cols):
        rows = [
            full_ref[pl.ds(pl.multiple_of((2 * chip + core) * (8 * cols) + 8 * col, 8), 8)]
            for chip in range(chips)
        ]
        out_ref[col] = jnp.concatenate(rows, axis=0).astype(BF16)


def call(kernel, outs, *args, scratch=(), flops=0):
    vmem = pl.BlockSpec(memory_space=pltpu.VMEM)
    return pl.pallas_call(
        kernel,
        out_shape=[jax.ShapeDtypeStruct(s, t) for s, t in outs],
        in_specs=[pl.BlockSpec(memory_space=pltpu.SMEM)] + [vmem] * (len(args) - 1),
        out_specs=[vmem] * len(outs),
        scratch_shapes=list(scratch),
        compiler_params=pltpu.CompilerParams(vmem_limit_bytes=VMEM_LIMIT),
        cost_estimate=pl.CostEstimate(flops=flops, bytes_accessed=4 << 20, transcendentals=0),
    )(*args)


def body(sizes, activations, qkv_weight, out_weight, cotangent):
    pipes, chips, cols = sizes

    def routed(block, step, plane=None):
        pairs = []
        for p in range(pipes):
            for z in range(chips):
                for k in range(2):
                    for c in range(cols):
                        if plane is not None and p != plane:
                            continue
                        p2, r2, c2 = step(p, 2 * z + k, c)
                        if 0 <= p2 < pipes and 0 <= r2 < 2 * chips and 0 <= c2 < cols:
                            source = (p * 2 * chips + 2 * z + k) * cols + c
                            pairs.append((source, (p2 * 2 * chips + r2) * cols + c2))
        return lax.ppermute(block, AXES, pairs)

    def halves(block):
        shaped = block.reshape(8, 2, 8, block.shape[-1])
        return shaped[:, 0].reshape(64, -1), shaped[:, 1].reshape(64, -1)

    def col_rims(left_half, right_half, down=0, plane=None):
        left = routed(right_half, lambda p, r, c: (p - down, r, c + 1), plane)
        right = routed(left_half, lambda p, r, c: (p - down, r, c - 1), plane)
        return left, right

    def row_rims(own, plane=None):
        mate = routed(own, lambda p, r, c: (p, r ^ 1, c), plane)
        beyond = routed(own, lambda p, r, c: (p, r - 1 + 2 * (r & 1), c), plane)
        return own, mate, beyond

    def spread(block, plane=None):
        left, right = col_rims(*halves(block), plane=plane)
        return row_rims(jnp.concatenate([block, left, right], axis=0), plane)

    pipe, z, core, col = (lax.axis_index(axis) for axis in AXES)
    x = activations.reshape(TOK, D)
    w_qkv, w_out = qkv_weight[0], out_weight[0]
    cot = cotangent.reshape(TOK, D)
    row_total, col_total = 16 * chips, 16 * cols
    where = jnp.stack(
        [8 * (2 * z + core), 16 * col, core, row_total, col_total, pipes - 1 - pipe]
    ).astype(jnp.int32)

    xs = spread(x)
    gs = spread(cot.astype(BF16), pipes - 1)
    proj, q_probs, pack, nlow = call(
        forward_kernel,
        [((REGION, 3 * D), BF16), ((PAIRS, OWN, REGION), BF16), ((TOK, D + 128), BF16), ((OWN, D), BF16)],
        where, *xs, w_qkv, flops=2 << 30,
    )
    packs = spread(pack)
    (k_probs,) = call(
        key_probs_kernel, [((PAIRS, OWN, REGION), BF16)], where, *packs, proj, flops=1 << 28
    )
    d_in = jnp.zeros((TOK, D), F32)
    d_proj = jnp.zeros((TOK, 3 * D), BF16)
    g_low = jnp.zeros((TOK, D), BF16)
    gradient = cot
    for turn in range(pipes):
        plane = pipes - 1 - turn
        if turn > 0:
            centre = routed(low, lambda p, r, c: (p - 1, r, c), plane + 1)
            left, right = col_rims(left_half, right_half, 1, plane + 1)
            gs = row_rims(jnp.concatenate([centre, left, right], axis=0), plane)
            gradient = centre
        (d_query,) = call(
            functools.partial(query_kernel, turn=turn), [((TOK, D), BF16)],
            where, gradient, w_out, pack, proj, q_probs, flops=1 << 29,
        )
        left_half, right_half, low, d_in, d_proj, g_low = call(
            functools.partial(key_kernel, turn=turn),
            [((64, D), BF16), ((64, D), BF16), ((TOK, D), BF16), ((TOK, D), F32),
             ((TOK, 3 * D), BF16), ((TOK, D), BF16)],
            where, gradient, *gs, w_out, *packs, proj, k_probs, d_query, w_qkv, x,
            d_in, d_proj, g_low,
            scratch=[pltpu.VMEM((REGION, D), BF16)], flops=1 << 30,
        )
    swap = lambda p, r, c: (p, r ^ 1, c)
    (part,) = call(
        weight_kernel, [((cols, 8 * chips, 4 * D), BF16)],
        where, nlow, d_proj, routed(d_proj, swap), pack[:, :D], packs[1][:TOK, :D],
        g_low, routed(g_low, swap),
        scratch=[pltpu.VMEM((D, 4 * D), F32)], flops=1 << 30,
    )
    part = lax.all_to_all(part, "col", 0, 0, tiled=True)
    part = jnp.sum(part.astype(F32), axis=0).astype(BF16).reshape(chips, 8, 4 * D)
    part = lax.all_to_all(part, "z", 0, 0, tiled=True)
    part = jnp.sum(part.astype(F32), axis=0) * (row_total * col_total) ** (-0.5)
    return d_in.reshape(1, 8, 16, D), part[None, :, : 3 * D], part[None, :, 3 * D :]


def solution(mesh):
    pipes, rows, cols = (mesh.shape[axis] for axis in ("pipe", "row", "col"))
    fine = Mesh(np.asarray(mesh.devices).reshape(pipes, rows // 2, 2, cols), AXES)
    row = ("z", "core")
    return jax.shard_map(
        functools.partial(body, (pipes, rows // 2, cols)),
        mesh=fine,
        in_specs=(
            P("pipe", row, "col", None),
            P("pipe", None, None),
            P("pipe", None, None),
            P(row, "col", None),
        ),
        out_specs=(
            P("pipe", row, "col", None),
            P("pipe", ("z", "core", "col"), None),
            P("pipe", ("z", "core", "col"), None),
        ),
        check_vma=False,
    )
```

```python
import functools

import jax
import jax.numpy as jnp
import numpy as np
from jax import lax
from jax.experimental import pallas as pl
from jax.experimental.pallas import tpu as pltpu
from jax.sharding import Mesh
from jax.sharding import PartitionSpec as P

F32 = jnp.float32
BF16 = jnp.bfloat16
AXES = ("pipe", "z", "core", "col")
D = 512
PAIRS = 4
TOK = 128
OWN = 256
REGION = 768
VMEM_LIMIT = 40 * 1024 * 1024


def nn(a, b):
    return lax.dot_general(a, b, (((1,), (0,)), ((), ())), preferred_element_type=F32)


def nt(a, b):
    return lax.dot_general(a, b, (((1,), (1,)), ((), ())), preferred_element_type=F32)


def tn(a, b):
    return lax.dot_general(a, b, (((0,), (0,)), ((), ())), preferred_element_type=F32)


def two_heads(block):
    lane = lax.broadcasted_iota(jnp.int32, block.shape, 1)
    zero = jnp.zeros_like(block)
    return jnp.concatenate(
        [jnp.where(lane < 64, block, zero), jnp.where(lane < 64, zero, block)], axis=0
    )


def one_block(stacked):
    half = stacked.shape[0] // 2
    lane = lax.broadcasted_iota(jnp.int32, (half, 128), 1)
    return jnp.where(lane < 64, stacked[:half], stacked[half:])


def place(index, core):
    piece = index >> 8
    inner = index & 255
    side = inner - 128
    is_centre = inner < 128
    row = jnp.where(is_centre, inner >> 4, (side & 63) >> 3)
    col = jnp.where(is_centre, inner & 15, jnp.where(side < 64, (side & 7) - 8, (side & 7) + 16))
    mate = jnp.where(core == 0, 8, -8)
    row = row + jnp.where(piece == 1, mate, jnp.where(piece == 2, -mate, 0))
    return row, col


def window(where_ref, keys_own):
    row0, col0, core, rows, cols = (where_ref[i] for i in range(5))
    own = lax.broadcasted_iota(jnp.int32, (TOK, REGION), 0)
    reach_row, reach_col = place(lax.broadcasted_iota(jnp.int32, (TOK, REGION), 1), core)
    step_row, step_col = reach_row - (own >> 4), reach_col - (own & 15)
    if keys_own:
        step_row, step_col = -step_row, -step_col
    ok = (step_row >= -8) & (step_row <= 7) & (step_col >= -8) & (step_col <= 7)
    grid_row, grid_col = row0 + reach_row, col0 + reach_col
    return ok & (grid_row >= 0) & (grid_row < rows) & (grid_col >= 0) & (grid_col < cols)


def rows_of(refs, at):
    return jnp.concatenate([ref[:, at] for ref in refs], axis=0)


def forward_kernel(where_ref, *refs):
    pieces, (w_ref, proj_ref, prob_ref, pack_ref, nlow_ref) = refs[:9], refs[9:]
    for piece in range(3):
        x = rows_of(pieces[3 * piece : 3 * piece + 3], slice(0, D)).astype(F32)
        inverse = lax.rsqrt(jnp.mean(x * x, axis=-1, keepdims=True) + 1e-06)
        low = (x * inverse).astype(BF16)
        if piece < 2:
            nlow_ref[piece * TOK : (piece + 1) * TOK] = low[:TOK]
        proj_ref[piece * OWN : (piece + 1) * OWN] = nn(low, w_ref[...]).astype(BF16)
    ok = window(where_ref, False)
    ok2 = jnp.concatenate([ok, ok], axis=0)
    lane = lax.broadcasted_iota(jnp.int32, (TOK, 128), 1)
    stats = jnp.zeros((TOK, 128), F32)
    for pair in range(PAIRS):
        at = slice(128 * pair, 128 * pair + 128)
        query = two_heads(proj_ref[:TOK, at])
        scores = nt(query, proj_ref[:, D + 128 * pair : D + 128 * pair + 128]) * 0.125
        scores = jnp.where(ok2, scores, -1e30)
        highest = jnp.max(scores, axis=-1, keepdims=True)
        grown = jnp.exp(scores - highest)
        total = jnp.sum(grown, axis=-1, keepdims=True)
        probs = (grown * (1.0 / total)).astype(BF16)
        prob_ref[pair] = probs
        value = proj_ref[:, 2 * D + 128 * pair : 2 * D + 128 * pair + 128]
        pack_ref[:, at] = one_block(nn(probs, value)).astype(BF16)
        log_total = highest + jnp.log(total)
        rest = log_total
        for part in range(3):
            piece = rest.astype(BF16).astype(F32)
            rest = rest - piece
            for head in range(2):
                chosen = lane == 8 * part + 2 * pair + head
                stats = jnp.where(chosen, piece[TOK * head : TOK * head + TOK], stats)
    pack_ref[:, D:] = stats.astype(BF16)


def key_probs_kernel(where_ref, *refs):
    pieces, (proj_ref, prob_ref) = refs[:9], refs[9:]
    head = lax.broadcasted_iota(jnp.int32, (8, 128), 0)
    lane = lax.broadcasted_iota(jnp.int32, (8, 128), 1)
    chosen = ((lane & 7) == head) & (lane < 24)
    pick = jnp.where(chosen, 1.0, 0.0).astype(BF16)
    log_total = nt(pick, rows_of(pieces, slice(D, D + 128)))
    ok = window(where_ref, True)
    for pair in range(PAIRS):
        key = two_heads(proj_ref[:TOK, D + 128 * pair : D + 128 * pair + 128])
        scores = nt(key, proj_ref[:, 128 * pair : 128 * pair + 128]) * 0.125
        for side in range(2):
            at = 2 * pair + side
            part = scores[TOK * side : TOK * side + TOK] - log_total[at : at + 1]
            probs = jnp.exp(jnp.where(ok, part, -1e30))
            prob_ref[pair, TOK * side : TOK * side + TOK] = probs.astype(BF16)


def query_kernel(where_ref, g_ref, w_ref, pack_ref, proj_ref, prob_ref, dq_ref, *, turn):
    @pl.when(where_ref[5] == turn)
    def _():
        d_mixed = nt(g_ref[...].astype(BF16), w_ref[...]).astype(BF16)
        lane = lax.broadcasted_iota(jnp.int32, (TOK, 128), 1)
        for pair in range(PAIRS):
            at = slice(128 * pair, 128 * pair + 128)
            grad = d_mixed[:, at]
            prod = grad.astype(F32) * pack_ref[:, at].astype(F32)
            delta = jnp.concatenate(
                [
                    jnp.sum(jnp.where(lane < 64, prod, 0.0), axis=-1, keepdims=True),
                    jnp.sum(jnp.where(lane < 64, 0.0, prod), axis=-1, keepdims=True),
                ],
                axis=0,
            )
            value = proj_ref[:, 2 * D + 128 * pair : 2 * D + 128 * pair + 128]
            pressure = nt(two_heads(grad), value)
            slopes = (prob_ref[pair].astype(F32) * (pressure - delta)).astype(BF16)
            key = proj_ref[:, D + 128 * pair : D + 128 * pair + 128]
            dq_ref[:, at] = (one_block(nn(slopes, key)) * 0.125).astype(BF16)


def key_side(first, grads, mixes, wo_ref, proj_ref, prob_ref):
    d_mixed = nt(rows_of(grads, slice(-D, None)), wo_ref[...]).astype(BF16)
    count = d_mixed.shape[0]
    head = lax.broadcasted_iota(jnp.int32, (8, D), 0)
    lane = lax.broadcasted_iota(jnp.int32, (8, D), 1)
    pick = jnp.where((lane >> 6) == head, 1.0, 0.0).astype(BF16)
    prod = d_mixed.astype(F32) * rows_of(mixes, slice(0, D)).astype(F32)
    high = prod.astype(BF16)
    rest = (prod - high.astype(F32)).astype(BF16)
    delta = nt(pick, high) + nt(pick, rest)
    terms = []
    for pair in range(PAIRS):
        at = slice(128 * pair, 128 * pair + 128)
        value = two_heads(proj_ref[:TOK, 2 * D + 128 * pair : 2 * D + 128 * pair + 128])
        grad = d_mixed[:, at]
        pressure = nt(value, grad)
        probs = prob_ref[pair, :, first : first + count]
        slopes = []
        for side in range(2):
            h = 2 * pair + side
            rows = slice(TOK * side, TOK * side + TOK)
            slopes.append(
                (probs[rows].astype(F32) * (pressure[rows] - delta[h : h + 1])).astype(BF16)
            )
        d_key = nn(jnp.concatenate(slopes, axis=0), proj_ref[first : first + count, at])
        terms.append((one_block(d_key), one_block(nn(probs, grad))))
    return terms


def near_kernel(where_ref, *refs, turn):
    grads, mixes, (wo_ref, proj_ref, prob_ref, sum_ref) = refs[:3], refs[3:6], refs[6:]

    @pl.when(where_ref[5] == turn)
    def _():
        terms = key_side(0, grads, mixes, wo_ref, proj_ref, prob_ref)
        for pair, (d_key, d_value) in enumerate(terms):
            sum_ref[:, 128 * pair : 128 * pair + 128] = d_key
            sum_ref[:, D + 128 * pair : D + 128 * pair + 128] = d_value


def far_kernel(where_ref, *refs, turn, last):
    grads, mixes, refs = refs[:6], refs[6:12], refs[12:]
    (wo_ref, proj_ref, prob_ref, sum_ref, g_ref, dq_ref, wq_ref, x_ref), refs = refs[:8], refs[8:]
    (in_prev, dp_prev, gl_prev), (in_ref, dp_ref, gl_ref, *sends) = refs[:3], refs[3:]
    active = where_ref[5] == turn

    @pl.when(jnp.logical_not(active))
    def _():
        in_ref[...] = in_prev[...]
        dp_ref[...] = dp_prev[...]
        gl_ref[...] = gl_prev[...]

    @pl.when(active)
    def _():
        dp_ref[:, :D] = dq_ref[...]
        terms = key_side(OWN, grads, mixes, wo_ref, proj_ref, prob_ref)
        for pair, (d_key, d_value) in enumerate(terms):
            low, high = 128 * pair, 128 * pair + 128
            d_key = (d_key + sum_ref[:, low:high]) * 0.125
            dp_ref[:, D + low : D + high] = d_key.astype(BF16)
            d_value = d_value + sum_ref[:, D + low : D + high]
            dp_ref[:, 2 * D + low : 2 * D + high] = d_value.astype(BF16)
        d_normed = nt(dp_ref[...], wq_ref[...])
        x = x_ref[...].astype(F32)
        inverse = lax.rsqrt(jnp.mean(x * x, axis=-1, keepdims=True) + 1e-06)
        normed = x * inverse
        inner = jnp.mean(d_normed * normed, axis=-1, keepdims=True)
        out = g_ref[...].astype(F32) + inverse * (d_normed - normed * inner)
        in_ref[...] = out
        gl_ref[:TOK] = g_ref[...].astype(BF16)
        gl_ref[TOK:] = grads[0][:, -D:]
        if not last:
            low_ref, left_ref, right_ref = sends
            low_ref[...] = out.astype(BF16)
            sides = out.reshape(8, 2, 8, D)
            left_ref[...] = sides[:, 0].reshape(64, D).astype(BF16)
            right_ref[...] = sides[:, 1].reshape(64, D).astype(BF16)


def weight_kernel(where_ref, n_ref, d0, d1, m0, m1, g_ref, *refs):
    outs, full_ref = refs[:-1], refs[-1]
    core, here = where_ref[2], where_ref[6]
    full_ref[:, : 3 * D] = tn(n_ref[:TOK], d0[...]) + tn(n_ref[TOK:], d1[...])
    full_ref[:, 3 * D :] = tn(m0[:, :D], g_ref[:TOK]) + tn(m1[:, :D], g_ref[TOK:])
    cols = len(outs)
    for distance, out_ref in enumerate(outs):
        col = lax.rem(here + distance, cols)
        rows = [
            full_ref[pl.ds(pl.multiple_of((2 * chip + core) * (8 * cols) + 8 * col, 8), 8)]
            for chip in range(out_ref.shape[0] // 8)
        ]
        out_ref[...] = jnp.concatenate(rows, axis=0).astype(BF16)


def call(kernel, outs, *args, scratch=(), flops=0):
    vmem = pl.BlockSpec(memory_space=pltpu.VMEM)
    return pl.pallas_call(
        kernel,
        out_shape=[jax.ShapeDtypeStruct(s, t) for s, t in outs],
        in_specs=[pl.BlockSpec(memory_space=pltpu.SMEM)] + [vmem] * (len(args) - 1),
        out_specs=[vmem] * len(outs),
        scratch_shapes=list(scratch),
        compiler_params=pltpu.CompilerParams(vmem_limit_bytes=VMEM_LIMIT),
        cost_estimate=pl.CostEstimate(flops=flops, bytes_accessed=4 << 20, transcendentals=0),
    )(*args)


def body(sizes, activations, qkv_weight, out_weight, cotangent):
    pipes, chips, cols = sizes

    def routed(block, step, plane=None):
        pairs = []
        for p in range(pipes):
            for z in range(chips):
                for k in range(2):
                    for c in range(cols):
                        if plane is not None and p != plane:
                            continue
                        p2, r2, c2 = step(p, 2 * z + k, c)
                        if 0 <= p2 < pipes and 0 <= r2 < 2 * chips and 0 <= c2 < cols:
                            source = (p * 2 * chips + 2 * z + k) * cols + c
                            pairs.append((source, (p2 * 2 * chips + r2) * cols + c2))
        return lax.ppermute(block, AXES, pairs)

    def side(block, at):
        return block.reshape(8, 2, 8, -1)[:, at].reshape(64, -1)

    def beyond(p, r, c):
        return p, r - 1 + 2 * (r & 1), c

    def mate(p, r, c):
        return p, r ^ 1, c

    def spread(block):
        low, high = side(block, 0), side(block, 1)
        left = routed(high, lambda p, r, c: (p, r, c + 1))
        right = routed(low, lambda p, r, c: (p, r, c - 1))
        far_left = routed(high, lambda p, r, c: beyond(p, r, c + 1))
        far_right = routed(low, lambda p, r, c: beyond(p, r, c - 1))
        far = routed(block, beyond)
        near = [routed(piece, mate) for piece in (block, left, right)]
        return [block, left, right, *near, far, far_left, far_right]

    pipe, z, core, col = (lax.axis_index(axis) for axis in AXES)
    x = activations.reshape(TOK, D)
    w_qkv, w_out = qkv_weight[0], out_weight[0]
    cot = cotangent.reshape(TOK, D)
    row_total, col_total = 16 * chips, 16 * cols
    where = jnp.stack(
        [8 * (2 * z + core), 16 * col, core, row_total, col_total, pipes - 1 - pipe, col]
    ).astype(jnp.int32)

    both = spread(jnp.concatenate([x, cot.astype(BF16)], axis=1))
    proj, q_probs, pack, nlow = call(
        forward_kernel,
        [((REGION, 3 * D), BF16), ((PAIRS, OWN, REGION), BF16), ((TOK, D + 128), BF16), ((OWN, D), BF16)],
        where, *both, w_qkv, flops=2 << 30,
    )
    packs = spread(pack)
    (k_probs,) = call(
        key_probs_kernel, [((PAIRS, OWN, REGION), BF16)], where, *packs, proj, flops=1 << 28
    )
    d_in = jnp.zeros((TOK, D), F32)
    d_proj = jnp.zeros((TOK, 3 * D), BF16)
    g_low = jnp.zeros((OWN, D), BF16)
    gradient = cot
    grads = both
    for turn in range(pipes):
        plane, last = pipes - 1 - turn, turn == pipes - 1
        if turn > 0:
            low, low_side, high_side = sends
            gradient = routed(low, lambda p, r, c: (p - 1, r, c), plane + 1)
            left = routed(high_side, lambda p, r, c: (p - 1, r, c + 1), plane + 1)
            right = routed(low_side, lambda p, r, c: (p - 1, r, c - 1), plane + 1)
            own = [gradient, left, right]
            grads = own + [None] * 6
            for at, piece in enumerate(own):
                grads[6 + at] = routed(piece, beyond, plane)
                grads[3 + at] = routed(piece, mate, plane)
        (d_query,) = call(
            functools.partial(query_kernel, turn=turn), [((TOK, D), BF16)],
            where, gradient, w_out, pack, proj, q_probs, flops=1 << 29,
        )
        (sums,) = call(
            functools.partial(near_kernel, turn=turn), [((TOK, 2 * D), F32)],
            where, *grads[:3], *packs[:3], w_out, proj, k_probs, flops=1 << 29,
        )
        halves = [((64, D), BF16), ((64, D), BF16)]
        d_in, d_proj, g_low, *sends = call(
            functools.partial(far_kernel, turn=turn, last=last),
            [((TOK, D), F32), ((TOK, 3 * D), BF16), ((OWN, D), BF16)]
            + ([] if last else [((TOK, D), BF16)] + halves),
            where, *grads[3:], *packs[3:], w_out, proj, k_probs, sums, gradient, d_query,
            w_qkv, x, d_in, d_proj, g_low, flops=1 << 30,
        )
    parts = call(
        weight_kernel, [((8 * chips, 4 * D), BF16)] * cols,
        where, nlow, d_proj, routed(d_proj, mate), pack, packs[3], g_low,
        scratch=[pltpu.VMEM((D, 4 * D), F32)], flops=1 << 30,
    )
    total = parts[0].astype(F32)
    for distance in range(1, cols):
        moved = lax.ppermute(
            parts[distance], "col", [(c, (c + distance) % cols) for c in range(cols)]
        )
        total = total + moved.astype(F32)
    part = lax.all_to_all(total.astype(BF16).reshape(chips, 8, 4 * D), "z", 0, 0, tiled=True)
    part = jnp.sum(part.astype(F32), axis=0) * (row_total * col_total) ** (-0.5)
    return d_in.reshape(1, 8, 16, D), part[None, :, : 3 * D], part[None, :, 3 * D :]


def solution(mesh):
    pipes, rows, cols = (mesh.shape[axis] for axis in ("pipe", "row", "col"))
    fine = Mesh(np.asarray(mesh.devices).reshape(pipes, rows // 2, 2, cols), AXES)
    row = ("z", "core")
    return jax.shard_map(
        functools.partial(body, (pipes, rows // 2, cols)),
        mesh=fine,
        in_specs=(
            P("pipe", row, "col", None),
            P("pipe", None, None),
            P("pipe", None, None),
            P(row, "col", None),
        ),
        out_specs=(
            P("pipe", row, "col", None),
            P("pipe", ("z", "core", "col"), None),
            P("pipe", ("z", "core", "col"), None),
        ),
        check_vma=False,
    )
```

```python
import functools

import jax
import jax.numpy as jnp
import numpy as np
from jax import lax
from jax.experimental import pallas as pl
from jax.experimental.pallas import tpu as pltpu
from jax.sharding import Mesh
from jax.sharding import PartitionSpec as P

F32 = jnp.float32
BF16 = jnp.bfloat16
AXES = ("pipe", "z", "core", "col")
D = 512
PAIRS = 4
TOK = 128
OWN = 256
REGION = 768
VMEM_LIMIT = 40 * 1024 * 1024


def nn(a, b):
    return lax.dot_general(a, b, (((1,), (0,)), ((), ())), preferred_element_type=F32)


def nt(a, b):
    return lax.dot_general(a, b, (((1,), (1,)), ((), ())), preferred_element_type=F32)


def tn(a, b):
    return lax.dot_general(a, b, (((0,), (0,)), ((), ())), preferred_element_type=F32)


def two_heads(block):
    lane = lax.broadcasted_iota(jnp.int32, block.shape, 1)
    zero = jnp.zeros_like(block)
    return jnp.concatenate(
        [jnp.where(lane < 64, block, zero), jnp.where(lane < 64, zero, block)], axis=0
    )


def one_block(stacked):
    half = stacked.shape[0] // 2
    lane = lax.broadcasted_iota(jnp.int32, (half, 128), 1)
    return jnp.where(lane < 64, stacked[:half], stacked[half:])


def place(index, core):
    piece = index >> 8
    inner = index & 255
    side = inner - 128
    is_centre = inner < 128
    row = jnp.where(is_centre, inner >> 4, (side & 63) >> 3)
    col = jnp.where(is_centre, inner & 15, jnp.where(side < 64, (side & 7) - 8, (side & 7) + 16))
    mate = jnp.where(core == 0, 8, -8)
    row = row + jnp.where(piece == 1, mate, jnp.where(piece == 2, -mate, 0))
    return row, col


def window(where_ref, keys_own):
    row0, col0, core, rows, cols = (where_ref[i] for i in range(5))
    own = lax.broadcasted_iota(jnp.int32, (TOK, 1), 0)
    reach_row, reach_col = place(lax.broadcasted_iota(jnp.int32, (1, REGION), 1), core)
    grid_row, grid_col = row0 + reach_row, col0 + reach_col
    inside = (grid_row >= 0) & (grid_row < rows) & (grid_col >= 0) & (grid_col < cols)
    reach_row = jnp.where(inside, reach_row, 1 << 20)
    if keys_own:
        step_row, step_col = (own >> 4) - reach_row, (own & 15) - reach_col
    else:
        step_row, step_col = reach_row - (own >> 4), reach_col - (own & 15)
    return (step_row >= -8) & (step_row <= 7) & (step_col >= -8) & (step_col <= 7)


def put_sides(block, left_ref, right_ref):
    sides = block.reshape(8, 2, 8, block.shape[-1])
    left_ref[...] = sides[:, 0].reshape(64, -1).astype(BF16)
    right_ref[...] = sides[:, 1].reshape(64, -1).astype(BF16)


def forward_kernel(
    where_ref, x0, x1, x2, w_ref, cot_ref, proj_ref, prob_ref, nlow_ref, pack_ref, left_ref, right_ref
):
    for piece, x_ref in enumerate((x0, x1, x2)):
        x = x_ref[...].astype(F32)
        inverse = lax.rsqrt(jnp.mean(x * x, axis=-1, keepdims=True) + 1e-06)
        low = (x * inverse).astype(BF16)
        if piece < 2:
            nlow_ref[piece * TOK : (piece + 1) * TOK] = low[:TOK]
        proj_ref[piece * OWN : (piece + 1) * OWN] = nn(low, w_ref[...]).astype(BF16)
    ok = window(where_ref, False)
    ok2 = jnp.concatenate([ok, ok], axis=0)
    lane = lax.broadcasted_iota(jnp.int32, (TOK, 128), 1)
    stats = jnp.zeros((TOK, 128), F32)
    for pair in range(PAIRS):
        at = slice(128 * pair, 128 * pair + 128)
        query = two_heads(proj_ref[:TOK, at] * 0.125)
        scores = nt(query, proj_ref[:, D + 128 * pair : D + 128 * pair + 128])
        scores = jnp.where(ok2, scores, -1e30)
        highest = jnp.max(scores, axis=-1, keepdims=True)
        grown = jnp.exp(scores - highest)
        total = jnp.sum(grown, axis=-1, keepdims=True)
        probs = (grown * (1.0 / total)).astype(BF16)
        prob_ref[pair] = probs
        value = proj_ref[:, 2 * D + 128 * pair : 2 * D + 128 * pair + 128]
        pack_ref[:, at] = one_block(nn(probs, value)).astype(BF16)
        log_total = highest + jnp.log(total)
        rest = log_total
        for part in range(3):
            piece = rest.astype(BF16).astype(F32)
            rest = rest - piece
            for head in range(2):
                chosen = lane == 8 * part + 2 * pair + head
                stats = jnp.where(chosen, piece[TOK * head : TOK * head + TOK], stats)
    pack_ref[:, D : D + 128] = stats.astype(BF16)
    pack_ref[:, D + 128 :] = cot_ref[...].astype(BF16)
    put_sides(pack_ref[...].astype(F32), left_ref, right_ref)


def key_probs_kernel(where_ref, p0, p1, p2, proj_ref, prob_ref):
    head = lax.broadcasted_iota(jnp.int32, (8, 128), 0)
    lane = lax.broadcasted_iota(jnp.int32, (8, 128), 1)
    chosen = ((lane & 7) == head) & (lane < 24)
    pick = jnp.where(chosen, 1.0, 0.0).astype(BF16)
    stats = jnp.concatenate([p[:, D : D + 128] for p in (p0, p1, p2)], axis=0)
    log_total = nt(pick, stats)
    ok = window(where_ref, True)
    for pair in range(PAIRS):
        key = two_heads(proj_ref[:TOK, D + 128 * pair : D + 128 * pair + 128] * 0.125)
        scores = nt(key, proj_ref[:, 128 * pair : 128 * pair + 128])
        for side in range(2):
            at = 2 * pair + side
            part = scores[TOK * side : TOK * side + TOK] - log_total[at : at + 1]
            probs = jnp.exp(jnp.where(ok, part, -1e30))
            prob_ref[pair, TOK * side : TOK * side + TOK] = probs.astype(BF16)


def query_kernel(where_ref, g_ref, w_ref, pack_ref, proj_ref, prob_ref, dq_ref, *, turn):
    @pl.when(where_ref[5] == turn)
    def _():
        d_mixed = nt(g_ref[...].astype(BF16), w_ref[...]).astype(BF16)
        lane = lax.broadcasted_iota(jnp.int32, (TOK, 128), 1)
        for pair in range(PAIRS):
            at = slice(128 * pair, 128 * pair + 128)
            grad = d_mixed[:, at]
            prod = grad.astype(F32) * pack_ref[:, at].astype(F32)
            delta = jnp.concatenate(
                [
                    jnp.sum(jnp.where(lane < 64, prod, 0.0), axis=-1, keepdims=True),
                    jnp.sum(jnp.where(lane < 64, 0.0, prod), axis=-1, keepdims=True),
                ],
                axis=0,
            )
            value = proj_ref[:, 2 * D + 128 * pair : 2 * D + 128 * pair + 128]
            pressure = nt(two_heads(grad), value)
            slopes = (prob_ref[pair].astype(F32) * (pressure - delta)).astype(BF16)
            key = proj_ref[:, D + 128 * pair : D + 128 * pair + 128]
            dq_ref[:, at] = (one_block(nn(slopes, key)) * 0.125).astype(BF16)


def key_kernel(
    where_ref, g_ref, g0, g1, g2, wo_ref, p0, p1, p2, proj_ref, prob_ref, dq_ref, wq_ref, x_ref,
    in_prev, dp_prev, gl_prev,
    in_ref, dp_ref, gl_ref, *rest, turn,
):
    sends, dm_ref = rest[:-1], rest[-1]
    active = where_ref[5] == turn

    @pl.when(jnp.logical_not(active))
    def _():
        in_ref[...] = in_prev[...]
        dp_ref[...] = dp_prev[...]
        gl_ref[...] = gl_prev[...]

    @pl.when(active)
    def _():
        head = lax.broadcasted_iota(jnp.int32, (8, D), 0)
        lane = lax.broadcasted_iota(jnp.int32, (8, D), 1)
        pick = jnp.where((lane >> 6) == head, 1.0, 0.0).astype(BF16)
        deltas = []
        for piece, (g, p) in enumerate(((g0, p0), (g1, p1), (g2, p2))):
            d_mixed = nt(g[:, -D:], wo_ref[...]).astype(BF16)
            dm_ref[piece * OWN : (piece + 1) * OWN] = d_mixed
            prod = d_mixed.astype(F32) * p[:, :D].astype(F32)
            high = prod.astype(BF16)
            rest = (prod - high.astype(F32)).astype(BF16)
            deltas.append(nt(pick, high) + nt(pick, rest))
        delta = jnp.concatenate(deltas, axis=1)
        dp_ref[:, :D] = dq_ref[...]
        for pair in range(PAIRS):
            at = slice(128 * pair, 128 * pair + 128)
            value = two_heads(proj_ref[:TOK, 2 * D + 128 * pair : 2 * D + 128 * pair + 128])
            grad = dm_ref[:, at]
            pressure = nt(value, grad)
            probs = prob_ref[pair]
            d_value = nn(probs, grad)
            slopes = []
            for side in range(2):
                h = 2 * pair + side
                rows = slice(TOK * side, TOK * side + TOK)
                slopes.append(
                    (probs[rows].astype(F32) * (pressure[rows] - delta[h : h + 1])).astype(BF16)
                )
            d_key = nn(jnp.concatenate(slopes, axis=0), proj_ref[:, at])
            dp_ref[:, D + 128 * pair : D + 128 * pair + 128] = (one_block(d_key) * 0.125).astype(BF16)
            dp_ref[:, 2 * D + 128 * pair : 2 * D + 128 * pair + 128] = one_block(d_value).astype(BF16)
        d_normed = nt(dp_ref[...], wq_ref[...])
        x = x_ref[...].astype(F32)
        inverse = lax.rsqrt(jnp.mean(x * x, axis=-1, keepdims=True) + 1e-06)
        normed = x * inverse
        inner = jnp.mean(d_normed * normed, axis=-1, keepdims=True)
        gradient = g_ref[...].astype(F32)
        out = gradient + inverse * (d_normed - normed * inner)
        in_ref[...] = out
        gl_ref[:TOK] = g_ref[...].astype(BF16)
        gl_ref[TOK:] = g1[:TOK, -D:]
        if sends:
            low_ref, left_ref, right_ref = sends
            low_ref[...] = out.astype(BF16)
            put_sides(out, left_ref, right_ref)


def weight_kernel(where_ref, n_ref, d0, d1, m0, m1, g_ref, out_ref, full_ref):
    core = where_ref[2]
    full_ref[:, : 3 * D] = tn(n_ref[:TOK], d0[...]) + tn(n_ref[TOK:], d1[...])
    full_ref[:, 3 * D :] = tn(m0[:, :D], g_ref[:TOK]) + tn(m1[:TOK, :D], g_ref[TOK:])
    chips, cols = out_ref.shape[1] // 8, out_ref.shape[0]
    for col in range(cols):
        rows = [
            full_ref[pl.ds(pl.multiple_of((2 * chip + core) * (8 * cols) + 8 * col, 8), 8)]
            for chip in range(chips)
        ]
        out_ref[col] = jnp.concatenate(rows, axis=0).astype(BF16)


def total_kernel(where_ref, part_ref, qkv_ref, out_ref, *, scale):
    total = part_ref[0].astype(F32)
    for source in range(1, part_ref.shape[0]):
        total = total + part_ref[source].astype(F32)
    qkv_ref[...] = total[:, : 3 * D] * scale
    out_ref[...] = total[:, 3 * D :] * scale


def call(kernel, outs, *args, scratch=(), flops=0):
    vmem = pl.BlockSpec(memory_space=pltpu.VMEM)
    return pl.pallas_call(
        kernel,
        out_shape=[jax.ShapeDtypeStruct(s, t) for s, t in outs],
        in_specs=[pl.BlockSpec(memory_space=pltpu.SMEM)] + [vmem] * (len(args) - 1),
        out_specs=[vmem] * len(outs),
        scratch_shapes=list(scratch),
        compiler_params=pltpu.CompilerParams(vmem_limit_bytes=VMEM_LIMIT),
        cost_estimate=pl.CostEstimate(flops=flops, bytes_accessed=4 << 20, transcendentals=0),
    )(*args)


def body(sizes, activations, qkv_weight, out_weight, cotangent):
    pipes, chips, cols = sizes

    def routed(block, step, plane=None):
        pairs = []
        for p in range(pipes):
            for z in range(chips):
                for k in range(2):
                    for c in range(cols):
                        if plane is not None and p != plane:
                            continue
                        p2, r2, c2 = step(p, 2 * z + k, c)
                        if 0 <= p2 < pipes and 0 <= r2 < 2 * chips and 0 <= c2 < cols:
                            source = (p * 2 * chips + 2 * z + k) * cols + c
                            pairs.append((source, (p2 * 2 * chips + r2) * cols + c2))
        return lax.ppermute(block, AXES, pairs)

    def col_rims(left_half, right_half, down=0, plane=None):
        left = routed(right_half, lambda p, r, c: (p - down, r, c + 1), plane)
        right = routed(left_half, lambda p, r, c: (p - down, r, c - 1), plane)
        return left, right

    def mate(p, r, c):
        return p, r ^ 1, c

    def row_rims(pieces, plane=None):
        own = jnp.concatenate(pieces, axis=0)
        beyond = routed(own, lambda p, r, c: (p, r - 1 + 2 * (r & 1), c), plane)
        return own, routed(own, mate, plane), beyond

    pipe, z, core, col = (lax.axis_index(axis) for axis in AXES)
    x = activations.reshape(TOK, D)
    w_qkv, w_out = qkv_weight[0], out_weight[0]
    cot = cotangent.reshape(TOK, D)
    row_total, col_total = 16 * chips, 16 * cols
    where = jnp.stack(
        [8 * (2 * z + core), 16 * col, core, row_total, col_total, pipes - 1 - pipe]
    ).astype(jnp.int32)

    x_sides = x.reshape(8, 2, 8, D)
    xs = row_rims([x, *col_rims(x_sides[:, 0].reshape(64, D), x_sides[:, 1].reshape(64, D))])
    wide = 2 * D + 128
    proj, q_probs, nlow, pack, low_side, high_side = call(
        forward_kernel,
        [((REGION, 3 * D), BF16), ((PAIRS, OWN, REGION), BF16), ((OWN, D), BF16),
         ((TOK, wide), BF16), ((64, wide), BF16), ((64, wide), BF16)],
        where, *xs, w_qkv, cot, flops=2 << 30,
    )
    packs = row_rims([pack, *col_rims(low_side, high_side)])
    (k_probs,) = call(
        key_probs_kernel, [((PAIRS, OWN, REGION), BF16)], where, *packs, proj, flops=1 << 28
    )
    d_in = jnp.zeros((TOK, D), F32)
    d_proj = jnp.zeros((TOK, 3 * D), BF16)
    g_low = jnp.zeros((OWN, D), BF16)
    gradient, gs = cot, packs
    for turn in range(pipes):
        plane, last = pipes - 1 - turn, turn == pipes - 1
        if turn > 0:
            low, low_side, high_side = sends
            gradient = routed(low, lambda p, r, c: (p - 1, r, c), plane + 1)
            gs = row_rims([gradient, *col_rims(low_side, high_side, 1, plane + 1)], plane)
        (d_query,) = call(
            functools.partial(query_kernel, turn=turn), [((TOK, D), BF16)],
            where, gradient, w_out, pack, proj, q_probs, flops=1 << 29,
        )
        halves = [((TOK, D), BF16), ((64, D), BF16), ((64, D), BF16)]
        d_in, d_proj, g_low, *sends = call(
            functools.partial(key_kernel, turn=turn),
            [((TOK, D), F32), ((TOK, 3 * D), BF16), ((OWN, D), BF16)] + ([] if last else halves),
            where, gradient, *gs, w_out, *packs, proj, k_probs, d_query, w_qkv, x,
            d_in, d_proj, g_low,
            scratch=[pltpu.VMEM((REGION, D), BF16)], flops=1 << 30,
        )
    (part,) = call(
        weight_kernel, [((cols, 8 * chips, 4 * D), BF16)],
        where, nlow, d_proj, routed(d_proj, mate), pack, packs[1], g_low,
        scratch=[pltpu.VMEM((D, 4 * D), F32)], flops=1 << 30,
    )
    part = lax.all_to_all(part, "col", 0, 0, tiled=True)
    part = jnp.sum(part.astype(F32), axis=0).astype(BF16).reshape(chips, 8, 4 * D)
    part = lax.all_to_all(part, "z", 0, 0, tiled=True)
    qkv_part, out_part = call(
        functools.partial(total_kernel, scale=(row_total * col_total) ** (-0.5)),
        [((8, 3 * D), F32), ((8, D), F32)], where, part,
    )
    return d_in.reshape(1, 8, 16, D), qkv_part[None], out_part[None]


def solution(mesh):
    pipes, rows, cols = (mesh.shape[axis] for axis in ("pipe", "row", "col"))
    fine = Mesh(np.asarray(mesh.devices).reshape(pipes, rows // 2, 2, cols), AXES)
    row = ("z", "core")
    return jax.shard_map(
        functools.partial(body, (pipes, rows // 2, cols)),
        mesh=fine,
        in_specs=(
            P("pipe", row, "col", None),
            P("pipe", None, None),
            P("pipe", None, None),
            P(row, "col", None),
        ),
        out_specs=(
            P("pipe", row, "col", None),
            P("pipe", ("z", "core", "col"), None),
            P("pipe", ("z", "core", "col"), None),
        ),
        check_vma=False,
    )
```

```python
import functools

import jax
import jax.numpy as jnp
import numpy as np
from jax import lax
from jax.experimental import pallas as pl
from jax.experimental.pallas import tpu as pltpu
from jax.sharding import Mesh
from jax.sharding import PartitionSpec as P

F32 = jnp.float32
BF16 = jnp.bfloat16
AXES = ("pipe", "z", "core", "col")
D = 512
PAIRS = 4
TOK = 128
OWN = 256
REGION = 768
VMEM_LIMIT = 40 * 1024 * 1024


def nn(a, b):
    return lax.dot_general(a, b, (((1,), (0,)), ((), ())), preferred_element_type=F32)


def nt(a, b):
    return lax.dot_general(a, b, (((1,), (1,)), ((), ())), preferred_element_type=F32)


def tn(a, b):
    return lax.dot_general(a, b, (((0,), (0,)), ((), ())), preferred_element_type=F32)


def two_heads(block):
    lane = lax.broadcasted_iota(jnp.int32, block.shape, 1)
    zero = jnp.zeros_like(block)
    return jnp.concatenate(
        [jnp.where(lane < 64, block, zero), jnp.where(lane < 64, zero, block)], axis=0
    )


def one_block(stacked):
    half = stacked.shape[0] // 2
    lane = lax.broadcasted_iota(jnp.int32, (half, 128), 1)
    return jnp.where(lane < 64, stacked[:half], stacked[half:])


def place(index, core):
    piece = index >> 8
    inner = index & 255
    side = inner - 128
    is_centre = inner < 128
    row = jnp.where(is_centre, inner >> 4, (side & 63) >> 3)
    col = jnp.where(is_centre, inner & 15, jnp.where(side < 64, (side & 7) - 8, (side & 7) + 16))
    mate = jnp.where(core == 0, 8, -8)
    row = row + jnp.where(piece == 1, mate, jnp.where(piece == 2, -mate, 0))
    return row, col


def window(where_ref, keys_own):
    row0, col0, core, rows, cols = (where_ref[i] for i in range(5))
    own = lax.broadcasted_iota(jnp.int32, (TOK, 1), 0)
    reach_row, reach_col = place(lax.broadcasted_iota(jnp.int32, (1, REGION), 1), core)
    grid_row, grid_col = row0 + reach_row, col0 + reach_col
    inside = (grid_row >= 0) & (grid_row < rows) & (grid_col >= 0) & (grid_col < cols)
    reach_row = jnp.where(inside, reach_row, 1 << 20)
    if keys_own:
        step_row, step_col = (own >> 4) - reach_row, (own & 15) - reach_col
    else:
        step_row, step_col = reach_row - (own >> 4), reach_col - (own & 15)
    return (step_row >= -8) & (step_row <= 7) & (step_col >= -8) & (step_col <= 7)


def put_sides(block, left_ref, right_ref):
    sides = block.reshape(8, 2, 8, block.shape[-1])
    left_ref[...] = sides[:, 0].reshape(64, -1).astype(BF16)
    right_ref[...] = sides[:, 1].reshape(64, -1).astype(BF16)


def forward_kernel(
    where_ref, x0, x1, x2, w_ref, cot_ref, proj_ref, prob_ref, nlow_ref, pack_ref, left_ref, right_ref
):
    for piece, x_ref in enumerate((x0, x1, x2)):
        x = x_ref[...].astype(F32)
        inverse = lax.rsqrt(jnp.mean(x * x, axis=-1, keepdims=True) + 1e-06)
        low = (x * inverse).astype(BF16)
        if piece < 2:
            nlow_ref[piece * TOK : (piece + 1) * TOK] = low[:TOK]
        proj_ref[piece * OWN : (piece + 1) * OWN] = nn(low, w_ref[...]).astype(BF16)
    ok = window(where_ref, False)
    ok2 = jnp.concatenate([ok, ok], axis=0)
    lane = lax.broadcasted_iota(jnp.int32, (TOK, 128), 1)
    stats = jnp.zeros((TOK, 128), F32)
    for pair in range(PAIRS):
        at = slice(128 * pair, 128 * pair + 128)
        query = two_heads(proj_ref[:TOK, at] * 0.125)
        scores = nt(query, proj_ref[:, D + 128 * pair : D + 128 * pair + 128])
        scores = jnp.where(ok2, scores, -1e30)
        highest = jnp.max(scores, axis=-1, keepdims=True)
        grown = jnp.exp(scores - highest)
        total = jnp.sum(grown, axis=-1, keepdims=True)
        probs = (grown * (1.0 / total)).astype(BF16)
        prob_ref[pair] = probs
        value = proj_ref[:, 2 * D + 128 * pair : 2 * D + 128 * pair + 128]
        pack_ref[:, at] = one_block(nn(probs, value)).astype(BF16)
        log_total = highest + jnp.log(total)
        rest = log_total
        for part in range(3):
            piece = rest.astype(BF16).astype(F32)
            rest = rest - piece
            for head in range(2):
                chosen = lane == 8 * part + 2 * pair + head
                stats = jnp.where(chosen, piece[TOK * head : TOK * head + TOK], stats)
    pack_ref[:, D : D + 128] = stats.astype(BF16)
    pack_ref[:, D + 128 :] = cot_ref[...].astype(BF16)
    put_sides(pack_ref[...].astype(F32), left_ref, right_ref)


def key_probs_kernel(where_ref, p0, p1, p2, proj_ref, prob_ref):
    head = lax.broadcasted_iota(jnp.int32, (8, 128), 0)
    lane = lax.broadcasted_iota(jnp.int32, (8, 128), 1)
    chosen = ((lane & 7) == head) & (lane < 24)
    pick = jnp.where(chosen, 1.0, 0.0).astype(BF16)
    stats = jnp.concatenate([p[:, D : D + 128] for p in (p0, p1, p2)], axis=0)
    log_total = nt(pick, stats)
    ok = window(where_ref, True)
    for pair in range(PAIRS):
        key = two_heads(proj_ref[:TOK, D + 128 * pair : D + 128 * pair + 128] * 0.125)
        scores = nt(key, proj_ref[:, 128 * pair : 128 * pair + 128])
        for side in range(2):
            at = 2 * pair + side
            part = scores[TOK * side : TOK * side + TOK] - log_total[at : at + 1]
            probs = jnp.exp(jnp.where(ok, part, -1e30))
            prob_ref[pair, TOK * side : TOK * side + TOK] = probs.astype(BF16)


def query_kernel(where_ref, g_ref, w_ref, pack_ref, proj_ref, prob_ref, dq_ref, *, turn):
    @pl.when(where_ref[5] == turn)
    def _():
        d_mixed = nt(g_ref[...].astype(BF16), w_ref[...]).astype(BF16)
        lane = lax.broadcasted_iota(jnp.int32, (TOK, 128), 1)
        for pair in range(PAIRS):
            at = slice(128 * pair, 128 * pair + 128)
            grad = d_mixed[:, at]
            prod = grad.astype(F32) * pack_ref[:, at].astype(F32)
            delta = jnp.concatenate(
                [
                    jnp.sum(jnp.where(lane < 64, prod, 0.0), axis=-1, keepdims=True),
                    jnp.sum(jnp.where(lane < 64, 0.0, prod), axis=-1, keepdims=True),
                ],
                axis=0,
            )
            value = proj_ref[:, 2 * D + 128 * pair : 2 * D + 128 * pair + 128]
            pressure = nt(two_heads(grad), value)
            slopes = (prob_ref[pair].astype(F32) * (pressure - delta)).astype(BF16)
            key = proj_ref[:, D + 128 * pair : D + 128 * pair + 128]
            dq_ref[:, at] = (one_block(nn(slopes, key)) * 0.125).astype(BF16)


def key_kernel(
    where_ref, g_ref, g0, g1, g2, wo_ref, p0, p1, p2, proj_ref, prob_ref, dq_ref, wq_ref, x_ref,
    *rest, turn,
):
    prev, rest = (rest[:3], rest[3:]) if turn else ((), rest)
    (in_ref, dp_ref, gl_ref), sends, dm_ref = rest[:3], rest[3:-1], rest[-1]
    active = where_ref[5] == turn

    if prev:

        @pl.when(jnp.logical_not(active))
        def _():
            for new, old in zip((in_ref, dp_ref, gl_ref), prev):
                new[...] = old[...]

    @pl.when(active)
    def _():
        head = lax.broadcasted_iota(jnp.int32, (8, D), 0)
        lane = lax.broadcasted_iota(jnp.int32, (8, D), 1)
        pick = jnp.where((lane >> 6) == head, 1.0, 0.0).astype(BF16)
        deltas = []
        for piece, (g, p) in enumerate(((g0, p0), (g1, p1), (g2, p2))):
            d_mixed = nt(g[:, -D:], wo_ref[...]).astype(BF16)
            dm_ref[piece * OWN : (piece + 1) * OWN] = d_mixed
            prod = d_mixed.astype(F32) * p[:, :D].astype(F32)
            high = prod.astype(BF16)
            rest = (prod - high.astype(F32)).astype(BF16)
            deltas.append(nt(pick, high) + nt(pick, rest))
        delta = jnp.concatenate(deltas, axis=1)
        dp_ref[:, :D] = dq_ref[...]
        for pair in range(PAIRS):
            at = slice(128 * pair, 128 * pair + 128)
            value = two_heads(proj_ref[:TOK, 2 * D + 128 * pair : 2 * D + 128 * pair + 128])
            grad = dm_ref[:, at]
            pressure = nt(value, grad)
            probs = prob_ref[pair]
            d_value = nn(probs, grad)
            slopes = []
            for side in range(2):
                h = 2 * pair + side
                rows = slice(TOK * side, TOK * side + TOK)
                slopes.append(
                    (probs[rows].astype(F32) * (pressure[rows] - delta[h : h + 1])).astype(BF16)
                )
            d_key = nn(jnp.concatenate(slopes, axis=0), proj_ref[:, at])
            dp_ref[:, D + 128 * pair : D + 128 * pair + 128] = (one_block(d_key) * 0.125).astype(BF16)
            dp_ref[:, 2 * D + 128 * pair : 2 * D + 128 * pair + 128] = one_block(d_value).astype(BF16)
        d_normed = nt(dp_ref[...], wq_ref[...])
        x = x_ref[...].astype(F32)
        inverse = lax.rsqrt(jnp.mean(x * x, axis=-1, keepdims=True) + 1e-06)
        normed = x * inverse
        inner = jnp.mean(d_normed * normed, axis=-1, keepdims=True)
        gradient = g_ref[...].astype(F32)
        out = gradient + inverse * (d_normed - normed * inner)
        in_ref[...] = out
        gl_ref[:TOK] = g_ref[...].astype(BF16)
        gl_ref[TOK:] = g1[:TOK, -D:]
        if sends:
            low_ref, left_ref, right_ref = sends
            low_ref[...] = out.astype(BF16)
            put_sides(out, left_ref, right_ref)


def weight_kernel(where_ref, n_ref, d0, d1, m0, m1, g_ref, out_ref, full_ref):
    core = where_ref[2]
    full_ref[:, : 3 * D] = tn(n_ref[:TOK], d0[...]) + tn(n_ref[TOK:], d1[...])
    full_ref[:, 3 * D :] = tn(m0[:, :D], g_ref[:TOK]) + tn(m1[:TOK, :D], g_ref[TOK:])
    chips, cols = out_ref.shape[1] // 8, out_ref.shape[0]
    for col in range(cols):
        rows = [
            full_ref[pl.ds(pl.multiple_of((2 * chip + core) * (8 * cols) + 8 * col, 8), 8)]
            for chip in range(chips)
        ]
        out_ref[col] = jnp.concatenate(rows, axis=0).astype(BF16)


def total_kernel(where_ref, part_ref, qkv_ref, out_ref, *, scale):
    total = part_ref[0].astype(F32)
    for source in range(1, part_ref.shape[0]):
        total = total + part_ref[source].astype(F32)
    qkv_ref[...] = total[:, : 3 * D] * scale
    out_ref[...] = total[:, 3 * D :] * scale


def stage_kernel(*refs):
    sources, targets, sems = refs[: len(refs) // 2], refs[len(refs) // 2 : -1], refs[-1]
    copies = [
        pltpu.make_async_copy(source, target, sems.at[at])
        for at, (source, target) in enumerate(zip(sources, targets))
    ]
    for copy in copies:
        copy.start()
    for copy in copies:
        copy.wait()


def staged(*arrays):
    return pl.pallas_call(
        stage_kernel,
        out_shape=[jax.ShapeDtypeStruct(a.shape, a.dtype) for a in arrays],
        in_specs=[pl.BlockSpec(memory_space=pl.ANY)] * len(arrays),
        out_specs=[pl.BlockSpec(memory_space=pltpu.VMEM)] * len(arrays),
        scratch_shapes=[pltpu.SemaphoreType.DMA((len(arrays),))],
        cost_estimate=pl.CostEstimate(flops=0, bytes_accessed=6 << 20, transcendentals=0),
    )(*arrays)


def call(kernel, outs, *args, scratch=(), flops=0):
    vmem = pl.BlockSpec(memory_space=pltpu.VMEM)
    return pl.pallas_call(
        kernel,
        out_shape=[jax.ShapeDtypeStruct(s, t) for s, t in outs],
        in_specs=[pl.BlockSpec(memory_space=pltpu.SMEM)] + [vmem] * (len(args) - 1),
        out_specs=[vmem] * len(outs),
        scratch_shapes=list(scratch),
        compiler_params=pltpu.CompilerParams(vmem_limit_bytes=VMEM_LIMIT),
        cost_estimate=pl.CostEstimate(flops=flops, bytes_accessed=4 << 20, transcendentals=0),
    )(*args)


def body(sizes, activations, qkv_weight, out_weight, cotangent):
    pipes, chips, cols = sizes

    def routed(block, step, plane=None):
        pairs = []
        for p in range(pipes):
            for z in range(chips):
                for k in range(2):
                    for c in range(cols):
                        if plane is not None and p != plane:
                            continue
                        p2, r2, c2 = step(p, 2 * z + k, c)
                        if 0 <= p2 < pipes and 0 <= r2 < 2 * chips and 0 <= c2 < cols:
                            source = (p * 2 * chips + 2 * z + k) * cols + c
                            pairs.append((source, (p2 * 2 * chips + r2) * cols + c2))
        return lax.ppermute(block, AXES, pairs)

    def col_rims(left_half, right_half, down=0, plane=None):
        left = routed(right_half, lambda p, r, c: (p - down, r, c + 1), plane)
        right = routed(left_half, lambda p, r, c: (p - down, r, c - 1), plane)
        return left, right

    def mate(p, r, c):
        return p, r ^ 1, c

    def row_rims(pieces, plane=None, beside=None):
        own = jnp.concatenate(pieces, axis=0)
        beyond = routed(own, lambda p, r, c: (p, r - 1 + 2 * (r & 1), c), plane)
        if beside is None:
            return own, routed(own, mate, plane), beyond
        late, done = lax.optimization_barrier((own, beside()))
        return (own, routed(late, mate, plane), beyond), done

    pipe, z, core, col = (lax.axis_index(axis) for axis in AXES)
    x = activations.reshape(TOK, D)
    w_qkv, w_out = qkv_weight[0], out_weight[0]
    cot = cotangent.reshape(TOK, D)
    row_total, col_total = 16 * chips, 16 * cols
    where = jnp.stack(
        [8 * (2 * z + core), 16 * col, core, row_total, col_total, pipes - 1 - pipe]
    ).astype(jnp.int32)

    x_sides = x.reshape(8, 2, 8, D)
    xs = row_rims([x, *col_rims(x_sides[:, 0].reshape(64, D), x_sides[:, 1].reshape(64, D))])
    x, cot, w_qkv, w_out = staged(x, cot, w_qkv, w_out)
    wide = 2 * D + 128
    proj, q_probs, nlow, pack, low_side, high_side = call(
        forward_kernel,
        [((REGION, 3 * D), BF16), ((PAIRS, OWN, REGION), BF16), ((OWN, D), BF16),
         ((TOK, wide), BF16), ((64, wide), BF16), ((64, wide), BF16)],
        where, *xs, w_qkv, cot, flops=2 << 30,
    )

    def query_side(turn, gradient):
        return call(
            functools.partial(query_kernel, turn=turn), [((TOK, D), BF16)],
            where, gradient, w_out, pack, proj, q_probs, flops=1 << 29,
        )[0]

    gradient = cot
    packs, d_query = row_rims(
        [pack, *col_rims(low_side, high_side)], beside=lambda: query_side(0, cot)
    )
    gs = packs
    (k_probs,) = call(
        key_probs_kernel, [((PAIRS, OWN, REGION), BF16)], where, *packs, proj, flops=1 << 28
    )
    state = ()
    for turn in range(pipes):
        plane, last = pipes - 1 - turn, turn == pipes - 1
        if turn > 0:
            low, low_side, high_side = sends
            gradient = routed(low, lambda p, r, c: (p - 1, r, c), plane + 1)
            sides = col_rims(low_side, high_side, 1, plane + 1)
            gs, d_query = row_rims(
                [gradient, *sides], plane, lambda: query_side(turn, gradient)
            )
        halves = [((TOK, D), BF16), ((64, D), BF16), ((64, D), BF16)]
        outs = call(
            functools.partial(key_kernel, turn=turn),
            [((TOK, D), F32), ((TOK, 3 * D), BF16), ((OWN, D), BF16)] + ([] if last else halves),
            where, gradient, *gs, w_out, *packs, proj, k_probs, d_query, w_qkv, x, *state,
            scratch=[pltpu.VMEM((REGION, D), BF16)], flops=1 << 30,
        )
        state, sends = outs[:3], outs[3:]
    d_in, d_proj, g_low = state
    (part,) = call(
        weight_kernel, [((cols, 8 * chips, 4 * D), BF16)],
        where, nlow, d_proj, routed(d_proj, mate), pack, packs[1], g_low,
        scratch=[pltpu.VMEM((D, 4 * D), F32)], flops=1 << 30,
    )
    part = lax.all_to_all(part, "col", 0, 0, tiled=True)
    part = jnp.sum(part.astype(F32), axis=0).astype(BF16).reshape(chips, 8, 4 * D)
    part = lax.all_to_all(part, "z", 0, 0, tiled=True)
    qkv_part, out_part = call(
        functools.partial(total_kernel, scale=(row_total * col_total) ** (-0.5)),
        [((8, 3 * D), F32), ((8, D), F32)], where, part,
    )
    return d_in.reshape(1, 8, 16, D), qkv_part[None], out_part[None]


def solution(mesh):
    pipes, rows, cols = (mesh.shape[axis] for axis in ("pipe", "row", "col"))
    fine = Mesh(np.asarray(mesh.devices).reshape(pipes, rows // 2, 2, cols), AXES)
    row = ("z", "core")
    return jax.shard_map(
        functools.partial(body, (pipes, rows // 2, cols)),
        mesh=fine,
        in_specs=(
            P("pipe", row, "col", None),
            P("pipe", None, None),
            P("pipe", None, None),
            P(row, "col", None),
        ),
        out_specs=(
            P("pipe", row, "col", None),
            P("pipe", ("z", "core", "col"), None),
            P("pipe", ("z", "core", "col"), None),
        ),
        check_vma=False,
    )
```

```python
import functools

import jax
import jax.numpy as jnp
import numpy as np
from jax import lax
from jax.experimental import pallas as pl
from jax.experimental.pallas import tpu as pltpu
from jax.sharding import Mesh
from jax.sharding import PartitionSpec as P

F32 = jnp.float32
BF16 = jnp.bfloat16
AXES = ("pipe", "z", "core", "col")
D = 512
PAIRS = 4
TOK = 128
OWN = 256
REGION = 768
VMEM_LIMIT = 40 * 1024 * 1024


def nn(a, b):
    return lax.dot_general(a, b, (((1,), (0,)), ((), ())), preferred_element_type=F32)


def nt(a, b):
    return lax.dot_general(a, b, (((1,), (1,)), ((), ())), preferred_element_type=F32)


def tn(a, b):
    return lax.dot_general(a, b, (((0,), (0,)), ((), ())), preferred_element_type=F32)


def two_heads(block):
    lane = lax.broadcasted_iota(jnp.int32, block.shape, 1)
    zero = jnp.zeros_like(block)
    return jnp.concatenate(
        [jnp.where(lane < 64, block, zero), jnp.where(lane < 64, zero, block)], axis=0
    )


def one_block(stacked):
    half = stacked.shape[0] // 2
    lane = lax.broadcasted_iota(jnp.int32, (half, 128), 1)
    return jnp.where(lane < 64, stacked[:half], stacked[half:])


def place(index, core):
    piece = index >> 8
    inner = index & 255
    side = inner - 128
    is_centre = inner < 128
    row = jnp.where(is_centre, inner >> 4, (side & 63) >> 3)
    col = jnp.where(is_centre, inner & 15, jnp.where(side < 64, (side & 7) - 8, (side & 7) + 16))
    mate = jnp.where(core == 0, 8, -8)
    row = row + jnp.where(piece == 1, mate, jnp.where(piece == 2, -mate, 0))
    return row, col


def window(where_ref, keys_own):
    row0, col0, core, rows, cols = (where_ref[i] for i in range(5))
    own = lax.broadcasted_iota(jnp.int32, (TOK, 1), 0)
    reach_row, reach_col = place(lax.broadcasted_iota(jnp.int32, (1, REGION), 1), core)
    grid_row, grid_col = row0 + reach_row, col0 + reach_col
    inside = (grid_row >= 0) & (grid_row < rows) & (grid_col >= 0) & (grid_col < cols)
    reach_row = jnp.where(inside, reach_row, 1 << 20)
    if keys_own:
        step_row, step_col = (own >> 4) - reach_row, (own & 15) - reach_col
    else:
        step_row, step_col = reach_row - (own >> 4), reach_col - (own & 15)
    return (step_row >= -8) & (step_row <= 7) & (step_col >= -8) & (step_col <= 7)


def put_sides(block, left_ref, right_ref):
    sides = block.reshape(8, 2, 8, block.shape[-1])
    left_ref[...] = sides[:, 0].reshape(64, -1).astype(BF16)
    right_ref[...] = sides[:, 1].reshape(64, -1).astype(BF16)


def first_kernel(where_ref, x_ref, base_ref, left_ref, right_ref):
    base_ref[:TOK] = x_ref[...]
    base_ref[TOK:] = jnp.zeros((TOK, D), BF16)
    put_sides(x_ref[...].astype(F32), left_ref, right_ref)


def normed_low(x_ref):
    x = x_ref[...].astype(F32)
    inverse = lax.rsqrt(jnp.mean(x * x, axis=-1, keepdims=True) + 1e-06)
    return (x * inverse).astype(BF16)


def own_kernel(where_ref, x_ref, w_ref, cot_ref, proj_ref, nlow_ref, cot_low_ref):
    low = normed_low(x_ref)
    nlow_ref[...] = low[:TOK]
    proj_ref[...] = nn(low, w_ref[...]).astype(BF16)
    cot_low_ref[...] = cot_ref[...].astype(BF16)


def forward_kernel(
    where_ref, x1, x2, proj_ref, w_ref, cot_ref,
    kv_ref, prob_ref, nlow_ref, far_ref, pack_ref, left_ref, right_ref,
):
    kv_ref[:OWN] = proj_ref[:, D:]
    for piece, x_ref in enumerate((x1, x2)):
        low = normed_low(x_ref)
        far_ref[piece * OWN : (piece + 1) * OWN] = low
        if piece == 0:
            nlow_ref[...] = low[:TOK]
        kv_ref[(piece + 1) * OWN : (piece + 2) * OWN] = nn(low, w_ref[:, D:]).astype(BF16)
    ok = window(where_ref, False)
    ok2 = jnp.concatenate([ok, ok], axis=0)
    lane = lax.broadcasted_iota(jnp.int32, (TOK, 128), 1)
    stats = jnp.zeros((TOK, 128), F32)
    for pair in range(PAIRS):
        at = slice(128 * pair, 128 * pair + 128)
        query = two_heads(proj_ref[:TOK, at] * 0.125)
        scores = nt(query, kv_ref[:, at])
        scores = jnp.where(ok2, scores, -1e30)
        highest = jnp.max(scores, axis=-1, keepdims=True)
        grown = jnp.exp(scores - highest)
        total = jnp.sum(grown, axis=-1, keepdims=True)
        probs = (grown * (1.0 / total)).astype(BF16)
        prob_ref[pair] = probs
        value = kv_ref[:, D + 128 * pair : D + 128 * pair + 128]
        pack_ref[:, at] = one_block(nn(probs, value)).astype(BF16)
        log_total = highest + jnp.log(total)
        rest = log_total
        for part in range(3):
            piece = rest.astype(BF16).astype(F32)
            rest = rest - piece
            for head in range(2):
                chosen = lane == 8 * part + 2 * pair + head
                stats = jnp.where(chosen, piece[TOK * head : TOK * head + TOK], stats)
    pack_ref[:, D : D + 128] = stats.astype(BF16)
    pack_ref[:, D + 128 :] = cot_ref[...]
    put_sides(pack_ref[...].astype(F32), left_ref, right_ref)


def turned_kernel(where_ref, proj_ref, far_ref, w_ref, query_ref):
    query_ref[:, :OWN] = proj_ref[:, :D].astype(F32).T.astype(BF16)
    far = nn(far_ref[...], w_ref[:, :D]).astype(BF16)
    query_ref[:, OWN:] = far.astype(F32).T.astype(BF16)


def key_probs_kernel(where_ref, p0, p1, p2, proj_ref, query_ref, prob_ref, mixed_ref):
    head = lax.broadcasted_iota(jnp.int32, (8, 128), 0)
    lane = lax.broadcasted_iota(jnp.int32, (8, 128), 1)
    chosen = ((lane & 7) == head) & (lane < 24)
    pick = jnp.where(chosen, 1.0, 0.0).astype(BF16)
    stats = jnp.concatenate([p[:, D : D + 128] for p in (p0, p1, p2)], axis=0)
    log_total = nt(pick, stats)
    for piece, p in enumerate((p0, p1, p2)):
        mixed_ref[:, piece * OWN : (piece + 1) * OWN] = p[:, :D].astype(F32).T.astype(BF16)
    ok = window(where_ref, True)
    for pair in range(PAIRS):
        key = two_heads(proj_ref[:TOK, D + 128 * pair : D + 128 * pair + 128] * 0.125)
        scores = nn(key, query_ref[128 * pair : 128 * pair + 128])
        for side in range(2):
            at = 2 * pair + side
            part = scores[TOK * side : TOK * side + TOK] - log_total[at : at + 1]
            probs = jnp.exp(jnp.where(ok, part, -1e30))
            prob_ref[pair, TOK * side : TOK * side + TOK] = probs.astype(BF16)


def query_kernel(where_ref, g_ref, w_ref, pack_ref, kv_ref, prob_ref, dq_ref, *, turn):
    @pl.when(where_ref[5] == turn)
    def _():
        d_mixed = nt(g_ref[...].astype(BF16), w_ref[...]).astype(BF16)
        lane = lax.broadcasted_iota(jnp.int32, (TOK, 128), 1)
        for pair in range(PAIRS):
            at = slice(128 * pair, 128 * pair + 128)
            grad = d_mixed[:, at]
            prod = grad.astype(F32) * pack_ref[:, at].astype(F32)
            delta = jnp.concatenate(
                [
                    jnp.sum(jnp.where(lane < 64, prod, 0.0), axis=-1, keepdims=True),
                    jnp.sum(jnp.where(lane < 64, 0.0, prod), axis=-1, keepdims=True),
                ],
                axis=0,
            )
            value = kv_ref[:, D + 128 * pair : D + 128 * pair + 128]
            pressure = nt(two_heads(grad), value)
            slopes = (prob_ref[pair].astype(F32) * (pressure - delta)).astype(BF16)
            dq_ref[:, at] = (one_block(nn(slopes, kv_ref[:, at])) * 0.125).astype(BF16)


def turned_block(stacked):
    row = lax.broadcasted_iota(jnp.int32, (128, 128), 0)
    return jnp.where(row < 64, stacked[:, :128], stacked[:, 128:]).T


def key_kernel(
    where_ref, g_ref, g0, g1, g2, wo_ref, mixed_ref, proj_ref, query_ref, prob_ref, dq_ref, wq_ref,
    x_ref, *rest, turn,
):
    prev, rest = (rest[:3], rest[3:]) if turn else ((), rest)
    (in_ref, dp_ref, gl_ref), sends, dm_ref = rest[:3], rest[3:-1], rest[-1]
    active = where_ref[5] == turn

    if prev:

        @pl.when(jnp.logical_not(active))
        def _():
            for new, old in zip((in_ref, dp_ref, gl_ref), prev):
                new[...] = old[...]

    @pl.when(active)
    def _():
        for piece, g in enumerate((g0, g1, g2)):
            d_mixed = nt(wo_ref[...], g[:, -D:]).astype(BF16)
            dm_ref[:, piece * OWN : (piece + 1) * OWN] = d_mixed
        dp_ref[:, :D] = dq_ref[...]
        for pair in range(PAIRS):
            at = slice(128 * pair, 128 * pair + 128)
            value = two_heads(proj_ref[:TOK, 2 * D + 128 * pair : 2 * D + 128 * pair + 128])
            grad = dm_ref[at]
            prod = grad.astype(F32) * mixed_ref[at].astype(F32)
            pressure = nn(value, grad)
            probs = prob_ref[pair]
            d_value = nt(grad, probs)
            slopes = []
            for side in range(2):
                delta = jnp.sum(prod[64 * side : 64 * side + 64], axis=0, keepdims=True)
                rows = slice(TOK * side, TOK * side + TOK)
                slopes.append((probs[rows].astype(F32) * (pressure[rows] - delta)).astype(BF16))
            d_key = nt(query_ref[at], jnp.concatenate(slopes, axis=0))
            low, high = D + 128 * pair, D + 128 * pair + 128
            dp_ref[:, low:high] = (turned_block(d_key) * 0.125).astype(BF16)
            dp_ref[:, D + low : D + high] = turned_block(d_value).astype(BF16)
        d_normed = nt(dp_ref[...], wq_ref[...])
        x = x_ref[...].astype(F32)
        inverse = lax.rsqrt(jnp.mean(x * x, axis=-1, keepdims=True) + 1e-06)
        normed = x * inverse
        inner = jnp.mean(d_normed * normed, axis=-1, keepdims=True)
        gradient = g_ref[...].astype(F32)
        out = gradient + inverse * (d_normed - normed * inner)
        in_ref[...] = out
        gl_ref[:TOK] = g_ref[...].astype(BF16)
        gl_ref[TOK:] = g1[:TOK, -D:]
        if sends:
            low_ref, left_ref, right_ref = sends
            low_ref[...] = out.astype(BF16)
            put_sides(out, left_ref, right_ref)


def weight_kernel(where_ref, n0, n1, d0, d1, m0, m1, g_ref, out_ref, full_ref):
    core = where_ref[2]
    full_ref[:, : 3 * D] = tn(n0[...], d0[...]) + tn(n1[...], d1[...])
    full_ref[:, 3 * D :] = tn(m0[:, :D], g_ref[:TOK]) + tn(m1[:TOK, :D], g_ref[TOK:])
    chips, cols = out_ref.shape[1] // 8, out_ref.shape[0]
    for col in range(cols):
        rows = [
            full_ref[pl.ds(pl.multiple_of((2 * chip + core) * (8 * cols) + 8 * col, 8), 8)]
            for chip in range(chips)
        ]
        out_ref[col] = jnp.concatenate(rows, axis=0).astype(BF16)


def total_kernel(where_ref, part_ref, qkv_ref, out_ref, *, scale):
    total = part_ref[0].astype(F32)
    for source in range(1, part_ref.shape[0]):
        total = total + part_ref[source].astype(F32)
    qkv_ref[...] = total[:, : 3 * D] * scale
    out_ref[...] = total[:, 3 * D :] * scale


def call(kernel, outs, *args, scratch=(), flops=0):
    vmem = pl.BlockSpec(memory_space=pltpu.VMEM)
    return pl.pallas_call(
        kernel,
        out_shape=[jax.ShapeDtypeStruct(s, t) for s, t in outs],
        in_specs=[pl.BlockSpec(memory_space=pltpu.SMEM)] + [vmem] * (len(args) - 1),
        out_specs=[vmem] * len(outs),
        scratch_shapes=list(scratch),
        compiler_params=pltpu.CompilerParams(vmem_limit_bytes=VMEM_LIMIT),
        cost_estimate=pl.CostEstimate(flops=flops, bytes_accessed=4 << 20, transcendentals=0),
    )(*args)


def body(sizes, activations, qkv_weight, out_weight, cotangent):
    pipes, chips, cols = sizes

    def routed(block, step, plane=None):
        pairs = []
        for p in range(pipes):
            for z in range(chips):
                for k in range(2):
                    for c in range(cols):
                        if plane is not None and p != plane:
                            continue
                        p2, r2, c2 = step(p, 2 * z + k, c)
                        if 0 <= p2 < pipes and 0 <= r2 < 2 * chips and 0 <= c2 < cols:
                            source = (p * 2 * chips + 2 * z + k) * cols + c
                            pairs.append((source, (p2 * 2 * chips + r2) * cols + c2))
        return lax.ppermute(block, AXES, pairs)

    def col_rims(left_half, right_half, down=0, plane=None):
        left = routed(right_half, lambda p, r, c: (p - down, r, c + 1), plane)
        right = routed(left_half, lambda p, r, c: (p - down, r, c - 1), plane)
        return left, right

    def mate(p, r, c):
        return p, r ^ 1, c

    def row_rims(pieces, plane=None):
        own = jnp.concatenate(pieces, axis=0)
        beyond = routed(own, lambda p, r, c: (p, r - 1 + 2 * (r & 1), c), plane)
        return own, routed(own, mate, plane), beyond

    pipe, z, core, col = (lax.axis_index(axis) for axis in AXES)
    x = activations.reshape(TOK, D)
    w_qkv, w_out = qkv_weight[0], out_weight[0]
    cot = cotangent.reshape(TOK, D)
    row_total, col_total = 16 * chips, 16 * cols
    where = jnp.stack(
        [8 * (2 * z + core), 16 * col, core, row_total, col_total, pipes - 1 - pipe]
    ).astype(jnp.int32)

    base, low_side, high_side = call(
        first_kernel, [((OWN, D), BF16), ((64, D), BF16), ((64, D), BF16)], where, x
    )
    left, right = col_rims(low_side, high_side)
    own = lax.dynamic_update_slice(base, left, (TOK, 0))
    own, near, far = row_rims([lax.dynamic_update_slice(own, right, (TOK + 64, 0))])
    proj, nlow, cot_low = call(
        own_kernel, [((OWN, 3 * D), BF16), ((TOK, D), BF16), ((TOK, D), BF16)],
        where, own, w_qkv, cot, flops=1 << 29,
    )
    wide = 2 * D + 128
    kv, q_probs, nlow_mate, low_far, pack, low_side, high_side = call(
        forward_kernel,
        [((REGION, 2 * D), BF16), ((PAIRS, OWN, REGION), BF16), ((TOK, D), BF16),
         ((2 * OWN, D), BF16), ((TOK, wide), BF16), ((64, wide), BF16), ((64, wide), BF16)],
        where, near, far, proj, w_qkv, cot_low, flops=2 << 30,
    )
    packs = row_rims([pack, *col_rims(low_side, high_side)])
    (queries,) = call(
        turned_kernel, [((D, REGION), BF16)], where, proj, low_far, w_qkv, flops=1 << 28
    )
    k_probs, mixed = call(
        key_probs_kernel, [((PAIRS, OWN, REGION), BF16), ((D, REGION), BF16)],
        where, *packs, proj, queries, flops=1 << 28,
    )
    gradient, gs = cot, packs
    state = ()
    for turn in range(pipes):
        plane, last = pipes - 1 - turn, turn == pipes - 1
        if turn > 0:
            low, low_side, high_side = sends
            gradient = routed(low, lambda p, r, c: (p - 1, r, c), plane + 1)
            gs = row_rims([gradient, *col_rims(low_side, high_side, 1, plane + 1)], plane)
        (d_query,) = call(
            functools.partial(query_kernel, turn=turn), [((TOK, D), BF16)],
            where, gradient, w_out, pack, kv, q_probs, flops=1 << 29,
        )
        halves = [((TOK, D), BF16), ((64, D), BF16), ((64, D), BF16)]
        outs = call(
            functools.partial(key_kernel, turn=turn),
            [((TOK, D), F32), ((TOK, 3 * D), BF16), ((OWN, D), BF16)] + ([] if last else halves),
            where, gradient, *gs, w_out, mixed, proj, queries, k_probs, d_query, w_qkv, x, *state,
            scratch=[pltpu.VMEM((D, REGION), BF16)], flops=1 << 30,
        )
        state, sends = outs[:3], outs[3:]
    d_in, d_proj, g_low = state
    (part,) = call(
        weight_kernel, [((cols, 8 * chips, 4 * D), BF16)],
        where, nlow, nlow_mate, d_proj, routed(d_proj, mate), pack, packs[1], g_low,
        scratch=[pltpu.VMEM((D, 4 * D), F32)], flops=1 << 30,
    )
    part = lax.all_to_all(part, "col", 0, 0, tiled=True)
    part = jnp.sum(part.astype(F32), axis=0).astype(BF16).reshape(chips, 8, 4 * D)
    part = lax.all_to_all(part, "z", 0, 0, tiled=True)
    qkv_part, out_part = call(
        functools.partial(total_kernel, scale=(row_total * col_total) ** (-0.5)),
        [((8, 3 * D), F32), ((8, D), F32)], where, part,
    )
    return d_in.reshape(1, 8, 16, D), qkv_part[None], out_part[None]


def solution(mesh):
    pipes, rows, cols = (mesh.shape[axis] for axis in ("pipe", "row", "col"))
    fine = Mesh(np.asarray(mesh.devices).reshape(pipes, rows // 2, 2, cols), AXES)
    row = ("z", "core")
    return jax.shard_map(
        functools.partial(body, (pipes, rows // 2, cols)),
        mesh=fine,
        in_specs=(
            P("pipe", row, "col", None),
            P("pipe", None, None),
            P("pipe", None, None),
            P(row, "col", None),
        ),
        out_specs=(
            P("pipe", row, "col", None),
            P("pipe", ("z", "core", "col"), None),
            P("pipe", ("z", "core", "col"), None),
        ),
        check_vma=False,
    )
```

```python
import functools

import jax
import jax.numpy as jnp
import numpy as np
from jax import lax
from jax.experimental import pallas as pl
from jax.experimental.pallas import tpu as pltpu
from jax.sharding import Mesh
from jax.sharding import PartitionSpec as P

F32 = jnp.float32
BF16 = jnp.bfloat16
AXES = ("pipe", "z", "core", "col")
D = 512
PAIRS = 4
TOK = 128
OWN = 256
REGION = 768
BLOCK = 32
VMEM_LIMIT = 40 * 1024 * 1024


def nn(a, b):
    return lax.dot_general(a, b, (((1,), (0,)), ((), ())), preferred_element_type=F32)


def nt(a, b):
    return lax.dot_general(a, b, (((1,), (1,)), ((), ())), preferred_element_type=F32)


def tn(a, b):
    return lax.dot_general(a, b, (((0,), (0,)), ((), ())), preferred_element_type=F32)


def two_heads(block):
    lane = lax.broadcasted_iota(jnp.int32, block.shape, 1)
    zero = jnp.zeros_like(block)
    return jnp.concatenate(
        [jnp.where(lane < 64, block, zero), jnp.where(lane < 64, zero, block)], axis=0
    )


def one_block(stacked):
    half = stacked.shape[0] // 2
    lane = lax.broadcasted_iota(jnp.int32, (half, 128), 1)
    return jnp.where(lane < 64, stacked[:half], stacked[half:])


def place(index, core):
    piece = index >> 8
    inner = index & 255
    side = inner - 128
    is_centre = inner < 128
    row = jnp.where(is_centre, inner >> 4, (side & 63) >> 3)
    col = jnp.where(is_centre, inner & 15, jnp.where(side < 64, (side & 7) - 8, (side & 7) + 16))
    mate = jnp.where(core == 0, 8, -8)
    row = row + jnp.where(piece == 1, mate, jnp.where(piece == 2, -mate, 0))
    return row, col


def window(where_ref, keys_own):
    row0, col0, core, rows, cols = (where_ref[i] for i in range(5))
    own = lax.broadcasted_iota(jnp.int32, (TOK, 1), 0)
    reach_row, reach_col = place(lax.broadcasted_iota(jnp.int32, (1, REGION), 1), core)
    grid_row, grid_col = row0 + reach_row, col0 + reach_col
    inside = (grid_row >= 0) & (grid_row < rows) & (grid_col >= 0) & (grid_col < cols)
    reach_row = jnp.where(inside, reach_row, 1 << 20)
    if keys_own:
        step_row, step_col = (own >> 4) - reach_row, (own & 15) - reach_col
    else:
        step_row, step_col = reach_row - (own >> 4), reach_col - (own & 15)
    return (step_row >= -8) & (step_row <= 7) & (step_col >= -8) & (step_col <= 7)


def put_sides(block, left_ref, right_ref):
    sides = block.reshape(8, 2, 8, block.shape[-1])
    left_ref[...] = sides[:, 0].reshape(64, -1).astype(BF16)
    right_ref[...] = sides[:, 1].reshape(64, -1).astype(BF16)


def first_kernel(where_ref, x_ref, base_ref, left_ref, right_ref):
    base_ref[:TOK] = x_ref[...]
    base_ref[TOK:] = jnp.zeros((TOK, D), BF16)
    put_sides(x_ref[...].astype(F32), left_ref, right_ref)


def normed_low(x_ref):
    x = x_ref[...].astype(F32)
    inverse = lax.rsqrt(jnp.mean(x * x, axis=-1, keepdims=True) + 1e-06)
    return (x * inverse).astype(BF16)


def centre_kernel(where_ref, x_ref, w_ref, wo_ref, cot_ref, proj_ref, nlow_ref, cot_low_ref, dm_ref):
    low = normed_low(x_ref)
    nlow_ref[...] = low
    proj_ref[...] = nn(low, w_ref[...]).astype(BF16)
    grad = cot_ref[...].astype(BF16)
    cot_low_ref[...] = grad
    dm_ref[...] = nt(grad, wo_ref[...]).astype(BF16)


def side_kernel(where_ref, left_ref, right_ref, w_ref, proj_ref):
    low = jnp.concatenate([normed_low(left_ref), normed_low(right_ref)], axis=0)
    proj_ref[...] = nn(low, w_ref[...]).astype(BF16)


def forward_kernel(
    where_ref, x1, x2, proj_ref, side_ref, w_ref, cot_ref, dm_ref,
    kv_ref, prob_ref, nlow_ref, far_ref, mixed_ref, pack_ref, left_ref, right_ref,
):
    kv_ref[:TOK] = proj_ref[:, D:]
    kv_ref[TOK:OWN] = side_ref[:, D:]
    for piece, x_ref in enumerate((x1, x2)):
        low = normed_low(x_ref)
        far_ref[piece * OWN : (piece + 1) * OWN] = low
        if piece == 0:
            nlow_ref[...] = low[:TOK]
        kv_ref[(piece + 1) * OWN : (piece + 2) * OWN] = nn(low, w_ref[:, D:]).astype(BF16)
    ok = window(where_ref, False)
    ok2 = jnp.concatenate([ok, ok], axis=0)
    lane = lax.broadcasted_iota(jnp.int32, (TOK, 128), 1)
    stats = jnp.zeros((TOK, 128), F32)
    for pair in range(PAIRS):
        at = slice(128 * pair, 128 * pair + 128)
        query = two_heads(proj_ref[:, at] * 0.125)
        scores = nt(query, kv_ref[:, at])
        scores = jnp.where(ok2, scores, -1e30)
        highest = jnp.max(scores, axis=-1, keepdims=True)
        grown = jnp.exp(scores - highest)
        total = jnp.sum(grown, axis=-1, keepdims=True)
        probs = (grown * (1.0 / total)).astype(BF16)
        prob_ref[pair] = probs
        value = kv_ref[:, D + 128 * pair : D + 128 * pair + 128]
        mixed = one_block(nn(probs, value)).astype(BF16)
        mixed_ref[:, at] = mixed
        log_total = highest + jnp.log(total)
        delta = two_sums(dm_ref[:, at], mixed)
        for first, rest in ((0, log_total), (24, delta)):
            for part in range(3):
                piece = rest.astype(BF16).astype(F32)
                rest = rest - piece
                for head in range(2):
                    chosen = lane == first + 8 * part + 2 * pair + head
                    stats = jnp.where(chosen, piece[TOK * head : TOK * head + TOK], stats)
    starts = where_ref[5] == 0
    pack_ref[:, D:] = stats.astype(BF16)

    @pl.when(starts)
    def _():
        pack_ref[:, :D] = cot_ref[...]

    @pl.when(jnp.logical_not(starts))
    def _():
        pack_ref[:, :D] = mixed_ref[...]

    put_sides(pack_ref[...].astype(F32), left_ref, right_ref)


def turned_kernel(where_ref, proj_ref, side_ref, far_ref, w_ref, n0, n1, query_ref, nt_ref, full_ref):
    query_ref[:, :TOK] = proj_ref[:, :D].astype(F32).T.astype(BF16)
    query_ref[:, TOK:OWN] = side_ref[:, :D].astype(F32).T.astype(BF16)
    far = nn(far_ref[...], w_ref[:, :D]).astype(BF16)
    query_ref[:, OWN:] = far.astype(F32).T.astype(BF16)
    full_ref[:, :TOK] = n0[...].astype(F32).T
    full_ref[:, TOK:] = n1[...].astype(F32).T
    nt_ref[...] = own_half(where_ref, full_ref).astype(BF16)


def own_half(where_ref, full_ref):
    rows = [
        full_ref[pl.ds(pl.multiple_of((2 * at + where_ref[2]) * BLOCK, BLOCK), BLOCK)]
        for at in range(full_ref.shape[0] // (2 * BLOCK))
    ]
    return jnp.concatenate(rows, axis=0)


def key_probs_kernel(
    where_ref, p0, p1, p2, proj_ref, query_ref, prob_ref, mixed_ref, delta_ref
):
    head = lax.broadcasted_iota(jnp.int32, (8, 128), 0)
    lane = lax.broadcasted_iota(jnp.int32, (8, 128), 1)
    stats = jnp.concatenate([p[:, D:] for p in (p0, p1, p2)], axis=0)
    sums = []
    for first in (0, 24):
        chosen = ((lane & 7) == head) & (lane >= first) & (lane < first + 24)
        sums.append(nt(jnp.where(chosen, 1.0, 0.0).astype(BF16), stats))
    log_total, delta_ref[...] = sums

    @pl.when(where_ref[5] != 0)
    def _():
        for piece, p in enumerate((p0, p1, p2)):
            mixed_ref[:, piece * OWN : (piece + 1) * OWN] = p[:, :D].astype(F32).T.astype(BF16)

    ok = window(where_ref, True)
    for pair in range(PAIRS):
        key = two_heads(proj_ref[:, D + 128 * pair : D + 128 * pair + 128] * 0.125)
        scores = nn(key, query_ref[128 * pair : 128 * pair + 128])
        for side in range(2):
            at = 2 * pair + side
            part = scores[TOK * side : TOK * side + TOK] - log_total[at : at + 1]
            probs = jnp.exp(jnp.where(ok, part, -1e30))
            prob_ref[pair, TOK * side : TOK * side + TOK] = probs.astype(BF16)


def two_sums(grad, mixed):
    prod = grad.astype(F32) * mixed.astype(F32)
    lane = lax.broadcasted_iota(jnp.int32, prod.shape, 1)
    return jnp.concatenate(
        [
            jnp.sum(jnp.where(lane < 64, prod, 0.0), axis=-1, keepdims=True),
            jnp.sum(jnp.where(lane < 64, 0.0, prod), axis=-1, keepdims=True),
        ],
        axis=0,
    )


def query_kernel(where_ref, g_ref, w_ref, mixed_ref, kv_ref, prob_ref, dq_ref, *, turn):
    @pl.when(where_ref[5] == turn)
    def _():
        d_mixed = nt(g_ref[...], w_ref[...]).astype(BF16)
        for pair in range(PAIRS):
            at = slice(128 * pair, 128 * pair + 128)
            grad = d_mixed[:, at]
            delta = two_sums(grad, mixed_ref[:, at])
            value = kv_ref[:, D + 128 * pair : D + 128 * pair + 128]
            pressure = nt(two_heads(grad), value)
            slopes = (prob_ref[pair].astype(F32) * (pressure - delta)).astype(BF16)
            dq_ref[:, at] = (one_block(nn(slopes, kv_ref[:, at])) * 0.125).astype(BF16)


def turned_block(stacked):
    row = lax.broadcasted_iota(jnp.int32, (128, 128), 0)
    return jnp.where(row < 64, stacked[:, :128], stacked[:, 128:]).T


def key_kernel(
    where_ref, g0, g1, g2, wo_ref, delta_ref, proj_ref, query_ref, prob_ref, dq_ref, mixed_ref,
    *rest, turn, last,
):
    ins, rest = ((), rest) if last else (rest[:3], rest[3:])
    prev = (3 - last) if turn else 0
    prev, rest = rest[:prev], rest[prev:]
    outs, sends, dm_ref = rest[: 3 - last], rest[3 - last : -1], rest[-1]
    dp_ref, gl_ref = outs[:2]
    active = where_ref[5] == turn

    if prev:

        @pl.when(jnp.logical_not(active))
        def _():
            for new, old in zip(outs, prev):
                new[...] = old[...]

    @pl.when(active)
    def _():
        for piece, g in enumerate((g0, g1, g2)):
            d_mixed = nt(wo_ref[...], g[:, :D]).astype(BF16)
            dm_ref[:, piece * OWN : (piece + 1) * OWN] = d_mixed
        dp_ref[:, :D] = dq_ref[...]
        dp_ref[:, 3 * D :] = mixed_ref[...]
        gl_ref[:TOK] = g0[:TOK, :D]
        gl_ref[TOK:] = g1[:TOK, :D]
        for pair in range(PAIRS):
            at = slice(128 * pair, 128 * pair + 128)
            value = two_heads(proj_ref[:, 2 * D + 128 * pair : 2 * D + 128 * pair + 128])
            grad = dm_ref[at]
            if turn:
                prod = grad.astype(F32) * delta_ref[at].astype(F32)
                deltas = [jnp.sum(prod[r : r + 64], axis=0, keepdims=True) for r in (0, 64)]
            else:
                deltas = [delta_ref[2 * pair + side : 2 * pair + side + 1] for side in range(2)]
            pressure = nn(value, grad)
            probs = prob_ref[pair]
            d_value = nt(grad, probs)
            slopes = []
            for side in range(2):
                rows = slice(TOK * side, TOK * side + TOK)
                slopes.append(
                    (probs[rows].astype(F32) * (pressure[rows] - deltas[side])).astype(BF16)
                )
            d_key = nt(query_ref[at], jnp.concatenate(slopes, axis=0))
            low, high = D + 128 * pair, D + 128 * pair + 128
            dp_ref[:, low:high] = (turned_block(d_key) * 0.125).astype(BF16)
            dp_ref[:, D + low : D + high] = turned_block(d_value).astype(BF16)
        if not last:
            out = input_grad(dp_ref, *ins)
            outs[2][...] = out
            low_ref, left_ref, right_ref = sends
            low_ref[...] = out.astype(BF16)
            put_sides(out, left_ref, right_ref)


def input_grad(dp_ref, g_ref, wq_ref, x_ref):
    d_normed = nt(dp_ref[:, : 3 * D], wq_ref[...])
    x = x_ref[...].astype(F32)
    inverse = lax.rsqrt(jnp.mean(x * x, axis=-1, keepdims=True) + 1e-06)
    normed = x * inverse
    inner = jnp.mean(d_normed * normed, axis=-1, keepdims=True)
    return g_ref[...].astype(F32) + inverse * (d_normed - normed * inner)


def input_kernel(where_ref, dp_ref, g_ref, wq_ref, x_ref, prev_ref, in_ref, *, turn):
    @pl.when(where_ref[5] == turn)
    def _():
        in_ref[...] = input_grad(dp_ref, g_ref, wq_ref, x_ref)

    @pl.when(where_ref[5] != turn)
    def _():
        in_ref[...] = prev_ref[...]


def weight_kernel(where_ref, nt_ref, d0, d1, g_ref, out_ref, full_ref):
    d_proj = jnp.concatenate([d0[:, : 3 * D], d1[:, : 3 * D]], axis=0)
    mixed = jnp.concatenate([d0[:, 3 * D :], d1[:, 3 * D :]], axis=0)
    full_ref[...] = tn(mixed, g_ref[...])
    left, right = nn(nt_ref[...], d_proj), own_half(where_ref, full_ref)
    cols = out_ref.shape[0]
    for col in range(cols):
        for at, part in ((slice(0, 3 * D), left), (slice(3 * D, 4 * D), right)):
            rows = [
                part[BLOCK * chip + 8 * col : BLOCK * chip + 8 * col + 8]
                for chip in range(out_ref.shape[1] // 8)
            ]
            out_ref[col, :, at] = jnp.concatenate(rows, axis=0).astype(BF16)


def total_kernel(where_ref, part_ref, qkv_ref, out_ref, *, scale):
    total = part_ref[0].astype(F32)
    for source in range(1, part_ref.shape[0]):
        total = total + part_ref[source].astype(F32)
    qkv_ref[...] = total[:, : 3 * D] * scale
    out_ref[...] = total[:, 3 * D :] * scale


def call(kernel, outs, *args, scratch=(), flops=0):
    vmem = pl.BlockSpec(memory_space=pltpu.VMEM)
    return pl.pallas_call(
        kernel,
        out_shape=[jax.ShapeDtypeStruct(s, t) for s, t in outs],
        in_specs=[pl.BlockSpec(memory_space=pltpu.SMEM)] + [vmem] * (len(args) - 1),
        out_specs=[vmem] * len(outs),
        scratch_shapes=list(scratch),
        compiler_params=pltpu.CompilerParams(vmem_limit_bytes=VMEM_LIMIT),
        cost_estimate=pl.CostEstimate(flops=flops, bytes_accessed=4 << 20, transcendentals=0),
    )(*args)


def body(sizes, activations, qkv_weight, out_weight, cotangent):
    pipes, chips, cols = sizes

    def routed(block, step, plane=None):
        pairs = []
        for p in range(pipes):
            for z in range(chips):
                for k in range(2):
                    for c in range(cols):
                        if plane is not None and p != plane:
                            continue
                        p2, r2, c2 = step(p, 2 * z + k, c)
                        if 0 <= p2 < pipes and 0 <= r2 < 2 * chips and 0 <= c2 < cols:
                            source = (p * 2 * chips + 2 * z + k) * cols + c
                            pairs.append((source, (p2 * 2 * chips + r2) * cols + c2))
        return lax.ppermute(block, AXES, pairs)

    def col_rims(left_half, right_half, down=0, plane=None):
        left = routed(right_half, lambda p, r, c: (p - down, r, c + 1), plane)
        right = routed(left_half, lambda p, r, c: (p - down, r, c - 1), plane)
        return left, right

    def mate(p, r, c):
        return p, r ^ 1, c

    def row_rims(pieces, plane=None):
        own = jnp.concatenate(pieces, axis=0)
        beyond = routed(own, lambda p, r, c: (p, r - 1 + 2 * (r & 1), c), plane)
        return own, routed(own, mate, plane), beyond

    pipe, z, core, col = (lax.axis_index(axis) for axis in AXES)
    x = activations.reshape(TOK, D)
    w_qkv, w_out = qkv_weight[0], out_weight[0]
    cot = cotangent.reshape(TOK, D)
    row_total, col_total = 16 * chips, 16 * cols
    where = jnp.stack(
        [8 * (2 * z + core), 16 * col, core, row_total, col_total, pipes - 1 - pipe]
    ).astype(jnp.int32)

    base, low_side, high_side = call(
        first_kernel, [((OWN, D), BF16), ((64, D), BF16), ((64, D), BF16)], where, x
    )
    proj, nlow, cot_low, d_mixed = call(
        centre_kernel, [((TOK, 3 * D), BF16), ((TOK, D), BF16), ((TOK, D), BF16), ((TOK, D), BF16)],
        where, x, w_qkv, w_out, cot, flops=1 << 28,
    )
    left, right = col_rims(low_side, high_side)
    base, proj = lax.optimization_barrier((base, proj))
    own = lax.dynamic_update_slice(base, left, (TOK, 0))
    own, near, far = row_rims([lax.dynamic_update_slice(own, right, (TOK + 64, 0))])
    (side_proj,) = call(
        side_kernel, [((TOK, 3 * D), BF16)], where, left, right, w_qkv, flops=1 << 28
    )
    wide = D + 128
    kv, q_probs, nlow_mate, low_far, mixed, pack, low_side, high_side = call(
        forward_kernel,
        [((REGION, 2 * D), BF16), ((PAIRS, OWN, REGION), BF16), ((TOK, D), BF16),
         ((2 * OWN, D), BF16), ((TOK, D), BF16), ((TOK, wide), BF16), ((64, wide), BF16),
         ((64, wide), BF16)],
        where, near, far, proj, side_proj, w_qkv, cot_low, d_mixed, flops=2 << 30,
    )
    packs = row_rims([pack, *col_rims(low_side, high_side)])
    queries, n_turned = call(
        turned_kernel, [((D, REGION), BF16), ((OWN, OWN), BF16)],
        where, proj, side_proj, low_far, w_qkv, nlow, nlow_mate,
        scratch=[pltpu.VMEM((D, OWN), F32)], flops=1 << 28,
    )
    k_probs, mixed_turned, delta = call(
        key_probs_kernel,
        [((PAIRS, OWN, REGION), BF16), ((D, REGION), BF16), ((8, REGION), F32)],
        where, *packs, proj, queries, flops=1 << 28,
    )
    gradient, gs = cot_low, packs
    state = ()
    for turn in range(pipes):
        plane, last = pipes - 1 - turn, turn == pipes - 1
        if turn > 0:
            low, low_side, high_side = sends
            gradient = routed(low, lambda p, r, c: (p - 1, r, c), plane + 1)
            gs = row_rims([gradient, *col_rims(low_side, high_side, 1, plane + 1)], plane)
        (d_query,) = call(
            functools.partial(query_kernel, turn=turn), [((TOK, D), BF16)],
            where, gradient, w_out, mixed, kv, q_probs, flops=1 << 29,
        )
        outs = [((TOK, 4 * D), BF16), ((OWN, D), BF16)]
        if not last:
            outs += [((TOK, D), F32), ((TOK, D), BF16), ((64, D), BF16), ((64, D), BF16)]
        ins = () if last else (gradient if turn else cot, w_qkv, x)
        outs = call(
            functools.partial(key_kernel, turn=turn, last=last), outs,
            where, *gs, w_out, mixed_turned if turn else delta, proj, queries, k_probs, d_query,
            mixed, *ins, *state[: 2 if last else 3],
            scratch=[pltpu.VMEM((D, REGION), BF16)], flops=1 << 30,
        )
        if last:
            d_proj, g_low = outs
            (d_in,) = call(
                functools.partial(input_kernel, turn=turn), [((TOK, D), F32)],
                where, d_proj, gradient, w_qkv, x, state[2], flops=1 << 28,
            )
        state, sends = outs[:3], outs[3:]
    (part,) = call(
        weight_kernel, [((cols, 8 * chips, 4 * D), BF16)],
        where, n_turned, d_proj, routed(d_proj, mate), g_low,
        scratch=[pltpu.VMEM((D, D), F32)], flops=1 << 29,
    )
    part = lax.all_to_all(part, "col", 0, 0, tiled=True)
    part = jnp.sum(part.astype(F32), axis=0).astype(BF16).reshape(chips, 8, 4 * D)
    part = lax.all_to_all(part, "z", 0, 0, tiled=True)
    qkv_part, out_part = call(
        functools.partial(total_kernel, scale=(row_total * col_total) ** (-0.5)),
        [((8, 3 * D), F32), ((8, D), F32)], where, part,
    )
    return d_in.reshape(1, 8, 16, D), qkv_part[None], out_part[None]


def solution(mesh):
    pipes, rows, cols = (mesh.shape[axis] for axis in ("pipe", "row", "col"))
    fine = Mesh(np.asarray(mesh.devices).reshape(pipes, rows // 2, 2, cols), AXES)
    row = ("z", "core")
    return jax.shard_map(
        functools.partial(body, (pipes, rows // 2, cols)),
        mesh=fine,
        in_specs=(
            P("pipe", row, "col", None),
            P("pipe", None, None),
            P("pipe", None, None),
            P(row, "col", None),
        ),
        out_specs=(
            P("pipe", row, "col", None),
            P("pipe", ("z", "core", "col"), None),
            P("pipe", ("z", "core", "col"), None),
        ),
        check_vma=False,
    )
```

```python
import functools

import jax
import jax.numpy as jnp
import numpy as np
from jax import lax
from jax.experimental import pallas as pl
from jax.experimental.pallas import tpu as pltpu
from jax.sharding import Mesh
from jax.sharding import PartitionSpec as P

F32 = jnp.float32
BF16 = jnp.bfloat16
AXES = ("pipe", "z", "core", "col")
D = 512
PAIRS = 4
TOK = 128
OWN = 256
REGION = 768
BLOCK = 32
VMEM_LIMIT = 40 * 1024 * 1024


def nn(a, b):
    return lax.dot_general(a, b, (((1,), (0,)), ((), ())), preferred_element_type=F32)


def nt(a, b):
    return lax.dot_general(a, b, (((1,), (1,)), ((), ())), preferred_element_type=F32)


def tn(a, b):
    return lax.dot_general(a, b, (((0,), (0,)), ((), ())), preferred_element_type=F32)


def two_heads(block):
    lane = lax.broadcasted_iota(jnp.int32, block.shape, 1)
    zero = jnp.zeros_like(block)
    return jnp.concatenate(
        [jnp.where(lane < 64, block, zero), jnp.where(lane < 64, zero, block)], axis=0
    )


def one_block(stacked):
    half = stacked.shape[0] // 2
    lane = lax.broadcasted_iota(jnp.int32, (half, 128), 1)
    return jnp.where(lane < 64, stacked[:half], stacked[half:])


def place(index, core):
    piece = index >> 8
    inner = index & 255
    side = inner - 128
    is_centre = inner < 128
    row = jnp.where(is_centre, inner >> 4, (side & 63) >> 3)
    col = jnp.where(is_centre, inner & 15, jnp.where(side < 64, (side & 7) - 8, (side & 7) + 16))
    mate = jnp.where(core == 0, 8, -8)
    row = row + jnp.where(piece == 1, mate, jnp.where(piece == 2, -mate, 0))
    return row, col


def window(where_ref, keys_own):
    row0, col0, core, rows, cols = (where_ref[i] for i in range(5))
    own = lax.broadcasted_iota(jnp.int32, (TOK, 1), 0)
    reach_row, reach_col = place(lax.broadcasted_iota(jnp.int32, (1, REGION), 1), core)
    grid_row, grid_col = row0 + reach_row, col0 + reach_col
    inside = (grid_row >= 0) & (grid_row < rows) & (grid_col >= 0) & (grid_col < cols)
    reach_row = jnp.where(inside, reach_row, 1 << 20)
    if keys_own:
        step_row, step_col = (own >> 4) - reach_row, (own & 15) - reach_col
    else:
        step_row, step_col = reach_row - (own >> 4), reach_col - (own & 15)
    return (step_row >= -8) & (step_row <= 7) & (step_col >= -8) & (step_col <= 7)


def put_sides(block, left_ref, right_ref):
    sides = block.reshape(8, 2, 8, block.shape[-1])
    left_ref[...] = sides[:, 0].reshape(64, -1).astype(BF16)
    right_ref[...] = sides[:, 1].reshape(64, -1).astype(BF16)


def first_kernel(where_ref, x_ref, base_ref, left_ref, right_ref):
    base_ref[:TOK] = x_ref[...]
    base_ref[TOK:] = jnp.zeros((TOK, D), BF16)
    put_sides(x_ref[...].astype(F32), left_ref, right_ref)


def normed_low(x_ref):
    x = x_ref[...].astype(F32)
    inverse = lax.rsqrt(jnp.mean(x * x, axis=-1, keepdims=True) + 1e-06)
    return (x * inverse).astype(BF16)


def centre_kernel(where_ref, x_ref, w_ref, cot_ref, proj_ref, nlow_ref, cot_low_ref):
    low = normed_low(x_ref)
    nlow_ref[...] = low
    proj_ref[...] = nn(low, w_ref[...]).astype(BF16)
    cot_low_ref[...] = cot_ref[...].astype(BF16)


def side_kernel(where_ref, left_ref, right_ref, w_ref, wo_ref, cot_ref, proj_ref, dm_ref):
    low = jnp.concatenate([normed_low(left_ref), normed_low(right_ref)], axis=0)
    proj_ref[...] = nn(low, w_ref[...]).astype(BF16)
    dm_ref[...] = nt(cot_ref[...], wo_ref[...]).astype(BF16)


def forward_kernel(
    where_ref, x1, x2, proj_ref, side_ref, w_ref, cot_ref, dm_ref,
    kv_ref, prob_ref, nlow_ref, far_ref, mixed_ref, pack_ref, left_ref, right_ref,
):
    kv_ref[:TOK] = proj_ref[:, D:]
    kv_ref[TOK:OWN] = side_ref[:, D:]
    for piece, x_ref in enumerate((x1, x2)):
        low = normed_low(x_ref)
        far_ref[piece * OWN : (piece + 1) * OWN] = low
        if piece == 0:
            nlow_ref[...] = low[:TOK]
        kv_ref[(piece + 1) * OWN : (piece + 2) * OWN] = nn(low, w_ref[:, D:]).astype(BF16)
    ok = window(where_ref, False)
    ok2 = jnp.concatenate([ok, ok], axis=0)
    lane = lax.broadcasted_iota(jnp.int32, (TOK, 128), 1)
    stats = jnp.zeros((TOK, 128), F32)
    for pair in range(PAIRS):
        at = slice(128 * pair, 128 * pair + 128)
        query = two_heads(proj_ref[:, at] * 0.125)
        scores = nt(query, kv_ref[:, at])
        scores = jnp.where(ok2, scores, -1e30)
        highest = jnp.max(scores, axis=-1, keepdims=True)
        grown = jnp.exp(scores - highest)
        total = jnp.sum(grown, axis=-1, keepdims=True)
        probs = (grown * (1.0 / total)).astype(BF16)
        prob_ref[pair] = probs
        value = kv_ref[:, D + 128 * pair : D + 128 * pair + 128]
        mixed = one_block(nn(probs, value)).astype(BF16)
        mixed_ref[:, at] = mixed
        log_total = highest + jnp.log(total)
        delta = two_sums(dm_ref[:, at], mixed)
        for first, rest in ((0, log_total), (24, delta)):
            for part in range(3):
                piece = rest.astype(BF16).astype(F32)
                rest = rest - piece
                for head in range(2):
                    chosen = lane == first + 8 * part + 2 * pair + head
                    stats = jnp.where(chosen, piece[TOK * head : TOK * head + TOK], stats)
    starts = where_ref[5] == 0
    pack_ref[:, D:] = stats.astype(BF16)

    @pl.when(starts)
    def _():
        pack_ref[:, :D] = cot_ref[...]

    @pl.when(jnp.logical_not(starts))
    def _():
        pack_ref[:, :D] = mixed_ref[...]

    put_sides(pack_ref[...].astype(F32), left_ref, right_ref)


def turned_kernel(where_ref, proj_ref, side_ref, far_ref, w_ref, n0, n1, query_ref, nt_ref, full_ref):
    query_ref[:, :TOK] = proj_ref[:, :D].astype(F32).T.astype(BF16)
    query_ref[:, TOK:OWN] = side_ref[:, :D].astype(F32).T.astype(BF16)
    far = nn(far_ref[...], w_ref[:, :D]).astype(BF16)
    query_ref[:, OWN:] = far.astype(F32).T.astype(BF16)
    full_ref[:, :TOK] = n0[...].astype(F32).T
    full_ref[:, TOK:] = n1[...].astype(F32).T
    nt_ref[...] = own_half(where_ref, full_ref).astype(BF16)


def own_half(where_ref, full_ref):
    rows = [
        full_ref[pl.ds(pl.multiple_of((2 * at + where_ref[2]) * BLOCK, BLOCK), BLOCK)]
        for at in range(full_ref.shape[0] // (2 * BLOCK))
    ]
    return jnp.concatenate(rows, axis=0)


def key_probs_kernel(
    where_ref, p0, p1, p2, proj_ref, query_ref, prob_ref, mixed_ref, delta_ref
):
    head = lax.broadcasted_iota(jnp.int32, (8, 128), 0)
    lane = lax.broadcasted_iota(jnp.int32, (8, 128), 1)
    stats = jnp.concatenate([p[:, D:] for p in (p0, p1, p2)], axis=0)
    sums = []
    for first in (0, 24):
        chosen = ((lane & 7) == head) & (lane >= first) & (lane < first + 24)
        sums.append(nt(jnp.where(chosen, 1.0, 0.0).astype(BF16), stats))
    log_total, delta_ref[...] = sums

    @pl.when(where_ref[5] != 0)
    def _():
        for piece, p in enumerate((p0, p1, p2)):
            mixed_ref[:, piece * OWN : (piece + 1) * OWN] = p[:, :D].astype(F32).T.astype(BF16)

    ok = window(where_ref, True)
    for pair in range(PAIRS):
        key = two_heads(proj_ref[:, D + 128 * pair : D + 128 * pair + 128] * 0.125)
        scores = nn(key, query_ref[128 * pair : 128 * pair + 128])
        for side in range(2):
            at = 2 * pair + side
            part = scores[TOK * side : TOK * side + TOK] - log_total[at : at + 1]
            probs = jnp.exp(jnp.where(ok, part, -1e30))
            prob_ref[pair, TOK * side : TOK * side + TOK] = probs.astype(BF16)


def two_sums(grad, mixed):
    prod = grad.astype(F32) * mixed.astype(F32)
    lane = lax.broadcasted_iota(jnp.int32, prod.shape, 1)
    return jnp.concatenate(
        [
            jnp.sum(jnp.where(lane < 64, prod, 0.0), axis=-1, keepdims=True),
            jnp.sum(jnp.where(lane < 64, 0.0, prod), axis=-1, keepdims=True),
        ],
        axis=0,
    )


def query_kernel(where_ref, g_ref, w_ref, mixed_ref, kv_ref, prob_ref, dq_ref, *, turn):
    @pl.when(where_ref[5] == turn)
    def _():
        d_mixed = nt(g_ref[...], w_ref[...]).astype(BF16)
        for pair in range(PAIRS):
            at = slice(128 * pair, 128 * pair + 128)
            grad = d_mixed[:, at]
            delta = two_sums(grad, mixed_ref[:, at])
            value = kv_ref[:, D + 128 * pair : D + 128 * pair + 128]
            pressure = nt(two_heads(grad), value)
            slopes = (prob_ref[pair].astype(F32) * (pressure - delta)).astype(BF16)
            dq_ref[:, at] = (one_block(nn(slopes, kv_ref[:, at])) * 0.125).astype(BF16)


def turned_block(stacked):
    row = lax.broadcasted_iota(jnp.int32, (128, 128), 0)
    return jnp.where(row < 64, stacked[:, :128], stacked[:, 128:]).T


def key_kernel(
    where_ref, g0, g1, g2, wo_ref, delta_ref, proj_ref, query_ref, prob_ref, dq_ref, mixed_ref,
    *rest, turn, last,
):
    ins, rest = ((), rest) if last else (rest[:3], rest[3:])
    prev = (3 - last) if turn else 0
    prev, rest = rest[:prev], rest[prev:]
    outs, sends, dm_ref = rest[: 3 - last], rest[3 - last : -1], rest[-1]
    dp_ref, gl_ref = outs[:2]
    active = where_ref[5] == turn

    if prev:

        @pl.when(jnp.logical_not(active))
        def _():
            for new, old in zip(outs, prev):
                new[...] = old[...]

    @pl.when(active)
    def _():
        for piece, g in enumerate((g0, g1, g2)):
            d_mixed = nt(wo_ref[...], g[:, :D]).astype(BF16)
            dm_ref[:, piece * OWN : (piece + 1) * OWN] = d_mixed
        dp_ref[:, :D] = dq_ref[...]
        dp_ref[:, 3 * D :] = mixed_ref[...]
        gl_ref[:TOK] = g0[:TOK, :D]
        gl_ref[TOK:] = g1[:TOK, :D]
        for pair in range(PAIRS):
            at = slice(128 * pair, 128 * pair + 128)
            value = two_heads(proj_ref[:, 2 * D + 128 * pair : 2 * D + 128 * pair + 128])
            grad = dm_ref[at]
            if turn:
                prod = grad.astype(F32) * delta_ref[at].astype(F32)
                deltas = [jnp.sum(prod[r : r + 64], axis=0, keepdims=True) for r in (0, 64)]
            else:
                deltas = [delta_ref[2 * pair + side : 2 * pair + side + 1] for side in range(2)]
            pressure = nn(value, grad)
            probs = prob_ref[pair]
            d_value = nt(grad, probs)
            slopes = []
            for side in range(2):
                rows = slice(TOK * side, TOK * side + TOK)
                slopes.append(
                    (probs[rows].astype(F32) * (pressure[rows] - deltas[side])).astype(BF16)
                )
            d_key = nt(query_ref[at], jnp.concatenate(slopes, axis=0))
            low, high = D + 128 * pair, D + 128 * pair + 128
            dp_ref[:, low:high] = (turned_block(d_key) * 0.125).astype(BF16)
            dp_ref[:, D + low : D + high] = turned_block(d_value).astype(BF16)
        if not last:
            out = input_grad(dp_ref, *ins)
            outs[2][...] = out
            low_ref, left_ref, right_ref = sends
            low_ref[...] = out.astype(BF16)
            put_sides(out, left_ref, right_ref)


def input_grad(dp_ref, g_ref, wq_ref, x_ref):
    d_normed = nt(dp_ref[:, : 3 * D], wq_ref[...])
    x = x_ref[...].astype(F32)
    inverse = lax.rsqrt(jnp.mean(x * x, axis=-1, keepdims=True) + 1e-06)
    normed = x * inverse
    inner = jnp.mean(d_normed * normed, axis=-1, keepdims=True)
    return g_ref[...].astype(F32) + inverse * (d_normed - normed * inner)


def input_kernel(where_ref, dp_ref, g_ref, wq_ref, x_ref, prev_ref, in_ref, *, turn):
    @pl.when(where_ref[5] == turn)
    def _():
        in_ref[...] = input_grad(dp_ref, g_ref, wq_ref, x_ref)

    @pl.when(where_ref[5] != turn)
    def _():
        in_ref[...] = prev_ref[...]


def weight_kernel(where_ref, nt_ref, d0, d1, g_ref, *refs):
    outs, (left_ref, full_ref) = refs[:-2], refs[-2:]
    d_proj = jnp.concatenate([d0[:, : 3 * D], d1[:, : 3 * D]], axis=0)
    mixed = jnp.concatenate([d0[:, 3 * D :], d1[:, 3 * D :]], axis=0)
    full_ref[...] = tn(mixed, g_ref[...])
    left_ref[...] = nn(nt_ref[...], d_proj)
    core, cols = where_ref[2], len(outs)
    for distance, out_ref in enumerate(outs):
        col = lax.rem(where_ref[6] + distance, cols)
        for at, ref, step, first in (
            (slice(0, 3 * D), left_ref, BLOCK, 0), (slice(3 * D, 4 * D), full_ref, 2 * BLOCK, core)
        ):
            rows = [
                ref[pl.ds(pl.multiple_of(step * chip + first * BLOCK + 8 * col, 8), 8)]
                for chip in range(out_ref.shape[0] // 8)
            ]
            out_ref[:, at] = jnp.concatenate(rows, axis=0).astype(BF16)


def col_total_kernel(where_ref, *refs):
    total = refs[0][...].astype(F32)
    for ref in refs[1:-1]:
        total = total + ref[...].astype(F32)
    refs[-1][...] = total.astype(BF16)


def total_kernel(where_ref, part_ref, qkv_ref, out_ref, *, scale):
    total = part_ref[0].astype(F32)
    for source in range(1, part_ref.shape[0]):
        total = total + part_ref[source].astype(F32)
    qkv_ref[...] = total[:, : 3 * D] * scale
    out_ref[...] = total[:, 3 * D :] * scale


def call(kernel, outs, *args, scratch=(), flops=0):
    vmem = pl.BlockSpec(memory_space=pltpu.VMEM)
    return pl.pallas_call(
        kernel,
        out_shape=[jax.ShapeDtypeStruct(s, t) for s, t in outs],
        in_specs=[pl.BlockSpec(memory_space=pltpu.SMEM)] + [vmem] * (len(args) - 1),
        out_specs=[vmem] * len(outs),
        scratch_shapes=list(scratch),
        compiler_params=pltpu.CompilerParams(vmem_limit_bytes=VMEM_LIMIT),
        cost_estimate=pl.CostEstimate(flops=flops, bytes_accessed=4 << 20, transcendentals=0),
    )(*args)


def body(sizes, activations, qkv_weight, out_weight, cotangent):
    pipes, chips, cols = sizes

    def routed(block, step, plane=None):
        pairs = []
        for p in range(pipes) if plane is None else (plane,):
            for r in range(2 * chips):
                for c in range(cols):
                    p2, r2, c2 = step(p, r, c)
                    target = (p2 * 2 * chips + r2 % (2 * chips)) * cols + c2 % cols
                    pairs.append(((p * 2 * chips + r) * cols + c, target))
        return lax.ppermute(block, AXES, pairs)

    def col_rims(left_half, right_half, down=0, plane=None):
        left = routed(right_half, lambda p, r, c: (p - down, r, c + 1), plane)
        right = routed(left_half, lambda p, r, c: (p - down, r, c - 1), plane)
        return left, right

    def mate(p, r, c):
        return p, r ^ 1, c

    def row_rims(pieces, plane=None):
        own = jnp.concatenate(pieces, axis=0)
        beyond = routed(own, lambda p, r, c: (p, r - 1 + 2 * (r & 1), c), plane)
        return own, routed(own, mate, plane), beyond

    pipe, z, core, col = (lax.axis_index(axis) for axis in AXES)
    x = activations.reshape(TOK, D)
    w_qkv, w_out = qkv_weight[0], out_weight[0]
    cot = cotangent.reshape(TOK, D)
    row_total, col_total = 16 * chips, 16 * cols
    where = jnp.stack(
        [8 * (2 * z + core), 16 * col, core, row_total, col_total, pipes - 1 - pipe, col]
    ).astype(jnp.int32)

    base, low_side, high_side = call(
        first_kernel, [((OWN, D), BF16), ((64, D), BF16), ((64, D), BF16)], where, x
    )
    proj, nlow, cot_low = call(
        centre_kernel, [((TOK, 3 * D), BF16), ((TOK, D), BF16), ((TOK, D), BF16)],
        where, x, w_qkv, cot, flops=1 << 28,
    )
    left, right = col_rims(low_side, high_side)
    base, proj = lax.optimization_barrier((base, proj))
    own = lax.dynamic_update_slice(base, left, (TOK, 0))
    own, near, far = row_rims([lax.dynamic_update_slice(own, right, (TOK + 64, 0))])
    side_proj, d_mixed = call(
        side_kernel, [((TOK, 3 * D), BF16), ((TOK, D), BF16)],
        where, left, right, w_qkv, w_out, cot_low, flops=1 << 28,
    )
    wide = D + 128
    kv, q_probs, nlow_mate, low_far, mixed, pack, low_side, high_side = call(
        forward_kernel,
        [((REGION, 2 * D), BF16), ((PAIRS, OWN, REGION), BF16), ((TOK, D), BF16),
         ((2 * OWN, D), BF16), ((TOK, D), BF16), ((TOK, wide), BF16), ((64, wide), BF16),
         ((64, wide), BF16)],
        where, near, far, proj, side_proj, w_qkv, cot_low, d_mixed, flops=2 << 30,
    )
    sides = col_rims(low_side, high_side)
    queries, n_turned = call(
        turned_kernel, [((D, REGION), BF16), ((OWN, OWN), BF16)],
        where, proj, side_proj, low_far, w_qkv, nlow, nlow_mate,
        scratch=[pltpu.VMEM((D, OWN), F32)], flops=1 << 28,
    )

    def query_side(turn, gradient):
        return call(
            functools.partial(query_kernel, turn=turn), [((TOK, D), BF16)],
            where, gradient, w_out, mixed, kv, q_probs, flops=1 << 29,
        )[0]

    d_query = query_side(0, cot_low)
    pack, queries, d_query = lax.optimization_barrier((pack, queries, d_query))
    packs = row_rims([pack, *sides])
    k_probs, mixed_turned, delta = call(
        key_probs_kernel,
        [((PAIRS, OWN, REGION), BF16), ((D, REGION), BF16), ((8, REGION), F32)],
        where, *packs, proj, queries, flops=1 << 28,
    )
    gradient, gs = cot_low, packs
    state = ()
    for turn in range(pipes):
        plane, last = pipes - 1 - turn, turn == pipes - 1
        if turn > 0:
            low, low_side, high_side = sends
            gradient = routed(low, lambda p, r, c: (p - 1, r, c), plane + 1)
            gs = row_rims([gradient, *col_rims(low_side, high_side, 1, plane + 1)], plane)
            d_query = query_side(turn, gradient)
        outs = [((TOK, 4 * D), BF16), ((OWN, D), BF16)]
        if not last:
            outs += [((TOK, D), F32), ((TOK, D), BF16), ((64, D), BF16), ((64, D), BF16)]
        ins = () if last else (gradient if turn else cot, w_qkv, x)
        outs = call(
            functools.partial(key_kernel, turn=turn, last=last), outs,
            where, *gs, w_out, mixed_turned if turn else delta, proj, queries, k_probs, d_query,
            mixed, *ins, *state[: 2 if last else 3],
            scratch=[pltpu.VMEM((D, REGION), BF16)], flops=1 << 30,
        )
        if last:
            d_proj, g_low = outs
            (d_in,) = call(
                functools.partial(input_kernel, turn=turn), [((TOK, D), F32)],
                where, d_proj, gradient, w_qkv, x, state[2], flops=1 << 28,
            )
        state, sends = outs[:3], outs[3:]
    parts = call(
        weight_kernel, [((8 * chips, 4 * D), BF16)] * cols,
        where, n_turned, d_proj, routed(d_proj, mate), g_low,
        scratch=[pltpu.VMEM((OWN, 3 * D), F32), pltpu.VMEM((D, D), F32)], flops=1 << 29,
    )
    parts = list(parts)
    for distance in sorted(range(1, cols), key=lambda d: -min(d, cols - d)):
        parts[distance] = routed(parts[distance], lambda p, r, c: (p, r, c + distance))
    (part,) = call(col_total_kernel, [((8 * chips, 4 * D), BF16)], where, *parts)
    part = part.reshape(chips, 8, 4 * D)
    part = lax.all_to_all(part, "z", 0, 0, tiled=True)
    qkv_part, out_part = call(
        functools.partial(total_kernel, scale=(row_total * col_total) ** (-0.5)),
        [((8, 3 * D), F32), ((8, D), F32)], where, part,
    )
    return d_in.reshape(1, 8, 16, D), qkv_part[None], out_part[None]


def solution(mesh):
    pipes, rows, cols = (mesh.shape[axis] for axis in ("pipe", "row", "col"))
    fine = Mesh(np.asarray(mesh.devices).reshape(pipes, rows // 2, 2, cols), AXES)
    row = ("z", "core")
    return jax.shard_map(
        functools.partial(body, (pipes, rows // 2, cols)),
        mesh=fine,
        in_specs=(
            P("pipe", row, "col", None),
            P("pipe", None, None),
            P("pipe", None, None),
            P(row, "col", None),
        ),
        out_specs=(
            P("pipe", row, "col", None),
            P("pipe", ("z", "core", "col"), None),
            P("pipe", ("z", "core", "col"), None),
        ),
        check_vma=False,
    )
```

```python
import functools

import jax
import jax.numpy as jnp
import numpy as np
from jax import lax
from jax.experimental import pallas as pl
from jax.experimental.pallas import tpu as pltpu
from jax.sharding import Mesh
from jax.sharding import PartitionSpec as P

F32 = jnp.float32
BF16 = jnp.bfloat16
AXES = ("pipe", "z", "core", "col")
D = 512
PAIRS = 4
TOK = 128
OWN = 256
REGION = 768
BLOCK = 32
VMEM_LIMIT = 40 * 1024 * 1024


def nn(a, b):
    return lax.dot_general(a, b, (((1,), (0,)), ((), ())), preferred_element_type=F32)


def nt(a, b):
    return lax.dot_general(a, b, (((1,), (1,)), ((), ())), preferred_element_type=F32)


def tn(a, b):
    return lax.dot_general(a, b, (((0,), (0,)), ((), ())), preferred_element_type=F32)


def two_heads(block):
    lane = lax.broadcasted_iota(jnp.int32, block.shape, 1)
    zero = jnp.zeros_like(block)
    return jnp.concatenate(
        [jnp.where(lane < 64, block, zero), jnp.where(lane < 64, zero, block)], axis=0
    )


def one_block(stacked):
    half = stacked.shape[0] // 2
    lane = lax.broadcasted_iota(jnp.int32, (half, 128), 1)
    return jnp.where(lane < 64, stacked[:half], stacked[half:])


def place(index, core):
    piece = index >> 8
    inner = index & 255
    side = inner - 128
    is_centre = inner < 128
    row = jnp.where(is_centre, inner >> 4, (side & 63) >> 3)
    col = jnp.where(is_centre, inner & 15, jnp.where(side < 64, (side & 7) - 8, (side & 7) + 16))
    mate = jnp.where(core == 0, 8, -8)
    row = row + jnp.where(piece == 1, mate, jnp.where(piece == 2, -mate, 0))
    return row, col


def window(where_ref, keys_own):
    row0, col0, core, rows, cols = (where_ref[i] for i in range(5))
    own = lax.broadcasted_iota(jnp.int32, (TOK, 1), 0)
    reach_row, reach_col = place(lax.broadcasted_iota(jnp.int32, (1, REGION), 1), core)
    grid_row, grid_col = row0 + reach_row, col0 + reach_col
    inside = (grid_row >= 0) & (grid_row < rows) & (grid_col >= 0) & (grid_col < cols)
    reach_row = jnp.where(inside, reach_row, 1 << 20)
    if keys_own:
        step_row, step_col = (own >> 4) - reach_row, (own & 15) - reach_col
    else:
        step_row, step_col = reach_row - (own >> 4), reach_col - (own & 15)
    return (step_row >= -8) & (step_row <= 7) & (step_col >= -8) & (step_col <= 7)


def put_sides(block, left_ref, right_ref):
    sides = block.reshape(8, 2, 8, block.shape[-1])
    left_ref[...] = sides[:, 0].reshape(64, -1).astype(BF16)
    right_ref[...] = sides[:, 1].reshape(64, -1).astype(BF16)


def first_kernel(where_ref, x_ref, base_ref, left_ref, right_ref):
    base_ref[:TOK] = x_ref[...]
    base_ref[TOK:] = jnp.zeros((TOK, D), BF16)
    put_sides(x_ref[...].astype(F32), left_ref, right_ref)


def normed_low(x_ref):
    x = x_ref[...].astype(F32)
    inverse = lax.rsqrt(jnp.mean(x * x, axis=-1, keepdims=True) + 1e-06)
    return (x * inverse).astype(BF16)


def centre_kernel(where_ref, x_ref, w_ref, cot_ref, proj_ref, nlow_ref, cot_low_ref):
    low = normed_low(x_ref)
    nlow_ref[...] = low
    proj_ref[...] = nn(low, w_ref[...]).astype(BF16)
    cot_low_ref[...] = cot_ref[...].astype(BF16)


def side_kernel(where_ref, left_ref, right_ref, w_ref, wo_ref, cot_ref, proj_ref, dm_ref):
    low = jnp.concatenate([normed_low(left_ref), normed_low(right_ref)], axis=0)
    proj_ref[...] = nn(low, w_ref[...]).astype(BF16)
    dm_ref[...] = nt(cot_ref[...], wo_ref[...]).astype(BF16)


def forward_kernel(
    where_ref, x1, x2, proj_ref, side_ref, w_ref, cot_ref, dm_ref,
    kv_ref, prob_ref, nlow_ref, far_ref, mixed_ref, pack_ref, left_ref, right_ref,
):
    kv_ref[:TOK] = proj_ref[:, D:]
    kv_ref[TOK:OWN] = side_ref[:, D:]
    for piece, x_ref in enumerate((x1, x2)):
        low = normed_low(x_ref)
        far_ref[piece * OWN : (piece + 1) * OWN] = low
        if piece == 0:
            nlow_ref[...] = low[:TOK]
        kv_ref[(piece + 1) * OWN : (piece + 2) * OWN] = nn(low, w_ref[:, D:]).astype(BF16)
    ok = window(where_ref, False)
    ok2 = jnp.concatenate([ok, ok], axis=0)
    lane = lax.broadcasted_iota(jnp.int32, (TOK, 128), 1)
    stats = jnp.zeros((TOK, 128), F32)
    for pair in range(PAIRS):
        at = slice(128 * pair, 128 * pair + 128)
        query = two_heads(proj_ref[:, at] * 0.125)
        scores = nt(query, kv_ref[:, at])
        scores = jnp.where(ok2, scores, -1e30)
        highest = jnp.max(scores, axis=-1, keepdims=True)
        grown = jnp.exp(scores - highest)
        total = jnp.sum(grown, axis=-1, keepdims=True)
        probs = (grown * (1.0 / total)).astype(BF16)
        prob_ref[pair] = probs
        value = kv_ref[:, D + 128 * pair : D + 128 * pair + 128]
        mixed = one_block(nn(probs, value)).astype(BF16)
        mixed_ref[:, at] = mixed
        log_total = highest + jnp.log(total)
        delta = two_sums(dm_ref[:, at], mixed)
        for first, rest in ((0, log_total), (24, delta)):
            for part in range(3):
                piece = rest.astype(BF16).astype(F32)
                rest = rest - piece
                for head in range(2):
                    chosen = lane == first + 8 * part + 2 * pair + head
                    stats = jnp.where(chosen, piece[TOK * head : TOK * head + TOK], stats)
    starts = where_ref[5] == 0
    pack_ref[:, D:] = stats.astype(BF16)

    @pl.when(starts)
    def _():
        pack_ref[:, :D] = cot_ref[...]

    @pl.when(jnp.logical_not(starts))
    def _():
        pack_ref[:, :D] = mixed_ref[...]

    put_sides(pack_ref[...].astype(F32), left_ref, right_ref)


def turned_kernel(where_ref, proj_ref, side_ref, far_ref, w_ref, n0, n1, query_ref, nt_ref, full_ref):
    query_ref[:, :TOK] = proj_ref[:, :D].astype(F32).T.astype(BF16)
    query_ref[:, TOK:OWN] = side_ref[:, :D].astype(F32).T.astype(BF16)
    far = nn(far_ref[...], w_ref[:, :D]).astype(BF16)
    query_ref[:, OWN:] = far.astype(F32).T.astype(BF16)
    full_ref[:, :TOK] = n0[...].astype(F32).T
    full_ref[:, TOK:] = n1[...].astype(F32).T
    nt_ref[...] = own_half(where_ref, full_ref).astype(BF16)


def own_half(where_ref, full_ref):
    rows = [
        full_ref[pl.ds(pl.multiple_of((2 * at + where_ref[2]) * BLOCK, BLOCK), BLOCK)]
        for at in range(full_ref.shape[0] // (2 * BLOCK))
    ]
    return jnp.concatenate(rows, axis=0)


def key_probs_kernel(
    where_ref, p0, p1, p2, proj_ref, query_ref, prob_ref, mixed_ref, delta_ref
):
    head = lax.broadcasted_iota(jnp.int32, (8, 128), 0)
    lane = lax.broadcasted_iota(jnp.int32, (8, 128), 1)
    stats = jnp.concatenate([p[:, D:] for p in (p0, p1, p2)], axis=0)
    sums = []
    for first in (0, 24):
        chosen = ((lane & 7) == head) & (lane >= first) & (lane < first + 24)
        sums.append(nt(jnp.where(chosen, 1.0, 0.0).astype(BF16), stats))
    log_total, delta_ref[...] = sums

    @pl.when(where_ref[5] != 0)
    def _():
        for piece, p in enumerate((p0, p1, p2)):
            mixed_ref[:, piece * OWN : (piece + 1) * OWN] = p[:, :D].astype(F32).T.astype(BF16)

    ok = window(where_ref, True)
    for pair in range(PAIRS):
        key = two_heads(proj_ref[:, D + 128 * pair : D + 128 * pair + 128] * 0.125)
        scores = nn(key, query_ref[128 * pair : 128 * pair + 128])
        for side in range(2):
            at = 2 * pair + side
            part = scores[TOK * side : TOK * side + TOK] - log_total[at : at + 1]
            probs = jnp.exp(jnp.where(ok, part, -1e30))
            prob_ref[pair, TOK * side : TOK * side + TOK] = probs.astype(BF16)


def two_sums(grad, mixed):
    prod = grad.astype(F32) * mixed.astype(F32)
    lane = lax.broadcasted_iota(jnp.int32, prod.shape, 1)
    return jnp.concatenate(
        [
            jnp.sum(jnp.where(lane < 64, prod, 0.0), axis=-1, keepdims=True),
            jnp.sum(jnp.where(lane < 64, 0.0, prod), axis=-1, keepdims=True),
        ],
        axis=0,
    )


def query_kernel(where_ref, g_ref, w_ref, mixed_ref, kv_ref, prob_ref, dq_ref, *, turn):
    @pl.when(where_ref[5] == turn)
    def _():
        d_mixed = nt(g_ref[...], w_ref[...]).astype(BF16)
        for pair in range(PAIRS):
            at = slice(128 * pair, 128 * pair + 128)
            grad = d_mixed[:, at]
            delta = two_sums(grad, mixed_ref[:, at])
            value = kv_ref[:, D + 128 * pair : D + 128 * pair + 128]
            pressure = nt(two_heads(grad), value)
            slopes = (prob_ref[pair].astype(F32) * (pressure - delta)).astype(BF16)
            dq_ref[:, at] = (one_block(nn(slopes, kv_ref[:, at])) * 0.125).astype(BF16)


def turned_block(stacked):
    row = lax.broadcasted_iota(jnp.int32, (128, 128), 0)
    return jnp.where(row < 64, stacked[:, :128], stacked[:, 128:]).T


def key_kernel(
    where_ref, g0, g1, g2, wo_ref, delta_ref, proj_ref, query_ref, prob_ref, dq_ref, mixed_ref,
    *rest, turn, last,
):
    ins, rest = ((), rest) if last else (rest[:3], rest[3:])
    prev = (3 - last) if turn else 0
    prev, rest = rest[:prev], rest[prev:]
    outs, sends, dm_ref = rest[: 3 - last], rest[3 - last : -1], rest[-1]
    dp_ref, gl_ref = outs[:2]
    active = where_ref[5] == turn

    if prev:

        @pl.when(jnp.logical_not(active))
        def _():
            for new, old in zip(outs, prev):
                new[...] = old[...]

    @pl.when(active)
    def _():
        for piece, g in enumerate((g0, g1, g2)):
            d_mixed = nt(wo_ref[...], g[:, :D]).astype(BF16)
            dm_ref[:, piece * OWN : (piece + 1) * OWN] = d_mixed
        dp_ref[:, :D] = dq_ref[...]
        dp_ref[:, 3 * D :] = mixed_ref[...]
        gl_ref[:TOK] = g0[:TOK, :D]
        gl_ref[TOK:] = g1[:TOK, :D]
        for pair in range(PAIRS):
            at = slice(128 * pair, 128 * pair + 128)
            value = two_heads(proj_ref[:, 2 * D + 128 * pair : 2 * D + 128 * pair + 128])
            grad = dm_ref[at]
            if turn:
                prod = grad.astype(F32) * delta_ref[at].astype(F32)
                deltas = [jnp.sum(prod[r : r + 64], axis=0, keepdims=True) for r in (0, 64)]
            else:
                deltas = [delta_ref[2 * pair + side : 2 * pair + side + 1] for side in range(2)]
            pressure = nn(value, grad)
            probs = prob_ref[pair]
            d_value = nt(grad, probs)
            slopes = []
            for side in range(2):
                rows = slice(TOK * side, TOK * side + TOK)
                slopes.append(
                    (probs[rows].astype(F32) * (pressure[rows] - deltas[side])).astype(BF16)
                )
            d_key = nt(query_ref[at], jnp.concatenate(slopes, axis=0))
            low, high = D + 128 * pair, D + 128 * pair + 128
            dp_ref[:, low:high] = (turned_block(d_key) * 0.125).astype(BF16)
            dp_ref[:, D + low : D + high] = turned_block(d_value).astype(BF16)
        if not last:
            out = input_grad(dp_ref, *ins)
            outs[2][...] = out
            low_ref, left_ref, right_ref = sends
            low_ref[...] = out.astype(BF16)
            put_sides(out, left_ref, right_ref)


def input_grad(dp_ref, g_ref, wq_ref, x_ref):
    d_normed = nt(dp_ref[:, : 3 * D], wq_ref[...])
    x = x_ref[...].astype(F32)
    inverse = lax.rsqrt(jnp.mean(x * x, axis=-1, keepdims=True) + 1e-06)
    normed = x * inverse
    inner = jnp.mean(d_normed * normed, axis=-1, keepdims=True)
    return g_ref[...].astype(F32) + inverse * (d_normed - normed * inner)


def input_kernel(where_ref, dp_ref, g_ref, wq_ref, x_ref, prev_ref, in_ref, *, turn):
    @pl.when(where_ref[5] == turn)
    def _():
        in_ref[...] = input_grad(dp_ref, g_ref, wq_ref, x_ref)

    @pl.when(where_ref[5] != turn)
    def _():
        in_ref[...] = prev_ref[...]


def weight_kernel(where_ref, nt_ref, d0, d1, g_ref, *refs):
    outs, (left_ref, full_ref) = refs[:-2], refs[-2:]
    d_proj = jnp.concatenate([d0[:, : 3 * D], d1[:, : 3 * D]], axis=0)
    mixed = jnp.concatenate([d0[:, 3 * D :], d1[:, 3 * D :]], axis=0)
    full_ref[...] = tn(mixed, g_ref[...])
    left_ref[...] = nn(nt_ref[...], d_proj)
    core, cols = where_ref[2], len(outs)
    for distance, out_ref in enumerate(outs):
        col = lax.rem(where_ref[6] + distance, cols)
        for at, ref, step, first in (
            (slice(0, 3 * D), left_ref, BLOCK, 0), (slice(3 * D, 4 * D), full_ref, 2 * BLOCK, core)
        ):
            rows = [
                ref[pl.ds(pl.multiple_of(step * chip + first * BLOCK + 8 * col, 8), 8)]
                for chip in range(out_ref.shape[0] // 8)
            ]
            out_ref[:, at] = jnp.concatenate(rows, axis=0).astype(BF16)


def col_total_kernel(where_ref, *refs):
    total = refs[0][...].astype(F32)
    for ref in refs[1:-1]:
        total = total + ref[...].astype(F32)
    refs[-1][...] = total.astype(BF16)


def total_kernel(where_ref, part_ref, qkv_ref, out_ref, *, scale):
    total = part_ref[0].astype(F32)
    for source in range(1, part_ref.shape[0]):
        total = total + part_ref[source].astype(F32)
    qkv_ref[...] = total[:, : 3 * D] * scale
    out_ref[...] = total[:, 3 * D :] * scale


def call(kernel, outs, *args, scratch=(), flops=0):
    vmem = pl.BlockSpec(memory_space=pltpu.VMEM)
    return pl.pallas_call(
        kernel,
        out_shape=[jax.ShapeDtypeStruct(s, t) for s, t in outs],
        in_specs=[pl.BlockSpec(memory_space=pltpu.SMEM)] + [vmem] * (len(args) - 1),
        out_specs=[vmem] * len(outs),
        scratch_shapes=list(scratch),
        compiler_params=pltpu.CompilerParams(vmem_limit_bytes=VMEM_LIMIT),
        cost_estimate=pl.CostEstimate(flops=flops, bytes_accessed=4 << 20, transcendentals=0),
    )(*args)


def body(sizes, activations, qkv_weight, out_weight, cotangent):
    pipes, chips, cols = sizes

    def routed(block, step):
        pairs = []
        for p in range(pipes):
            for r in range(2 * chips):
                for c in range(cols):
                    p2, r2, c2 = step(p, r, c)
                    target = ((p2 % pipes) * 2 * chips + r2 % (2 * chips)) * cols + c2 % cols
                    pairs.append(((p * 2 * chips + r) * cols + c, target))
        return lax.ppermute(block, AXES, pairs)

    def col_rims(left_half, right_half, down=0):
        left = routed(right_half, lambda p, r, c: (p - down, r, c + 1))
        right = routed(left_half, lambda p, r, c: (p - down, r, c - 1))
        return left, right

    def mate(p, r, c):
        return p, r ^ 1, c

    def row_rims(pieces):
        own = jnp.concatenate(pieces, axis=0)
        beyond = routed(own, lambda p, r, c: (p, r - 1 + 2 * (r & 1), c))
        return own, routed(own, mate), beyond

    pipe, z, core, col = (lax.axis_index(axis) for axis in AXES)
    x = activations.reshape(TOK, D)
    w_qkv, w_out = qkv_weight[0], out_weight[0]
    cot = cotangent.reshape(TOK, D)
    row_total, col_total = 16 * chips, 16 * cols
    where = jnp.stack(
        [8 * (2 * z + core), 16 * col, core, row_total, col_total, pipes - 1 - pipe, col]
    ).astype(jnp.int32)

    base, low_side, high_side = call(
        first_kernel, [((OWN, D), BF16), ((64, D), BF16), ((64, D), BF16)], where, x
    )
    proj, nlow, cot_low = call(
        centre_kernel, [((TOK, 3 * D), BF16), ((TOK, D), BF16), ((TOK, D), BF16)],
        where, x, w_qkv, cot, flops=1 << 28,
    )
    left, right = col_rims(low_side, high_side)
    base, proj = lax.optimization_barrier((base, proj))
    own = lax.dynamic_update_slice(base, left, (TOK, 0))
    own, near, far = row_rims([lax.dynamic_update_slice(own, right, (TOK + 64, 0))])
    side_proj, d_mixed = call(
        side_kernel, [((TOK, 3 * D), BF16), ((TOK, D), BF16)],
        where, left, right, w_qkv, w_out, cot_low, flops=1 << 28,
    )
    wide = D + 128
    kv, q_probs, nlow_mate, low_far, mixed, pack, low_side, high_side = call(
        forward_kernel,
        [((REGION, 2 * D), BF16), ((PAIRS, OWN, REGION), BF16), ((TOK, D), BF16),
         ((2 * OWN, D), BF16), ((TOK, D), BF16), ((TOK, wide), BF16), ((64, wide), BF16),
         ((64, wide), BF16)],
        where, near, far, proj, side_proj, w_qkv, cot_low, d_mixed, flops=2 << 30,
    )
    sides = col_rims(low_side, high_side)
    queries, n_turned = call(
        turned_kernel, [((D, REGION), BF16), ((OWN, OWN), BF16)],
        where, proj, side_proj, low_far, w_qkv, nlow, nlow_mate,
        scratch=[pltpu.VMEM((D, OWN), F32)], flops=1 << 28,
    )

    def query_side(turn, gradient):
        return call(
            functools.partial(query_kernel, turn=turn), [((TOK, D), BF16)],
            where, gradient, w_out, mixed, kv, q_probs, flops=1 << 29,
        )[0]

    d_query = query_side(0, cot_low)
    pack, queries, d_query = lax.optimization_barrier((pack, queries, d_query))
    packs = row_rims([pack, *sides])
    k_probs, mixed_turned, delta = call(
        key_probs_kernel,
        [((PAIRS, OWN, REGION), BF16), ((D, REGION), BF16), ((8, REGION), F32)],
        where, *packs, proj, queries, flops=1 << 28,
    )
    gradient, gs = cot_low, packs
    state = ()
    for turn in range(pipes):
        last = turn == pipes - 1
        if turn > 0:
            low, low_side, high_side = sends
            gradient = routed(low, lambda p, r, c: (p - 1, r, c))
            gs = row_rims([gradient, *col_rims(low_side, high_side, 1)])
            d_query = query_side(turn, gradient)
        outs = [((TOK, 4 * D), BF16), ((OWN, D), BF16)]
        if not last:
            outs += [((TOK, D), F32), ((TOK, D), BF16), ((64, D), BF16), ((64, D), BF16)]
        ins = () if last else (gradient if turn else cot, w_qkv, x)
        outs = call(
            functools.partial(key_kernel, turn=turn, last=last), outs,
            where, *gs, w_out, mixed_turned if turn else delta, proj, queries, k_probs, d_query,
            mixed, *ins, *state[: 2 if last else 3],
            scratch=[pltpu.VMEM((D, REGION), BF16)], flops=1 << 30,
        )
        if last:
            d_proj, g_low = outs
            (d_in,) = call(
                functools.partial(input_kernel, turn=turn), [((TOK, D), F32)],
                where, d_proj, gradient, w_qkv, x, state[2], flops=1 << 28,
            )
        state, sends = outs[:3], outs[3:]
    parts = call(
        weight_kernel, [((8 * chips, 4 * D), BF16)] * cols,
        where, n_turned, d_proj, routed(d_proj, mate), g_low,
        scratch=[pltpu.VMEM((OWN, 3 * D), F32), pltpu.VMEM((D, D), F32)], flops=1 << 29,
    )
    parts = list(parts)
    for distance in sorted(range(1, cols), key=lambda d: -min(d, cols - d)):
        parts[distance] = routed(parts[distance], lambda p, r, c: (p, r, c + distance))
    parts[-1], d_in = lax.optimization_barrier((parts[-1], d_in))
    (part,) = call(col_total_kernel, [((8 * chips, 4 * D), BF16)], where, *parts)
    part = part.reshape(chips, 8, 4 * D)
    part = lax.all_to_all(part, "z", 0, 0, tiled=True)
    qkv_part, out_part = call(
        functools.partial(total_kernel, scale=(row_total * col_total) ** (-0.5)),
        [((8, 3 * D), F32), ((8, D), F32)], where, part,
    )
    return d_in.reshape(1, 8, 16, D), qkv_part[None], out_part[None]


def solution(mesh):
    pipes, rows, cols = (mesh.shape[axis] for axis in ("pipe", "row", "col"))
    fine = Mesh(np.asarray(mesh.devices).reshape(pipes, rows // 2, 2, cols), AXES)
    row = ("z", "core")
    return jax.shard_map(
        functools.partial(body, (pipes, rows // 2, cols)),
        mesh=fine,
        in_specs=(
            P("pipe", row, "col", None),
            P("pipe", None, None),
            P("pipe", None, None),
            P(row, "col", None),
        ),
        out_specs=(
            P("pipe", row, "col", None),
            P("pipe", ("z", "core", "col"), None),
            P("pipe", ("z", "core", "col"), None),
        ),
        check_vma=False,
    )
```

```python
import functools

import jax
import jax.numpy as jnp
import numpy as np
from jax import lax
from jax.experimental import pallas as pl
from jax.experimental.pallas import tpu as pltpu
from jax.sharding import Mesh
from jax.sharding import PartitionSpec as P

F32 = jnp.float32
BF16 = jnp.bfloat16
AXES = ("pipe", "z", "core", "col")
D = 512
PAIRS = 4
TOK = 128
OWN = 256
REGION = 768
BLOCK = 32
VMEM_LIMIT = 40 * 1024 * 1024


def nn(a, b):
    return lax.dot_general(a, b, (((1,), (0,)), ((), ())), preferred_element_type=F32)


def nt(a, b):
    return lax.dot_general(a, b, (((1,), (1,)), ((), ())), preferred_element_type=F32)


def tn(a, b):
    return lax.dot_general(a, b, (((0,), (0,)), ((), ())), preferred_element_type=F32)


def two_heads(block):
    lane = lax.broadcasted_iota(jnp.int32, block.shape, 1)
    zero = jnp.zeros_like(block)
    return jnp.concatenate(
        [jnp.where(lane < 64, block, zero), jnp.where(lane < 64, zero, block)], axis=0
    )


def one_block(stacked):
    half = stacked.shape[0] // 2
    lane = lax.broadcasted_iota(jnp.int32, (half, 128), 1)
    return jnp.where(lane < 64, stacked[:half], stacked[half:])


def place(index, core):
    piece = index >> 8
    inner = index & 255
    side = inner - 128
    is_centre = inner < 128
    row = jnp.where(is_centre, inner >> 4, (side & 63) >> 3)
    col = jnp.where(is_centre, inner & 15, jnp.where(side < 64, (side & 7) - 8, (side & 7) + 16))
    mate = jnp.where(core == 0, 8, -8)
    row = row + jnp.where(piece == 1, mate, jnp.where(piece == 2, -mate, 0))
    return row, col


def window(where_ref, keys_own):
    row0, col0, core, rows, cols = (where_ref[i] for i in range(5))
    own = lax.broadcasted_iota(jnp.int32, (TOK, 1), 0)
    reach_row, reach_col = place(lax.broadcasted_iota(jnp.int32, (1, REGION), 1), core)
    grid_row, grid_col = row0 + reach_row, col0 + reach_col
    inside = (grid_row >= 0) & (grid_row < rows) & (grid_col >= 0) & (grid_col < cols)
    reach_row = jnp.where(inside, reach_row, 1 << 20)
    if keys_own:
        step_row, step_col = (own >> 4) - reach_row, (own & 15) - reach_col
    else:
        step_row, step_col = reach_row - (own >> 4), reach_col - (own & 15)
    return (step_row >= -8) & (step_row <= 7) & (step_col >= -8) & (step_col <= 7)


def put_sides(block, left_ref, right_ref):
    sides = block.reshape(8, 2, 8, block.shape[-1])
    left_ref[...] = sides[:, 0].reshape(64, -1).astype(BF16)
    right_ref[...] = sides[:, 1].reshape(64, -1).astype(BF16)


def first_kernel(where_ref, x_ref, base_ref, left_ref, right_ref):
    base_ref[:TOK] = x_ref[...]
    base_ref[TOK:] = jnp.zeros((TOK, D), BF16)
    put_sides(x_ref[...].astype(F32), left_ref, right_ref)


def normed_low(x_ref):
    x = x_ref[...].astype(F32)
    inverse = lax.rsqrt(jnp.mean(x * x, axis=-1, keepdims=True) + 1e-06)
    return (x * inverse).astype(BF16)


def centre_kernel(where_ref, x_ref, w_ref, cot_ref, proj_ref, nlow_ref, cot_low_ref):
    low = normed_low(x_ref)
    nlow_ref[...] = low
    proj_ref[...] = nn(low, w_ref[...]).astype(BF16)
    cot_low_ref[...] = cot_ref[...].astype(BF16)


def side_kernel(where_ref, left_ref, right_ref, w_ref, wo_ref, cot_ref, proj_ref, dm_ref):
    low = jnp.concatenate([normed_low(left_ref), normed_low(right_ref)], axis=0)
    proj_ref[...] = nn(low, w_ref[...]).astype(BF16)
    dm_ref[...] = nt(cot_ref[...], wo_ref[...]).astype(BF16)


def forward_kernel(
    where_ref, x1, x2, proj_ref, side_ref, w_ref, cot_ref, dm_ref,
    kv_ref, prob_ref, nlow_ref, far_ref, mixed_ref, pack_ref, left_ref, right_ref,
):
    kv_ref[:TOK] = proj_ref[:, D:]
    kv_ref[TOK:OWN] = side_ref[:, D:]
    for piece, x_ref in enumerate((x1, x2)):
        low = normed_low(x_ref)
        far_ref[piece * OWN : (piece + 1) * OWN] = low
        if piece == 0:
            nlow_ref[...] = low[:TOK]
        kv_ref[(piece + 1) * OWN : (piece + 2) * OWN] = nn(low, w_ref[:, D:]).astype(BF16)
    ok = window(where_ref, False)
    ok2 = jnp.concatenate([ok, ok], axis=0)
    lane = lax.broadcasted_iota(jnp.int32, (TOK, 128), 1)
    stats = jnp.zeros((TOK, 128), F32)
    for pair in range(PAIRS):
        at = slice(128 * pair, 128 * pair + 128)
        query = two_heads(proj_ref[:, at] * 0.125)
        scores = nt(query, kv_ref[:, at])
        scores = jnp.where(ok2, scores, -1e30)
        highest = jnp.max(scores, axis=-1, keepdims=True)
        grown = jnp.exp(scores - highest)
        total = jnp.sum(grown, axis=-1, keepdims=True)
        probs = (grown * (1.0 / total)).astype(BF16)
        prob_ref[pair] = probs
        value = kv_ref[:, D + 128 * pair : D + 128 * pair + 128]
        mixed = one_block(nn(probs, value)).astype(BF16)
        mixed_ref[:, at] = mixed
        log_total = highest + jnp.log(total)
        delta = two_sums(dm_ref[:, at], mixed)
        for first, rest in ((0, log_total), (24, delta)):
            for part in range(3):
                piece = rest.astype(BF16).astype(F32)
                rest = rest - piece
                for head in range(2):
                    chosen = lane == first + 8 * part + 2 * pair + head
                    stats = jnp.where(chosen, piece[TOK * head : TOK * head + TOK], stats)
    starts = where_ref[5] == 0
    pack_ref[:, D:] = stats.astype(BF16)

    @pl.when(starts)
    def _():
        pack_ref[:, :D] = cot_ref[...]

    @pl.when(jnp.logical_not(starts))
    def _():
        pack_ref[:, :D] = mixed_ref[...]

    put_sides(pack_ref[...].astype(F32), left_ref, right_ref)


def turned_kernel(where_ref, proj_ref, side_ref, far_ref, w_ref, n0, n1, query_ref, nt_ref, full_ref):
    query_ref[:, :TOK] = proj_ref[:, :D].astype(F32).T.astype(BF16)
    query_ref[:, TOK:OWN] = side_ref[:, :D].astype(F32).T.astype(BF16)
    far = nn(far_ref[...], w_ref[:, :D]).astype(BF16)
    query_ref[:, OWN:] = far.astype(F32).T.astype(BF16)
    full_ref[:, :TOK] = n0[...].astype(F32).T
    full_ref[:, TOK:] = n1[...].astype(F32).T
    nt_ref[...] = own_half(where_ref, full_ref).astype(BF16)


def own_half(where_ref, full_ref):
    rows = [
        full_ref[pl.ds(pl.multiple_of((2 * at + where_ref[2]) * BLOCK, BLOCK), BLOCK)]
        for at in range(full_ref.shape[0] // (2 * BLOCK))
    ]
    return jnp.concatenate(rows, axis=0)


def key_probs_kernel(
    where_ref, p0, p1, p2, proj_ref, query_ref, prob_ref, mixed_ref, delta_ref
):
    head = lax.broadcasted_iota(jnp.int32, (8, 128), 0)
    lane = lax.broadcasted_iota(jnp.int32, (8, 128), 1)
    stats = jnp.concatenate([p[:, D:] for p in (p0, p1, p2)], axis=0)
    sums = []
    for first in (0, 24):
        chosen = ((lane & 7) == head) & (lane >= first) & (lane < first + 24)
        sums.append(nt(jnp.where(chosen, 1.0, 0.0).astype(BF16), stats))
    log_total, delta_ref[...] = sums

    @pl.when(where_ref[5] != 0)
    def _():
        for piece, p in enumerate((p0, p1, p2)):
            mixed_ref[:, piece * OWN : (piece + 1) * OWN] = p[:, :D].astype(F32).T.astype(BF16)

    ok = window(where_ref, True)
    for pair in range(PAIRS):
        key = two_heads(proj_ref[:, D + 128 * pair : D + 128 * pair + 128] * 0.125)
        scores = nn(key, query_ref[128 * pair : 128 * pair + 128])
        for side in range(2):
            at = 2 * pair + side
            part = scores[TOK * side : TOK * side + TOK] - log_total[at : at + 1]
            probs = jnp.exp(jnp.where(ok, part, -1e30))
            prob_ref[pair, TOK * side : TOK * side + TOK] = probs.astype(BF16)


def two_sums(grad, mixed):
    prod = grad.astype(F32) * mixed.astype(F32)
    lane = lax.broadcasted_iota(jnp.int32, prod.shape, 1)
    return jnp.concatenate(
        [
            jnp.sum(jnp.where(lane < 64, prod, 0.0), axis=-1, keepdims=True),
            jnp.sum(jnp.where(lane < 64, 0.0, prod), axis=-1, keepdims=True),
        ],
        axis=0,
    )


def query_kernel(where_ref, g_ref, w_ref, mixed_ref, kv_ref, prob_ref, dq_ref, dm_ref, *, turn):
    @pl.when(where_ref[5] == turn)
    def _():
        dm_ref[...] = nt(g_ref[...], w_ref[...]).astype(BF16)

        def one_pair(pair, carry):
            low = pl.multiple_of(128 * pair, 128)
            at = pl.ds(low, 128)
            grad = dm_ref[:, at]
            delta = two_sums(grad, mixed_ref[:, at])
            pressure = nt(two_heads(grad), kv_ref[:, pl.ds(low + D, 128)])
            slopes = (prob_ref[pair].astype(F32) * (pressure - delta)).astype(BF16)
            dq_ref[:, at] = (one_block(nn(slopes, kv_ref[:, at])) * 0.125).astype(BF16)
            return carry

        lax.fori_loop(0, PAIRS, one_pair, 0)


def turned_block(stacked):
    row = lax.broadcasted_iota(jnp.int32, (128, 128), 0)
    return jnp.where(row < 64, stacked[:, :128], stacked[:, 128:]).T


def key_kernel(
    where_ref, g0, g1, g2, wo_ref, delta_ref, proj_ref, query_ref, prob_ref, dq_ref, mixed_ref,
    *rest, turn, last,
):
    ins, rest = ((), rest) if last else (rest[:3], rest[3:])
    prev = (3 - last) if turn else 0
    prev, rest = rest[:prev], rest[prev:]
    outs, sends, dm_ref = rest[: 3 - last], rest[3 - last : -1], rest[-1]
    dp_ref, gl_ref = outs[:2]
    active = where_ref[5] == turn

    if prev:

        @pl.when(jnp.logical_not(active))
        def _():
            for new, old in zip(outs, prev):
                new[...] = old[...]

    @pl.when(active)
    def _():
        for piece, g in enumerate((g0, g1, g2)):
            d_mixed = nt(wo_ref[...], g[:, :D]).astype(BF16)
            dm_ref[:, piece * OWN : (piece + 1) * OWN] = d_mixed
        dp_ref[:, :D] = dq_ref[...]
        dp_ref[:, 3 * D :] = mixed_ref[...]
        gl_ref[:TOK] = g0[:TOK, :D]
        gl_ref[TOK:] = g1[:TOK, :D]
        for pair in range(PAIRS):
            at = slice(128 * pair, 128 * pair + 128)
            value = two_heads(proj_ref[:, 2 * D + 128 * pair : 2 * D + 128 * pair + 128])
            grad = dm_ref[at]
            if turn:
                prod = grad.astype(F32) * delta_ref[at].astype(F32)
                deltas = [jnp.sum(prod[r : r + 64], axis=0, keepdims=True) for r in (0, 64)]
            else:
                deltas = [delta_ref[2 * pair + side : 2 * pair + side + 1] for side in range(2)]
            pressure = nn(value, grad)
            probs = prob_ref[pair]
            d_value = nt(grad, probs)
            slopes = []
            for side in range(2):
                rows = slice(TOK * side, TOK * side + TOK)
                slopes.append(
                    (probs[rows].astype(F32) * (pressure[rows] - deltas[side])).astype(BF16)
                )
            d_key = nt(query_ref[at], jnp.concatenate(slopes, axis=0))
            low, high = D + 128 * pair, D + 128 * pair + 128
            dp_ref[:, low:high] = (turned_block(d_key) * 0.125).astype(BF16)
            dp_ref[:, D + low : D + high] = turned_block(d_value).astype(BF16)
        if not last:
            out = input_grad(dp_ref, *ins)
            outs[2][...] = out
            low_ref, left_ref, right_ref = sends
            low_ref[...] = out.astype(BF16)
            put_sides(out, left_ref, right_ref)


def input_grad(dp_ref, g_ref, wq_ref, x_ref):
    d_normed = nt(dp_ref[:, : 3 * D], wq_ref[...])
    x = x_ref[...].astype(F32)
    inverse = lax.rsqrt(jnp.mean(x * x, axis=-1, keepdims=True) + 1e-06)
    normed = x * inverse
    inner = jnp.mean(d_normed * normed, axis=-1, keepdims=True)
    return g_ref[...].astype(F32) + inverse * (d_normed - normed * inner)


def input_kernel(where_ref, dp_ref, g_ref, wq_ref, x_ref, prev_ref, in_ref, *, turn):
    @pl.when(where_ref[5] == turn)
    def _():
        in_ref[...] = input_grad(dp_ref, g_ref, wq_ref, x_ref)

    @pl.when(where_ref[5] != turn)
    def _():
        in_ref[...] = prev_ref[...]


def weight_kernel(where_ref, nt_ref, d0, d1, g_ref, *refs):
    outs, (left_ref, full_ref) = refs[:-2], refs[-2:]
    d_proj = jnp.concatenate([d0[:, : 3 * D], d1[:, : 3 * D]], axis=0)
    mixed = jnp.concatenate([d0[:, 3 * D :], d1[:, 3 * D :]], axis=0)
    full_ref[...] = tn(mixed, g_ref[...])
    left_ref[...] = nn(nt_ref[...], d_proj)
    core, cols = where_ref[2], len(outs)
    for distance, out_ref in enumerate(outs):
        col = lax.rem(where_ref[6] + distance, cols)
        for at, ref, step, first in (
            (slice(0, 3 * D), left_ref, BLOCK, 0), (slice(3 * D, 4 * D), full_ref, 2 * BLOCK, core)
        ):
            rows = [
                ref[pl.ds(pl.multiple_of(step * chip + first * BLOCK + 8 * col, 8), 8)]
                for chip in range(out_ref.shape[0] // 8)
            ]
            out_ref[:, at] = jnp.concatenate(rows, axis=0).astype(BF16)


def col_total_kernel(where_ref, *refs):
    total = refs[0][...].astype(F32)
    for ref in refs[1:-1]:
        total = total + ref[...].astype(F32)
    refs[-1][...] = total.astype(BF16)


def total_kernel(where_ref, part_ref, qkv_ref, out_ref, *, scale):
    total = part_ref[0].astype(F32)
    for source in range(1, part_ref.shape[0]):
        total = total + part_ref[source].astype(F32)
    qkv_ref[...] = total[:, : 3 * D] * scale
    out_ref[...] = total[:, 3 * D :] * scale


def call(kernel, outs, *args, scratch=(), flops=0):
    vmem = pl.BlockSpec(memory_space=pltpu.VMEM)
    return pl.pallas_call(
        kernel,
        out_shape=[jax.ShapeDtypeStruct(s, t) for s, t in outs],
        in_specs=[pl.BlockSpec(memory_space=pltpu.SMEM)] + [vmem] * (len(args) - 1),
        out_specs=[vmem] * len(outs),
        scratch_shapes=list(scratch),
        compiler_params=pltpu.CompilerParams(vmem_limit_bytes=VMEM_LIMIT),
        cost_estimate=pl.CostEstimate(flops=flops, bytes_accessed=4 << 20, transcendentals=0),
    )(*args)


def body(sizes, activations, qkv_weight, out_weight, cotangent):
    pipes, chips, cols = sizes

    def routed(block, step):
        pairs = []
        for p in range(pipes):
            for r in range(2 * chips):
                for c in range(cols):
                    p2, r2, c2 = step(p, r, c)
                    target = ((p2 % pipes) * 2 * chips + r2 % (2 * chips)) * cols + c2 % cols
                    pairs.append(((p * 2 * chips + r) * cols + c, target))
        return lax.ppermute(block, AXES, pairs)

    def col_rims(left_half, right_half, down=0):
        left = routed(right_half, lambda p, r, c: (p - down, r, c + 1))
        right = routed(left_half, lambda p, r, c: (p - down, r, c - 1))
        return left, right

    def mate(p, r, c):
        return p, r ^ 1, c

    def row_rims(pieces):
        own = jnp.concatenate(pieces, axis=0)
        beyond = routed(own, lambda p, r, c: (p, r - 1 + 2 * (r & 1), c))
        return own, routed(own, mate), beyond

    pipe, z, core, col = (lax.axis_index(axis) for axis in AXES)
    x = activations.reshape(TOK, D)
    w_qkv, w_out = qkv_weight[0], out_weight[0]
    cot = cotangent.reshape(TOK, D)
    row_total, col_total = 16 * chips, 16 * cols
    where = jnp.stack(
        [8 * (2 * z + core), 16 * col, core, row_total, col_total, pipes - 1 - pipe, col]
    ).astype(jnp.int32)

    base, low_side, high_side = call(
        first_kernel, [((OWN, D), BF16), ((64, D), BF16), ((64, D), BF16)], where, x
    )
    proj, nlow, cot_low = call(
        centre_kernel, [((TOK, 3 * D), BF16), ((TOK, D), BF16), ((TOK, D), BF16)],
        where, x, w_qkv, cot, flops=1 << 28,
    )
    left, right = col_rims(low_side, high_side)
    base, proj = lax.optimization_barrier((base, proj))
    own = lax.dynamic_update_slice(base, left, (TOK, 0))
    own, near, far = row_rims([lax.dynamic_update_slice(own, right, (TOK + 64, 0))])
    side_proj, d_mixed = call(
        side_kernel, [((TOK, 3 * D), BF16), ((TOK, D), BF16)],
        where, left, right, w_qkv, w_out, cot_low, flops=1 << 28,
    )
    wide = D + 128
    kv, q_probs, nlow_mate, low_far, mixed, pack, low_side, high_side = call(
        forward_kernel,
        [((REGION, 2 * D), BF16), ((PAIRS, OWN, REGION), BF16), ((TOK, D), BF16),
         ((2 * OWN, D), BF16), ((TOK, D), BF16), ((TOK, wide), BF16), ((64, wide), BF16),
         ((64, wide), BF16)],
        where, near, far, proj, side_proj, w_qkv, cot_low, d_mixed, flops=2 << 30,
    )
    sides = col_rims(low_side, high_side)
    queries, n_turned = call(
        turned_kernel, [((D, REGION), BF16), ((OWN, OWN), BF16)],
        where, proj, side_proj, low_far, w_qkv, nlow, nlow_mate,
        scratch=[pltpu.VMEM((D, OWN), F32)], flops=1 << 28,
    )

    def query_side(turn, gradient):
        return call(
            functools.partial(query_kernel, turn=turn), [((TOK, D), BF16)],
            where, gradient, w_out, mixed, kv, q_probs,
            scratch=[pltpu.VMEM((TOK, D), BF16)], flops=1 << 29,
        )[0]

    d_query = query_side(0, cot_low)
    left, right = sides
    right, queries, d_query = lax.optimization_barrier((right, queries, d_query))
    packs = row_rims([pack, left, right])
    k_probs, mixed_turned, delta = call(
        key_probs_kernel,
        [((PAIRS, OWN, REGION), BF16), ((D, REGION), BF16), ((8, REGION), F32)],
        where, *packs, proj, queries, flops=1 << 28,
    )
    gradient, gs = cot_low, packs
    state = ()
    for turn in range(pipes):
        last = turn == pipes - 1
        if turn > 0:
            low, low_side, high_side = sends
            gradient = routed(low, lambda p, r, c: (p - 1, r, c))
            left, right = col_rims(low_side, high_side, 1)
            left, d_query = lax.optimization_barrier((left, query_side(turn, gradient)))
            gs = row_rims([gradient, left, right])
        outs = [((TOK, 4 * D), BF16), ((OWN, D), BF16)]
        if not last:
            outs += [((TOK, D), F32), ((TOK, D), BF16), ((64, D), BF16), ((64, D), BF16)]
        ins = () if last else (gradient if turn else cot, w_qkv, x)
        outs = call(
            functools.partial(key_kernel, turn=turn, last=last), outs,
            where, *gs, w_out, mixed_turned if turn else delta, proj, queries, k_probs, d_query,
            mixed, *ins, *state[: 2 if last else 3],
            scratch=[pltpu.VMEM((D, REGION), BF16)], flops=1 << 30,
        )
        if last:
            d_proj, g_low = outs
            (d_in,) = call(
                functools.partial(input_kernel, turn=turn), [((TOK, D), F32)],
                where, d_proj, gradient, w_qkv, x, state[2], flops=1 << 28,
            )
        state, sends = outs[:3], outs[3:]
    parts = call(
        weight_kernel, [((8 * chips, 4 * D), BF16)] * cols,
        where, n_turned, d_proj, routed(d_proj, mate), g_low,
        scratch=[pltpu.VMEM((OWN, 3 * D), F32), pltpu.VMEM((D, D), F32)], flops=1 << 29,
    )
    parts = list(parts)
    for distance in sorted(range(1, cols), key=lambda d: -min(d, cols - d)):
        parts[distance] = routed(parts[distance], lambda p, r, c: (p, r, c + distance))
    parts[-1], d_in = lax.optimization_barrier((parts[-1], d_in))
    (part,) = call(col_total_kernel, [((8 * chips, 4 * D), BF16)], where, *parts)
    part = part.reshape(chips, 8, 4 * D)
    part = lax.all_to_all(part, "z", 0, 0, tiled=True)
    qkv_part, out_part = call(
        functools.partial(total_kernel, scale=(row_total * col_total) ** (-0.5)),
        [((8, 3 * D), F32), ((8, D), F32)], where, part,
    )
    return d_in.reshape(1, 8, 16, D), qkv_part[None], out_part[None]


def solution(mesh):
    pipes, rows, cols = (mesh.shape[axis] for axis in ("pipe", "row", "col"))
    fine = Mesh(np.asarray(mesh.devices).reshape(pipes, rows // 2, 2, cols), AXES)
    row = ("z", "core")
    return jax.shard_map(
        functools.partial(body, (pipes, rows // 2, cols)),
        mesh=fine,
        in_specs=(
            P("pipe", row, "col", None),
            P("pipe", None, None),
            P("pipe", None, None),
            P(row, "col", None),
        ),
        out_specs=(
            P("pipe", row, "col", None),
            P("pipe", ("z", "core", "col"), None),
            P("pipe", ("z", "core", "col"), None),
        ),
        check_vma=False,
    )
```

```python
import functools

import jax
import jax.numpy as jnp
import numpy as np
from jax import lax
from jax.experimental import pallas as pl
from jax.experimental.pallas import tpu as pltpu
from jax.sharding import Mesh
from jax.sharding import PartitionSpec as P

F32 = jnp.float32
BF16 = jnp.bfloat16
AXES = ("pipe", "z", "core", "col")
D = 512
PAIRS = 4
TOK = 128
OWN = 256
REGION = 768
BLOCK = 32
VMEM_LIMIT = 40 * 1024 * 1024


def nn(a, b):
    return lax.dot_general(a, b, (((1,), (0,)), ((), ())), preferred_element_type=F32)


def nt(a, b):
    return lax.dot_general(a, b, (((1,), (1,)), ((), ())), preferred_element_type=F32)


def tn(a, b):
    return lax.dot_general(a, b, (((0,), (0,)), ((), ())), preferred_element_type=F32)


def two_heads(block):
    lane = lax.broadcasted_iota(jnp.int32, block.shape, 1)
    zero = jnp.zeros_like(block)
    return jnp.concatenate(
        [jnp.where(lane < 64, block, zero), jnp.where(lane < 64, zero, block)], axis=0
    )


def one_block(stacked):
    half = stacked.shape[0] // 2
    lane = lax.broadcasted_iota(jnp.int32, (half, 128), 1)
    return jnp.where(lane < 64, stacked[:half], stacked[half:])


def place(index, core):
    piece = index >> 8
    inner = index & 255
    side = inner - 128
    is_centre = inner < 128
    row = jnp.where(is_centre, inner >> 4, (side & 63) >> 3)
    col = jnp.where(is_centre, inner & 15, jnp.where(side < 64, (side & 7) - 8, (side & 7) + 16))
    mate = jnp.where(core == 0, 8, -8)
    row = row + jnp.where(piece == 1, mate, jnp.where(piece == 2, -mate, 0))
    return row, col


def window(where_ref, keys_own):
    row0, col0, core, rows, cols = (where_ref[i] for i in range(5))
    own = lax.broadcasted_iota(jnp.int32, (TOK, 1), 0)
    reach_row, reach_col = place(lax.broadcasted_iota(jnp.int32, (1, REGION), 1), core)
    grid_row, grid_col = row0 + reach_row, col0 + reach_col
    inside = (grid_row >= 0) & (grid_row < rows) & (grid_col >= 0) & (grid_col < cols)
    reach_row = jnp.where(inside, reach_row, 1 << 20)
    if keys_own:
        step_row, step_col = (own >> 4) - reach_row, (own & 15) - reach_col
    else:
        step_row, step_col = reach_row - (own >> 4), reach_col - (own & 15)
    return (step_row >= -8) & (step_row <= 7) & (step_col >= -8) & (step_col <= 7)


def put_sides(block, left_ref, right_ref):
    sides = block.reshape(8, 2, 8, block.shape[-1])
    left_ref[...] = sides[:, 0].reshape(64, -1).astype(BF16)
    right_ref[...] = sides[:, 1].reshape(64, -1).astype(BF16)


def normed_low(x_ref):
    x = x_ref[...].astype(F32)
    inverse = lax.rsqrt(jnp.mean(x * x, axis=-1, keepdims=True) + 1e-06)
    return (x * inverse).astype(BF16)


def centre_kernel(where_ref, x_ref, w_ref, cot_ref, base_ref, proj_ref, nlow_ref, cot_low_ref):
    base_ref[:TOK] = x_ref[...]
    base_ref[TOK:] = jnp.zeros((TOK, D), BF16)
    low = normed_low(x_ref)
    nlow_ref[...] = low
    proj_ref[...] = nn(low, w_ref[...]).astype(BF16)
    cot_low_ref[...] = cot_ref[...].astype(BF16)


def side_kernel(where_ref, left_ref, right_ref, w_ref, wo_ref, cot_ref, proj_ref, dm_ref):
    low = jnp.concatenate([normed_low(left_ref), normed_low(right_ref)], axis=0)
    proj_ref[...] = nn(low, w_ref[...]).astype(BF16)
    dm_ref[...] = nt(cot_ref[...], wo_ref[...]).astype(BF16)


def forward_kernel(
    where_ref, x1, x2, proj_ref, side_ref, w_ref, cot_ref, dm_ref,
    kv_ref, prob_ref, nlow_ref, far_ref, mixed_ref, pack_ref, left_ref, right_ref,
):
    kv_ref[:TOK] = proj_ref[:, D:]
    kv_ref[TOK:OWN] = side_ref[:, D:]
    for piece, x_ref in enumerate((x1, x2)):
        low = normed_low(x_ref)
        far_ref[piece * OWN : (piece + 1) * OWN] = low
        if piece == 0:
            nlow_ref[...] = low[:TOK]
        kv_ref[(piece + 1) * OWN : (piece + 2) * OWN] = nn(low, w_ref[:, D:]).astype(BF16)
    ok = window(where_ref, False)
    ok2 = jnp.concatenate([ok, ok], axis=0)
    lane = lax.broadcasted_iota(jnp.int32, (TOK, 128), 1)
    stats = jnp.zeros((TOK, 128), F32)
    for pair in range(PAIRS):
        at = slice(128 * pair, 128 * pair + 128)
        query = two_heads(proj_ref[:, at] * 0.125)
        scores = nt(query, kv_ref[:, at])
        scores = jnp.where(ok2, scores, -1e30)
        highest = jnp.max(scores, axis=-1, keepdims=True)
        grown = jnp.exp(scores - highest)
        total = jnp.sum(grown, axis=-1, keepdims=True)
        probs = (grown * (1.0 / total)).astype(BF16)
        prob_ref[pair] = probs
        value = kv_ref[:, D + 128 * pair : D + 128 * pair + 128]
        mixed = one_block(nn(probs, value)).astype(BF16)
        mixed_ref[:, at] = mixed
        log_total = highest + jnp.log(total)
        delta = two_sums(dm_ref[:, at], mixed)
        for first, rest in ((0, log_total), (24, delta)):
            for part in range(3):
                piece = rest.astype(BF16).astype(F32)
                rest = rest - piece
                for head in range(2):
                    chosen = lane == first + 8 * part + 2 * pair + head
                    stats = jnp.where(chosen, piece[TOK * head : TOK * head + TOK], stats)
    starts = where_ref[5] == 0
    pack_ref[:, D:] = stats.astype(BF16)

    @pl.when(starts)
    def _():
        pack_ref[:, :D] = cot_ref[...]

    @pl.when(jnp.logical_not(starts))
    def _():
        pack_ref[:, :D] = mixed_ref[...]

    put_sides(pack_ref[...].astype(F32), left_ref, right_ref)


def turned_kernel(where_ref, proj_ref, side_ref, far_ref, w_ref, n0, n1, query_ref, nt_ref, full_ref):
    query_ref[:, :TOK] = proj_ref[:, :D].astype(F32).T.astype(BF16)
    query_ref[:, TOK:OWN] = side_ref[:, :D].astype(F32).T.astype(BF16)
    far = nn(far_ref[...], w_ref[:, :D]).astype(BF16)
    query_ref[:, OWN:] = far.astype(F32).T.astype(BF16)
    full_ref[:, :TOK] = n0[...].astype(F32).T
    full_ref[:, TOK:] = n1[...].astype(F32).T
    nt_ref[...] = own_half(where_ref, full_ref).astype(BF16)


def own_half(where_ref, full_ref):
    rows = [
        full_ref[pl.ds(pl.multiple_of((2 * at + where_ref[2]) * BLOCK, BLOCK), BLOCK)]
        for at in range(full_ref.shape[0] // (2 * BLOCK))
    ]
    return jnp.concatenate(rows, axis=0)


def key_probs_kernel(
    where_ref, p0, p1, p2, proj_ref, query_ref, prob_ref, mixed_ref, delta_ref
):
    head = lax.broadcasted_iota(jnp.int32, (8, 128), 0)
    lane = lax.broadcasted_iota(jnp.int32, (8, 128), 1)
    stats = jnp.concatenate([p[:, D:] for p in (p0, p1, p2)], axis=0)
    sums = []
    for first in (0, 24):
        chosen = ((lane & 7) == head) & (lane >= first) & (lane < first + 24)
        sums.append(nt(jnp.where(chosen, 1.0, 0.0).astype(BF16), stats))
    log_total, delta_ref[...] = sums

    @pl.when(where_ref[5] != 0)
    def _():
        for piece, p in enumerate((p0, p1, p2)):
            mixed_ref[:, piece * OWN : (piece + 1) * OWN] = p[:, :D].astype(F32).T.astype(BF16)

    ok = window(where_ref, True)
    for pair in range(PAIRS):
        key = two_heads(proj_ref[:, D + 128 * pair : D + 128 * pair + 128] * 0.125)
        scores = nn(key, query_ref[128 * pair : 128 * pair + 128])
        for side in range(2):
            at = 2 * pair + side
            part = scores[TOK * side : TOK * side + TOK] - log_total[at : at + 1]
            probs = jnp.exp(jnp.where(ok, part, -1e30))
            prob_ref[pair, TOK * side : TOK * side + TOK] = probs.astype(BF16)


def two_sums(grad, mixed):
    prod = grad.astype(F32) * mixed.astype(F32)
    lane = lax.broadcasted_iota(jnp.int32, prod.shape, 1)
    return jnp.concatenate(
        [
            jnp.sum(jnp.where(lane < 64, prod, 0.0), axis=-1, keepdims=True),
            jnp.sum(jnp.where(lane < 64, 0.0, prod), axis=-1, keepdims=True),
        ],
        axis=0,
    )


def query_kernel(where_ref, g_ref, w_ref, mixed_ref, kv_ref, prob_ref, dq_ref, dm_ref, *, turn):
    @pl.when(where_ref[5] == turn)
    def _():
        dm_ref[...] = nt(g_ref[...], w_ref[...]).astype(BF16)

        def one_pair(pair, carry):
            low = pl.multiple_of(128 * pair, 128)
            at = pl.ds(low, 128)
            grad = dm_ref[:, at]
            delta = two_sums(grad, mixed_ref[:, at])
            pressure = nt(two_heads(grad), kv_ref[:, pl.ds(low + D, 128)])
            slopes = (prob_ref[pair].astype(F32) * (pressure - delta)).astype(BF16)
            dq_ref[:, at] = (one_block(nn(slopes, kv_ref[:, at])) * 0.125).astype(BF16)
            return carry

        lax.fori_loop(0, PAIRS, one_pair, 0)


def turned_block(stacked):
    row = lax.broadcasted_iota(jnp.int32, (128, 128), 0)
    return jnp.where(row < 64, stacked[:, :128], stacked[:, 128:]).T


def key_side(grads, first, turn, wo_ref, delta_ref, proj_ref, query_ref, prob_ref, dm_ref):
    for piece, g in enumerate(grads):
        d_mixed = nt(wo_ref[...], g[:, :D]).astype(BF16)
        dm_ref[:, piece * OWN : (piece + 1) * OWN] = d_mixed
    span = slice(first, first + OWN * len(grads))
    for pair in range(PAIRS):
        at = slice(128 * pair, 128 * pair + 128)
        value = two_heads(proj_ref[:, 2 * D + 128 * pair : 2 * D + 128 * pair + 128])
        grad = dm_ref[at, : OWN * len(grads)]
        if turn:
            prod = grad.astype(F32) * delta_ref[at, span].astype(F32)
            deltas = [jnp.sum(prod[r : r + 64], axis=0, keepdims=True) for r in (0, 64)]
        else:
            deltas = [delta_ref[2 * pair + side : 2 * pair + side + 1, span] for side in range(2)]
        pressure = nn(value, grad)
        probs = prob_ref[pair, :, span]
        slopes = []
        for side in range(2):
            rows = slice(TOK * side, TOK * side + TOK)
            slopes.append((probs[rows].astype(F32) * (pressure[rows] - deltas[side])).astype(BF16))
        d_key = nt(query_ref[at, span], jnp.concatenate(slopes, axis=0))
        yield pair, turned_block(d_key), turned_block(nt(grad, probs))


def near_kernel(
    where_ref, g0, wo_ref, delta_ref, proj_ref, query_ref, prob_ref, sum_ref, dm_ref, *, turn
):
    @pl.when(where_ref[5] == turn)
    def _():
        side = key_side((g0,), 0, turn, wo_ref, delta_ref, proj_ref, query_ref, prob_ref, dm_ref)
        for pair, d_key, d_value in side:
            sum_ref[pair, 0] = d_key
            sum_ref[pair, 1] = d_value


def key_kernel(
    where_ref, g0, g1, g2, wo_ref, delta_ref, proj_ref, query_ref, prob_ref, dq_ref, mixed_ref,
    *rest, turn, last,
):
    sums, rest = (rest[:1], rest[1:]) if turn else ((), rest)
    ins, rest = ((), rest) if last else (rest[:3], rest[3:])
    prev = (3 - last) if turn else 0
    prev, rest = rest[:prev], rest[prev:]
    outs, sends, dm_ref = rest[: 3 - last], rest[3 - last : -1], rest[-1]
    dp_ref, gl_ref = outs[:2]
    active = where_ref[5] == turn

    if prev:

        @pl.when(jnp.logical_not(active))
        def _():
            for new, old in zip(outs, prev):
                new[...] = old[...]

    @pl.when(active)
    def _():
        dp_ref[:, :D] = dq_ref[...]
        dp_ref[:, 3 * D :] = mixed_ref[...]
        gl_ref[:TOK] = g0[:TOK, :D]
        gl_ref[TOK:] = g1[:TOK, :D]
        grads, first = ((g1, g2), OWN) if turn else ((g0, g1, g2), 0)
        side = key_side(
            grads, first, turn, wo_ref, delta_ref, proj_ref, query_ref, prob_ref, dm_ref
        )
        for pair, d_key, d_value in side:
            for ref in sums:
                d_key, d_value = d_key + ref[pair, 0], d_value + ref[pair, 1]
            low, high = D + 128 * pair, D + 128 * pair + 128
            dp_ref[:, low:high] = (d_key * 0.125).astype(BF16)
            dp_ref[:, D + low : D + high] = d_value.astype(BF16)
        if not last:
            out = input_grad(dp_ref, *ins)
            outs[2][...] = out
            low_ref, left_ref, right_ref = sends
            low_ref[...] = out.astype(BF16)
            put_sides(out, left_ref, right_ref)


def input_grad(dp_ref, g_ref, wq_ref, x_ref):
    d_normed = nt(dp_ref[:, : 3 * D], wq_ref[...])
    x = x_ref[...].astype(F32)
    inverse = lax.rsqrt(jnp.mean(x * x, axis=-1, keepdims=True) + 1e-06)
    normed = x * inverse
    inner = jnp.mean(d_normed * normed, axis=-1, keepdims=True)
    return g_ref[...].astype(F32) + inverse * (d_normed - normed * inner)


def input_kernel(where_ref, dp_ref, g_ref, wq_ref, x_ref, prev_ref, in_ref, *, turn):
    @pl.when(where_ref[5] == turn)
    def _():
        in_ref[...] = input_grad(dp_ref, g_ref, wq_ref, x_ref)

    @pl.when(where_ref[5] != turn)
    def _():
        in_ref[...] = prev_ref[...]


def weight_kernel(where_ref, nt_ref, d0, d1, g_ref, *refs):
    outs, (left_ref, full_ref) = refs[:-2], refs[-2:]
    d_proj = jnp.concatenate([d0[:, : 3 * D], d1[:, : 3 * D]], axis=0)
    mixed = jnp.concatenate([d0[:, 3 * D :], d1[:, 3 * D :]], axis=0)
    full_ref[...] = tn(mixed, g_ref[...])
    left_ref[...] = nn(nt_ref[...], d_proj)
    core, cols = where_ref[2], len(outs)
    for distance, out_ref in enumerate(outs):
        col = lax.rem(where_ref[6] + distance, cols)
        for at, ref, step, first in (
            (slice(0, 3 * D), left_ref, BLOCK, 0), (slice(3 * D, 4 * D), full_ref, 2 * BLOCK, core)
        ):
            rows = [
                ref[pl.ds(pl.multiple_of(step * chip + first * BLOCK + 8 * col, 8), 8)]
                for chip in range(out_ref.shape[0] // 8)
            ]
            out_ref[:, at] = jnp.concatenate(rows, axis=0).astype(BF16)


def col_total_kernel(where_ref, *refs):
    total = refs[0][...].astype(F32)
    for ref in refs[1:-1]:
        total = total + ref[...].astype(F32)
    refs[-1][...] = total.astype(BF16)


def total_kernel(where_ref, part_ref, qkv_ref, out_ref, *, scale):
    total = part_ref[0].astype(F32)
    for source in range(1, part_ref.shape[0]):
        total = total + part_ref[source].astype(F32)
    qkv_ref[...] = total[:, : 3 * D] * scale
    out_ref[...] = total[:, 3 * D :] * scale


def call(kernel, outs, *args, scratch=(), flops=0):
    vmem = pl.BlockSpec(memory_space=pltpu.VMEM)
    return pl.pallas_call(
        kernel,
        out_shape=[jax.ShapeDtypeStruct(s, t) for s, t in outs],
        in_specs=[pl.BlockSpec(memory_space=pltpu.SMEM)] + [vmem] * (len(args) - 1),
        out_specs=[vmem] * len(outs),
        scratch_shapes=list(scratch),
        compiler_params=pltpu.CompilerParams(vmem_limit_bytes=VMEM_LIMIT),
        cost_estimate=pl.CostEstimate(flops=flops, bytes_accessed=4 << 20, transcendentals=0),
    )(*args)


def body(sizes, activations, qkv_weight, out_weight, cotangent):
    pipes, chips, cols = sizes

    def routed(block, step):
        pairs = []
        for p in range(pipes):
            for r in range(2 * chips):
                for c in range(cols):
                    p2, r2, c2 = step(p, r, c)
                    target = ((p2 % pipes) * 2 * chips + r2 % (2 * chips)) * cols + c2 % cols
                    pairs.append(((p * 2 * chips + r) * cols + c, target))
        return lax.ppermute(block, AXES, pairs)

    def col_rims(left_half, right_half, down=0):
        left = routed(right_half, lambda p, r, c: (p - down, r, c + 1))
        right = routed(left_half, lambda p, r, c: (p - down, r, c - 1))
        return left, right

    def mate(p, r, c):
        return p, r ^ 1, c

    def row_rims(pieces):
        own = jnp.concatenate(pieces, axis=0)
        beyond = routed(own, lambda p, r, c: (p, r - 1 + 2 * (r & 1), c))
        return own, routed(own, mate), beyond

    pipe, z, core, col = (lax.axis_index(axis) for axis in AXES)
    x = activations.reshape(TOK, D)
    w_qkv, w_out = qkv_weight[0], out_weight[0]
    cot = cotangent.reshape(TOK, D)
    row_total, col_total = 16 * chips, 16 * cols
    where = jnp.stack(
        [8 * (2 * z + core), 16 * col, core, row_total, col_total, pipes - 1 - pipe, col]
    ).astype(jnp.int32)

    x_sides = x.reshape(8, 2, 8, D)
    low_side, high_side = x_sides[:, 0].reshape(64, D), x_sides[:, 1].reshape(64, D)
    base, proj, nlow, cot_low = call(
        centre_kernel, [((OWN, D), BF16), ((TOK, 3 * D), BF16), ((TOK, D), BF16), ((TOK, D), BF16)],
        where, x, w_qkv, cot, flops=1 << 28,
    )
    left, right = col_rims(low_side, high_side)
    own = lax.dynamic_update_slice(base, left, (TOK, 0))
    own, near, far = row_rims([lax.dynamic_update_slice(own, right, (TOK + 64, 0))])
    side_proj, d_mixed = call(
        side_kernel, [((TOK, 3 * D), BF16), ((TOK, D), BF16)],
        where, left, right, w_qkv, w_out, cot_low, flops=1 << 28,
    )
    wide = D + 128
    kv, q_probs, nlow_mate, low_far, mixed, pack, low_side, high_side = call(
        forward_kernel,
        [((REGION, 2 * D), BF16), ((PAIRS, OWN, REGION), BF16), ((TOK, D), BF16),
         ((2 * OWN, D), BF16), ((TOK, D), BF16), ((TOK, wide), BF16), ((64, wide), BF16),
         ((64, wide), BF16)],
        where, near, far, proj, side_proj, w_qkv, cot_low, d_mixed, flops=2 << 30,
    )
    sides = col_rims(low_side, high_side)
    queries, n_turned = call(
        turned_kernel, [((D, REGION), BF16), ((OWN, OWN), BF16)],
        where, proj, side_proj, low_far, w_qkv, nlow, nlow_mate,
        scratch=[pltpu.VMEM((D, OWN), F32)], flops=1 << 28,
    )

    def query_side(turn, gradient):
        return call(
            functools.partial(query_kernel, turn=turn), [((TOK, D), BF16)],
            where, gradient, w_out, mixed, kv, q_probs,
            scratch=[pltpu.VMEM((TOK, D), BF16)], flops=1 << 29,
        )[0]

    d_query = query_side(0, cot_low)
    left, right = sides
    right, queries, d_query = lax.optimization_barrier((right, queries, d_query))
    packs = row_rims([pack, left, right])
    k_probs, mixed_turned, delta = call(
        key_probs_kernel,
        [((PAIRS, OWN, REGION), BF16), ((D, REGION), BF16), ((8, REGION), F32)],
        where, *packs, proj, queries, flops=1 << 28,
    )
    gradient, gs = cot_low, packs
    state = ()
    for turn in range(pipes):
        last = turn == pipes - 1
        if turn > 0:
            low, low_side, high_side = sends
            gradient = routed(low, lambda p, r, c: (p - 1, r, c))
            left, right = col_rims(low_side, high_side, 1)
            left, d_query = lax.optimization_barrier((left, query_side(turn, gradient)))
            gs = row_rims([gradient, left, right])
        outs = [((TOK, 4 * D), BF16), ((OWN, D), BF16)]
        if not last:
            outs += [((TOK, D), F32), ((TOK, D), BF16), ((64, D), BF16), ((64, D), BF16)]
        ins = () if last else (gradient if turn else cot, w_qkv, x)
        fixed = (w_out, mixed_turned if turn else delta, proj, queries, k_probs)
        sums = ()
        if turn:
            sums = call(
                functools.partial(near_kernel, turn=turn), [((PAIRS, 2, 128, 128), F32)],
                where, gs[0], *fixed, scratch=[pltpu.VMEM((D, OWN), BF16)], flops=1 << 29,
            )
        outs = call(
            functools.partial(key_kernel, turn=turn, last=last), outs,
            where, *gs, *fixed, d_query, mixed, *sums, *ins, *state[: 2 if last else 3],
            scratch=[pltpu.VMEM((D, REGION), BF16)], flops=1 << 30,
        )
        if last:
            d_proj, g_low = outs
            (d_in,) = call(
                functools.partial(input_kernel, turn=turn), [((TOK, D), F32)],
                where, d_proj, gradient, w_qkv, x, state[2], flops=1 << 28,
            )
        state, sends = outs[:3], outs[3:]
    parts = call(
        weight_kernel, [((8 * chips, 4 * D), BF16)] * cols,
        where, n_turned, d_proj, routed(d_proj, mate), g_low,
        scratch=[pltpu.VMEM((OWN, 3 * D), F32), pltpu.VMEM((D, D), F32)], flops=1 << 29,
    )
    parts = list(parts)
    for distance in sorted(range(1, cols), key=lambda d: -min(d, cols - d)):
        parts[distance] = routed(parts[distance], lambda p, r, c: (p, r, c + distance))
    parts[-1], d_in = lax.optimization_barrier((parts[-1], d_in))
    (part,) = call(col_total_kernel, [((8 * chips, 4 * D), BF16)], where, *parts)
    part = part.reshape(chips, 8, 4 * D)
    part = lax.all_to_all(part, "z", 0, 0, tiled=True)
    qkv_part, out_part = call(
        functools.partial(total_kernel, scale=(row_total * col_total) ** (-0.5)),
        [((8, 3 * D), F32), ((8, D), F32)], where, part,
    )
    return d_in.reshape(1, 8, 16, D), qkv_part[None], out_part[None]


def solution(mesh):
    pipes, rows, cols = (mesh.shape[axis] for axis in ("pipe", "row", "col"))
    fine = Mesh(np.asarray(mesh.devices).reshape(pipes, rows // 2, 2, cols), AXES)
    row = ("z", "core")
    return jax.shard_map(
        functools.partial(body, (pipes, rows // 2, cols)),
        mesh=fine,
        in_specs=(
            P("pipe", row, "col", None),
            P("pipe", None, None),
            P("pipe", None, None),
            P(row, "col", None),
        ),
        out_specs=(
            P("pipe", row, "col", None),
            P("pipe", ("z", "core", "col"), None),
            P("pipe", ("z", "core", "col"), None),
        ),
        check_vma=False,
    )
```

```python
import functools

import jax
import jax.numpy as jnp
import numpy as np
from jax import lax
from jax.experimental import pallas as pl
from jax.experimental.pallas import tpu as pltpu
from jax.sharding import Mesh
from jax.sharding import PartitionSpec as P

F32 = jnp.float32
BF16 = jnp.bfloat16
AXES = ("pipe", "z", "core", "col")
D = 512
PAIRS = 4
TOK = 128
OWN = 256
REGION = 768
BLOCK = 32
VMEM_LIMIT = 40 * 1024 * 1024


def nn(a, b):
    return lax.dot_general(a, b, (((1,), (0,)), ((), ())), preferred_element_type=F32)


def nt(a, b):
    return lax.dot_general(a, b, (((1,), (1,)), ((), ())), preferred_element_type=F32)


def tn(a, b):
    return lax.dot_general(a, b, (((0,), (0,)), ((), ())), preferred_element_type=F32)


def two_heads(block):
    lane = lax.broadcasted_iota(jnp.int32, block.shape, 1)
    zero = jnp.zeros_like(block)
    return jnp.concatenate(
        [jnp.where(lane < 64, block, zero), jnp.where(lane < 64, zero, block)], axis=0
    )


def one_block(stacked):
    half = stacked.shape[0] // 2
    lane = lax.broadcasted_iota(jnp.int32, (half, 128), 1)
    return jnp.where(lane < 64, stacked[:half], stacked[half:])


def place(index, core):
    piece = index >> 8
    inner = index & 255
    side = inner - 128
    is_centre = inner < 128
    row = jnp.where(is_centre, inner >> 4, (side & 63) >> 3)
    col = jnp.where(is_centre, inner & 15, jnp.where(side < 64, (side & 7) - 8, (side & 7) + 16))
    mate = jnp.where(core == 0, 8, -8)
    row = row + jnp.where(piece == 1, mate, jnp.where(piece == 2, -mate, 0))
    return row, col


def window(where_ref, keys_own):
    row0, col0, core, rows, cols = (where_ref[i] for i in range(5))
    own = lax.broadcasted_iota(jnp.int32, (TOK, 1), 0)
    reach_row, reach_col = place(lax.broadcasted_iota(jnp.int32, (1, REGION), 1), core)
    grid_row, grid_col = row0 + reach_row, col0 + reach_col
    inside = (grid_row >= 0) & (grid_row < rows) & (grid_col >= 0) & (grid_col < cols)
    reach_row = jnp.where(inside, reach_row, 1 << 20)
    if keys_own:
        step_row, step_col = (own >> 4) - reach_row, (own & 15) - reach_col
    else:
        step_row, step_col = reach_row - (own >> 4), reach_col - (own & 15)
    return (step_row >= -8) & (step_row <= 7) & (step_col >= -8) & (step_col <= 7)


def put_sides(block, left_ref, right_ref):
    sides = block.reshape(8, 2, 8, block.shape[-1])
    left_ref[...] = sides[:, 0].reshape(64, -1).astype(BF16)
    right_ref[...] = sides[:, 1].reshape(64, -1).astype(BF16)


def normed_low(x_ref):
    x = x_ref[...].astype(F32)
    inverse = lax.rsqrt(jnp.mean(x * x, axis=-1, keepdims=True) + 1e-06)
    return (x * inverse).astype(BF16)


def centre_kernel(where_ref, x_ref, w_ref, base_ref, proj_ref, nlow_ref):
    base_ref[:TOK] = x_ref[...]
    base_ref[TOK:] = jnp.zeros((TOK, D), BF16)
    low = normed_low(x_ref)
    nlow_ref[...] = low
    proj_ref[...] = nn(low, w_ref[...]).astype(BF16)


def side_kernel(
    where_ref, left_ref, right_ref, w_ref, wo_ref, cot_ref, proj_ref, cot_low_ref, dm_ref
):
    low = jnp.concatenate([normed_low(left_ref), normed_low(right_ref)], axis=0)
    proj_ref[...] = nn(low, w_ref[...]).astype(BF16)
    grad = cot_ref[...].astype(BF16)
    cot_low_ref[...] = grad
    dm_ref[...] = nt(grad, wo_ref[...]).astype(BF16)


def forward_kernel(
    where_ref, x1, x2, proj_ref, side_ref, w_ref, cot_ref, dm_ref,
    kv_ref, prob_ref, nlow_ref, far_ref, mixed_ref, pack_ref, left_ref, right_ref,
):
    kv_ref[:TOK] = proj_ref[:, D:]
    kv_ref[TOK:OWN] = side_ref[:, D:]
    for piece, x_ref in enumerate((x1, x2)):
        low = normed_low(x_ref)
        far_ref[piece * OWN : (piece + 1) * OWN] = low
        if piece == 0:
            nlow_ref[...] = low[:TOK]
        kv_ref[(piece + 1) * OWN : (piece + 2) * OWN] = nn(low, w_ref[:, D:]).astype(BF16)
    ok = window(where_ref, False)
    ok2 = jnp.concatenate([ok, ok], axis=0)
    lane = lax.broadcasted_iota(jnp.int32, (TOK, 128), 1)
    stats = jnp.zeros((TOK, 128), F32)
    for pair in range(PAIRS):
        at = slice(128 * pair, 128 * pair + 128)
        query = two_heads(proj_ref[:, at] * 0.125)
        scores = nt(query, kv_ref[:, at])
        scores = jnp.where(ok2, scores, -1e30)
        highest = jnp.max(scores, axis=-1, keepdims=True)
        grown = jnp.exp(scores - highest)
        total = jnp.sum(grown, axis=-1, keepdims=True)
        probs = (grown * (1.0 / total)).astype(BF16)
        prob_ref[pair] = probs
        value = kv_ref[:, D + 128 * pair : D + 128 * pair + 128]
        mixed = one_block(nn(probs, value)).astype(BF16)
        mixed_ref[:, at] = mixed
        log_total = highest + jnp.log(total)
        delta = two_sums(dm_ref[:, at], mixed)
        for first, rest in ((0, log_total), (24, delta)):
            for part in range(3):
                piece = rest.astype(BF16).astype(F32)
                rest = rest - piece
                for head in range(2):
                    chosen = lane == first + 8 * part + 2 * pair + head
                    stats = jnp.where(chosen, piece[TOK * head : TOK * head + TOK], stats)
    starts = where_ref[5] == 0
    pack_ref[:, D:] = stats.astype(BF16)

    @pl.when(starts)
    def _():
        pack_ref[:, :D] = cot_ref[...]

    @pl.when(jnp.logical_not(starts))
    def _():
        pack_ref[:, :D] = mixed_ref[...]

    put_sides(pack_ref[...].astype(F32), left_ref, right_ref)


def turned_kernel(where_ref, proj_ref, side_ref, far_ref, w_ref, n0, n1, query_ref, nt_ref, full_ref):
    query_ref[:, :TOK] = proj_ref[:, :D].astype(F32).T.astype(BF16)
    query_ref[:, TOK:OWN] = side_ref[:, :D].astype(F32).T.astype(BF16)
    far = nn(far_ref[...], w_ref[:, :D]).astype(BF16)
    query_ref[:, OWN:] = far.astype(F32).T.astype(BF16)
    full_ref[:, :TOK] = n0[...].astype(F32).T
    full_ref[:, TOK:] = n1[...].astype(F32).T
    nt_ref[...] = own_half(where_ref, full_ref).astype(BF16)


def own_half(where_ref, full_ref):
    rows = [
        full_ref[pl.ds(pl.multiple_of((2 * at + where_ref[2]) * BLOCK, BLOCK), BLOCK)]
        for at in range(full_ref.shape[0] // (2 * BLOCK))
    ]
    return jnp.concatenate(rows, axis=0)


def key_probs_kernel(
    where_ref, p0, p1, p2, proj_ref, query_ref, prob_ref, mixed_ref, delta_ref, total_ref
):
    head = lax.broadcasted_iota(jnp.int32, (8, 128), 0)
    lane = lax.broadcasted_iota(jnp.int32, (8, 128), 1)
    stats = jnp.concatenate([p[:, D:] for p in (p0, p1, p2)], axis=0)
    sums = []
    for first in (0, 24):
        chosen = ((lane & 7) == head) & (lane >= first) & (lane < first + 24)
        sums.append(nt(jnp.where(chosen, 1.0, 0.0).astype(BF16), stats))
    log_total, delta_ref[...] = sums

    @pl.when(where_ref[5] != 0)
    def _():
        for piece, p in enumerate((p0, p1, p2)):
            mixed_ref[:, piece * OWN : (piece + 1) * OWN] = p[:, :D].astype(F32).T.astype(BF16)

    total_ref[...] = log_total
    ok = window(where_ref, True)

    def one_pair(pair, carry):
        low = pl.multiple_of(128 * pair, 128)
        key = two_heads(proj_ref[:, pl.ds(low + D, 128)] * 0.125)
        scores = nn(key, query_ref[pl.ds(low, 128)])
        for side in range(2):
            part = scores[TOK * side : TOK * side + TOK] - total_ref[pl.ds(2 * pair + side, 1)]
            probs = jnp.exp(jnp.where(ok, part, -1e30))
            prob_ref[pair, TOK * side : TOK * side + TOK] = probs.astype(BF16)
        return carry

    lax.fori_loop(0, PAIRS, one_pair, 0)


def two_sums(grad, mixed):
    prod = grad.astype(F32) * mixed.astype(F32)
    lane = lax.broadcasted_iota(jnp.int32, prod.shape, 1)
    return jnp.concatenate(
        [
            jnp.sum(jnp.where(lane < 64, prod, 0.0), axis=-1, keepdims=True),
            jnp.sum(jnp.where(lane < 64, 0.0, prod), axis=-1, keepdims=True),
        ],
        axis=0,
    )


def query_kernel(
    where_ref, g_ref, w_ref, mixed_ref, kv_ref, prob_ref, *rest, turn
):
    (dq_ref, dm_ref), prev = rest[-2:], rest[:-2]
    for ref in prev:

        @pl.when(where_ref[5] != turn)
        def _():
            dq_ref[...] = ref[:, :D]

    @pl.when(where_ref[5] == turn)
    def _():
        dm_ref[...] = nt(g_ref[...], w_ref[...]).astype(BF16)

        def one_pair(pair, carry):
            low = pl.multiple_of(128 * pair, 128)
            at = pl.ds(low, 128)
            grad = dm_ref[:, at]
            delta = two_sums(grad, mixed_ref[:, at])
            pressure = nt(two_heads(grad), kv_ref[:, pl.ds(low + D, 128)])
            slopes = (prob_ref[pair].astype(F32) * (pressure - delta)).astype(BF16)
            dq_ref[:, at] = (one_block(nn(slopes, kv_ref[:, at])) * 0.125).astype(BF16)
            return carry

        lax.fori_loop(0, PAIRS, one_pair, 0)


def turned_block(stacked):
    row = lax.broadcasted_iota(jnp.int32, (128, 128), 0)
    return jnp.where(row < 64, stacked[:, :128], stacked[:, 128:]).T


def key_kernel(
    where_ref, g0, g1, g2, wo_ref, delta_ref, proj_ref, query_ref, prob_ref, *rest, turn, last
):
    ins, rest = ((), rest) if last else (rest[:4], rest[4:])
    count = 1 if last else 3
    prev, rest = (rest[:count], rest[count:]) if turn else ((), rest)
    outs, sends, dm_ref = rest[:count], rest[count:-1], rest[-1]
    kv_ref = outs[0] if last else outs[0].at[:, D:]
    active = where_ref[5] == turn

    if prev:

        @pl.when(jnp.logical_not(active))
        def _():
            for new, old in zip(outs, prev):
                new[...] = old[:, D:] if last else old[...]

    @pl.when(active)
    def _():
        for piece, g in enumerate((g0, g1, g2)):
            d_mixed = nt(wo_ref[...], g[:OWN, :D]).astype(BF16)
            dm_ref[:, piece * OWN : (piece + 1) * OWN] = d_mixed
        for pair in range(PAIRS):
            at = slice(128 * pair, 128 * pair + 128)
            value = two_heads(proj_ref[:, 2 * D + 128 * pair : 2 * D + 128 * pair + 128])
            grad = dm_ref[at]
            if turn:
                prod = grad.astype(F32) * delta_ref[at].astype(F32)
                deltas = [jnp.sum(prod[r : r + 64], axis=0, keepdims=True) for r in (0, 64)]
            else:
                deltas = [delta_ref[2 * pair + side : 2 * pair + side + 1] for side in range(2)]
            pressure = nn(value, grad)
            probs = prob_ref[pair]
            d_value = nt(grad, probs)
            slopes = []
            for side in range(2):
                rows = slice(TOK * side, TOK * side + TOK)
                slopes.append(
                    (probs[rows].astype(F32) * (pressure[rows] - deltas[side])).astype(BF16)
                )
            d_key = nt(query_ref[at], jnp.concatenate(slopes, axis=0))
            kv_ref[:, at] = (turned_block(d_key) * 0.125).astype(BF16)
            kv_ref[:, D + 128 * pair : D + 128 * pair + 128] = turned_block(d_value).astype(BF16)
        if not last:
            dq_ref, *ins_rest = ins
            outs[0][:, :D] = dq_ref[...]
            outs[1][:TOK] = g0[:TOK, :D]
            outs[1][TOK:] = g1[:TOK, :D]
            out = input_grad(nt(outs[0][...], ins_rest[1][...]), ins_rest[0], ins_rest[2])
            outs[2][...] = out
            low_ref, left_ref, right_ref = sends
            low_ref[...] = out.astype(BF16)
            put_sides(out, left_ref, right_ref)


def input_grad(d_normed, g_ref, x_ref):
    x = x_ref[...].astype(F32)
    inverse = lax.rsqrt(jnp.mean(x * x, axis=-1, keepdims=True) + 1e-06)
    normed = x * inverse
    inner = jnp.mean(d_normed * normed, axis=-1, keepdims=True)
    return g_ref[...].astype(F32) + inverse * (d_normed - normed * inner)


def input_kernel(where_ref, dq_ref, kv_ref, g_ref, wq_ref, x_ref, prev_ref, in_ref, *, turn):
    @pl.when(where_ref[5] == turn)
    def _():
        d_normed = nt(dq_ref[...], wq_ref[:, :D]) + nt(kv_ref[...], wq_ref[:, D:])
        in_ref[...] = input_grad(d_normed, g_ref, x_ref)

    @pl.when(where_ref[5] != turn)
    def _():
        in_ref[...] = prev_ref[...]


def split_rows(where_ref, parts, outs):
    cols = len(outs)
    for distance, out_ref in enumerate(outs):
        col = lax.rem(where_ref[6] + distance, cols)
        for at, ref, step, first in parts:
            rows = [
                ref[pl.ds(pl.multiple_of(step * chip + first + 8 * col, 8), 8)]
                for chip in range(out_ref.shape[0] // 8)
            ]
            out_ref[:, at] = jnp.concatenate(rows, axis=0).astype(BF16)


def early_kernel(where_ref, nt_ref, dq_ref, mixed_ref, g0, m, prev_ref, *refs, turn):
    outs, (left_ref, full_ref, g_ref) = refs[:-3], refs[-3:]

    @pl.when(where_ref[5] == turn)
    def _():
        g_ref[:TOK] = g0[:TOK]
        g_ref[TOK:] = m[:TOK]

    @pl.when(where_ref[5] != turn)
    def _():
        g_ref[...] = prev_ref[...]

    d_query = jnp.concatenate([dq_ref[...], m[OWN : OWN + TOK]], axis=0)
    left_ref[...] = nn(nt_ref[...], d_query)
    mixed = jnp.concatenate([mixed_ref[...], m[OWN + TOK :]], axis=0)
    full_ref[...] = tn(mixed, g_ref[...])
    split_rows(
        where_ref,
        [(slice(0, D), left_ref, BLOCK, 0), (slice(D, 2 * D), full_ref, 2 * BLOCK, where_ref[2] * BLOCK)],
        outs,
    )


def late_kernel(where_ref, nt_ref, d0, d1, *refs):
    outs, left_ref = refs[:-1], refs[-1]
    left_ref[...] = nn(nt_ref[...], jnp.concatenate([d0[...], d1[...]], axis=0))
    split_rows(where_ref, [(slice(0, 2 * D), left_ref, BLOCK, 0)], outs)


def col_total_kernel(where_ref, *refs):
    count = (len(refs) - 1) // 2
    for at, parts in ((slice(0, 2 * D), refs[:count]), (slice(2 * D, 4 * D), refs[count:-1])):
        total = parts[0][...].astype(F32)
        for ref in parts[1:]:
            total = total + ref[...].astype(F32)
        refs[-1][:, at] = total.astype(BF16)


def total_kernel(where_ref, part_ref, qkv_ref, out_ref, *, scale):
    total = part_ref[0].astype(F32)
    for source in range(1, part_ref.shape[0]):
        total = total + part_ref[source].astype(F32)
    qkv_ref[:, :D] = total[:, :D] * scale
    qkv_ref[:, D:] = total[:, 2 * D :] * scale
    out_ref[...] = total[:, D : 2 * D] * scale


def call(kernel, outs, *args, scratch=(), flops=0, moved=4 << 20):
    vmem = pl.BlockSpec(memory_space=pltpu.VMEM)
    return pl.pallas_call(
        kernel,
        out_shape=[jax.ShapeDtypeStruct(s, t) for s, t in outs],
        in_specs=[pl.BlockSpec(memory_space=pltpu.SMEM)] + [vmem] * (len(args) - 1),
        out_specs=[vmem] * len(outs),
        scratch_shapes=list(scratch),
        compiler_params=pltpu.CompilerParams(vmem_limit_bytes=VMEM_LIMIT),
        cost_estimate=pl.CostEstimate(flops=flops, bytes_accessed=moved, transcendentals=0),
    )(*args)


def body(sizes, activations, qkv_weight, out_weight, cotangent):
    pipes, chips, cols = sizes

    def routed(block, step, plane=None):
        pairs = []
        for p in range(pipes) if plane is None else (plane,):
            for r in range(2 * chips):
                for c in range(cols):
                    p2, r2, c2 = step(p, r, c)
                    target = ((p2 % pipes) * 2 * chips + r2 % (2 * chips)) * cols + c2 % cols
                    pairs.append(((p * 2 * chips + r) * cols + c, target))
        return lax.ppermute(block, AXES, pairs)

    def col_rims(left_half, right_half, down=0):
        left = routed(right_half, lambda p, r, c: (p - down, r, c + 1))
        right = routed(left_half, lambda p, r, c: (p - down, r, c - 1))
        return left, right

    def mate(p, r, c):
        return p, r ^ 1, c

    def row_rims(pieces, plane=None, extra=()):
        own = jnp.concatenate(pieces, axis=0)
        beyond = routed(own, lambda p, r, c: (p, r - 1 + 2 * (r & 1), c), plane)
        if extra:
            return own, routed(jnp.concatenate([*pieces, *extra], axis=0), mate), beyond
        return own, routed(own, mate, plane), beyond

    pipe, z, core, col = (lax.axis_index(axis) for axis in AXES)
    x = activations.reshape(TOK, D)
    w_qkv, w_out = qkv_weight[0], out_weight[0]
    cot = cotangent.reshape(TOK, D)
    row_total, col_total = 16 * chips, 16 * cols
    where = jnp.stack(
        [8 * (2 * z + core), 16 * col, core, row_total, col_total, pipes - 1 - pipe, col]
    ).astype(jnp.int32)

    x_sides = x.reshape(8, 2, 8, D)
    low_side, high_side = x_sides[:, 0].reshape(64, D), x_sides[:, 1].reshape(64, D)
    base, proj, nlow = call(
        centre_kernel, [((OWN, D), BF16), ((TOK, 3 * D), BF16), ((TOK, D), BF16)],
        where, x, w_qkv, flops=1 << 28,
    )
    left, right = col_rims(low_side, high_side)
    own = lax.dynamic_update_slice(base, left, (TOK, 0))
    own, near, far = row_rims([lax.dynamic_update_slice(own, right, (TOK + 64, 0))])
    side_proj, cot_low, d_mixed = call(
        side_kernel, [((TOK, 3 * D), BF16), ((TOK, D), BF16), ((TOK, D), BF16)],
        where, left, right, w_qkv, w_out, cot, flops=1 << 28,
    )
    wide = D + 128
    kv, q_probs, nlow_mate, low_far, mixed, pack, low_side, high_side = call(
        forward_kernel,
        [((REGION, 2 * D), BF16), ((PAIRS, OWN, REGION), BF16), ((TOK, D), BF16),
         ((2 * OWN, D), BF16), ((TOK, D), BF16), ((TOK, wide), BF16), ((64, wide), BF16),
         ((64, wide), BF16)],
        where, near, far, proj, side_proj, w_qkv, cot_low, d_mixed, flops=2 << 30,
    )
    sides = col_rims(low_side, high_side)
    queries, n_turned = call(
        turned_kernel, [((D, REGION), BF16), ((OWN, OWN), BF16)],
        where, proj, side_proj, low_far, w_qkv, nlow, nlow_mate,
        scratch=[pltpu.VMEM((D, OWN), F32)], flops=1 << 28,
    )

    def query_side(turn, gradient, *prev):
        return call(
            functools.partial(query_kernel, turn=turn), [((TOK, D), BF16)],
            where, gradient, w_out, mixed, kv, q_probs, *prev,
            scratch=[pltpu.VMEM((TOK, D), BF16)], flops=1 << 29,
        )[0]

    d_query = query_side(0, cot_low)
    left, right = sides
    right, queries, d_query = lax.optimization_barrier((right, queries, d_query))
    packs = row_rims([pack, left, right])
    k_probs, mixed_turned, delta = call(
        key_probs_kernel,
        [((PAIRS, OWN, REGION), BF16), ((D, REGION), BF16), ((8, REGION), F32)],
        where, *packs, proj, queries, scratch=[pltpu.VMEM((8, REGION), F32)], flops=1 << 28,
    )
    gradient, gs = cot_low, packs
    def over_cols(parts):
        moved = list(parts)
        for distance in sorted(range(1, cols), key=lambda d: -min(d, cols - d)):
            moved[distance] = routed(parts[distance], lambda p, r, c: (p, r, c + distance))
        return moved

    state = ()
    for turn in range(pipes):
        plane, last = pipes - 1 - turn, turn == pipes - 1
        if turn > 0:
            low, low_side, high_side = sends
            gradient = routed(low, lambda p, r, c: (p - 1, r, c))
            left, right = col_rims(low_side, high_side, 1)
            left, d_query = lax.optimization_barrier(
                (left, query_side(turn, gradient, *((state[0],) if last else ())))
            )
            gs = row_rims([gradient, left, right], plane, (d_query, mixed) if last else ())
        fixed = (w_out, mixed_turned if turn else delta, proj, queries, k_probs)
        scratch = [pltpu.VMEM((D, REGION), BF16)]
        if not last:
            outs = call(
                functools.partial(key_kernel, turn=turn, last=False),
                [((TOK, 3 * D), BF16), ((OWN, D), BF16), ((TOK, D), F32), ((TOK, D), BF16),
                 ((64, D), BF16), ((64, D), BF16)],
                where, *gs, *fixed, d_query, gradient if turn else cot, w_qkv, x, *state,
                scratch=scratch, flops=1 << 30,
            )
            state, sends = outs[:3], outs[3:]
    d_proj, g_low, d_in = state
    early = call(
        functools.partial(early_kernel, turn=turn), [((8 * chips, 2 * D), BF16)] * cols,
        where, n_turned, d_query, mixed, gs[0], gs[1], g_low,
        scratch=[pltpu.VMEM((OWN, D), F32), pltpu.VMEM((D, D), F32), pltpu.VMEM((OWN, D), BF16)],
        flops=1 << 28,
    )
    _, beyond = lax.optimization_barrier((early[0], gs[2]))
    early, gs = over_cols(early), (*gs[:2], beyond)
    (d_kv,) = call(
        functools.partial(key_kernel, turn=turn, last=True), [((TOK, 2 * D), BF16)],
        where, *gs, *fixed, d_proj, scratch=scratch, flops=1 << 30,
    )
    late = call(
        late_kernel, [((8 * chips, 2 * D), BF16)] * cols, where, n_turned, d_kv, routed(d_kv, mate),
        scratch=[pltpu.VMEM((OWN, 2 * D), F32)], flops=1 << 29,
    )
    late = list(late)
    late[1], early[2] = lax.optimization_barrier((late[1], early[2]))
    late = over_cols(late)
    (d_in,) = call(
        functools.partial(input_kernel, turn=turn), [((TOK, D), F32)],
        where, d_query, d_kv, gradient, w_qkv, x, d_in, flops=1 << 28,
    )
    late[-1], d_in = lax.optimization_barrier((late[-1], d_in))
    (part,) = call(col_total_kernel, [((8 * chips, 4 * D), BF16)], where, *early, *late)
    part = part.reshape(chips, 8, 4 * D)
    part = lax.all_to_all(part, "z", 0, 0, tiled=True)
    qkv_part, out_part = call(
        functools.partial(total_kernel, scale=(row_total * col_total) ** (-0.5)),
        [((8, 3 * D), F32), ((8, D), F32)], where, part,
    )
    return d_in.reshape(1, 8, 16, D), qkv_part[None], out_part[None]


def solution(mesh):
    pipes, rows, cols = (mesh.shape[axis] for axis in ("pipe", "row", "col"))
    fine = Mesh(np.asarray(mesh.devices).reshape(pipes, rows // 2, 2, cols), AXES)
    row = ("z", "core")
    return jax.shard_map(
        functools.partial(body, (pipes, rows // 2, cols)),
        mesh=fine,
        in_specs=(
            P("pipe", row, "col", None),
            P("pipe", None, None),
            P("pipe", None, None),
            P(row, "col", None),
        ),
        out_specs=(
            P("pipe", row, "col", None),
            P("pipe", ("z", "core", "col"), None),
            P("pipe", ("z", "core", "col"), None),
        ),
        check_vma=False,
    )
```

```python
import functools

import jax
import jax.numpy as jnp
import numpy as np
from jax import lax
from jax.experimental import pallas as pl
from jax.experimental.pallas import tpu as pltpu
from jax.sharding import Mesh
from jax.sharding import PartitionSpec as P

F32 = jnp.float32
BF16 = jnp.bfloat16
AXES = ("pipe", "z", "core", "col")
D = 512
PAIRS = 4
TOK = 128
OWN = 256
REGION = 768
BLOCK = 32
VMEM_LIMIT = 40 * 1024 * 1024


def nn(a, b):
    return lax.dot_general(a, b, (((1,), (0,)), ((), ())), preferred_element_type=F32)


def nt(a, b):
    return lax.dot_general(a, b, (((1,), (1,)), ((), ())), preferred_element_type=F32)


def tn(a, b):
    return lax.dot_general(a, b, (((0,), (0,)), ((), ())), preferred_element_type=F32)


def two_heads(block):
    lane = lax.broadcasted_iota(jnp.int32, block.shape, 1)
    zero = jnp.zeros_like(block)
    return jnp.concatenate(
        [jnp.where(lane < 64, block, zero), jnp.where(lane < 64, zero, block)], axis=0
    )


def one_block(stacked):
    half = stacked.shape[0] // 2
    lane = lax.broadcasted_iota(jnp.int32, (half, 128), 1)
    return jnp.where(lane < 64, stacked[:half], stacked[half:])


def place(index, core):
    piece = index >> 8
    inner = index & 255
    side = inner - 128
    is_centre = inner < 128
    row = jnp.where(is_centre, inner >> 4, (side & 63) >> 3)
    col = jnp.where(is_centre, inner & 15, jnp.where(side < 64, (side & 7) - 8, (side & 7) + 16))
    mate = jnp.where(core == 0, 8, -8)
    row = row + jnp.where(piece == 1, mate, jnp.where(piece == 2, -mate, 0))
    return row, col


def window(where_ref, keys_own):
    row0, col0, core, rows, cols = (where_ref[i] for i in range(5))
    own = lax.broadcasted_iota(jnp.int32, (TOK, 1), 0)
    reach_row, reach_col = place(lax.broadcasted_iota(jnp.int32, (1, REGION), 1), core)
    grid_row, grid_col = row0 + reach_row, col0 + reach_col
    inside = (grid_row >= 0) & (grid_row < rows) & (grid_col >= 0) & (grid_col < cols)
    reach_row = jnp.where(inside, reach_row, 1 << 20)
    if keys_own:
        step_row, step_col = (own >> 4) - reach_row, (own & 15) - reach_col
    else:
        step_row, step_col = reach_row - (own >> 4), reach_col - (own & 15)
    return (step_row >= -8) & (step_row <= 7) & (step_col >= -8) & (step_col <= 7)


def put_sides(block, left_ref, right_ref):
    sides = block.reshape(8, 2, 8, block.shape[-1])
    left_ref[...] = sides[:, 0].reshape(64, -1).astype(BF16)
    right_ref[...] = sides[:, 1].reshape(64, -1).astype(BF16)


def normed_low(x_ref):
    x = x_ref[...].astype(F32)
    inverse = lax.rsqrt(jnp.mean(x * x, axis=-1, keepdims=True) + 1e-06)
    return (x * inverse).astype(BF16)


def centre_kernel(where_ref, x_ref, w_ref, base_ref, proj_ref, nlow_ref):
    base_ref[:TOK] = x_ref[...]
    base_ref[TOK:] = jnp.zeros((TOK, D), BF16)
    low = normed_low(x_ref)
    nlow_ref[...] = low
    proj_ref[...] = nn(low, w_ref[...]).astype(BF16)


def side_kernel(
    where_ref, left_ref, right_ref, w_ref, wo_ref, cot_ref, proj_ref, cot_low_ref, dm_ref
):
    low = jnp.concatenate([normed_low(left_ref), normed_low(right_ref)], axis=0)
    proj_ref[...] = nn(low, w_ref[...]).astype(BF16)
    grad = cot_ref[...].astype(BF16)
    cot_low_ref[...] = grad
    dm_ref[...] = nt(grad, wo_ref[...]).astype(BF16)


def forward_kernel(
    where_ref, x1, x2, proj_ref, side_ref, w_ref, cot_ref, dm_ref,
    kv_ref, prob_ref, nlow_ref, far_ref, mixed_ref, pack_ref, left_ref, right_ref,
):
    kv_ref[:TOK] = proj_ref[:, D:]
    kv_ref[TOK:OWN] = side_ref[:, D:]
    for piece, x_ref in enumerate((x1, x2)):
        low = normed_low(x_ref)
        far_ref[piece * OWN : (piece + 1) * OWN] = low
        if piece == 0:
            nlow_ref[...] = low[:TOK]
        kv_ref[(piece + 1) * OWN : (piece + 2) * OWN] = nn(low, w_ref[:, D:]).astype(BF16)
    ok = window(where_ref, False)
    ok2 = jnp.concatenate([ok, ok], axis=0)
    lane = lax.broadcasted_iota(jnp.int32, (TOK, 128), 1)
    stats = jnp.zeros((TOK, 128), F32)
    for pair in range(PAIRS):
        at = slice(128 * pair, 128 * pair + 128)
        query = two_heads(proj_ref[:, at] * 0.125)
        scores = nt(query, kv_ref[:, at])
        scores = jnp.where(ok2, scores, -1e30)
        highest = jnp.max(scores, axis=-1, keepdims=True)
        grown = jnp.exp(scores - highest)
        total = jnp.sum(grown, axis=-1, keepdims=True)
        probs = (grown * (1.0 / total)).astype(BF16)
        prob_ref[pair] = probs
        value = kv_ref[:, D + 128 * pair : D + 128 * pair + 128]
        mixed = one_block(nn(probs, value)).astype(BF16)
        mixed_ref[:, at] = mixed
        log_total = highest + jnp.log(total)
        delta = two_sums(dm_ref[:, at], mixed)
        for first, rest in ((0, log_total), (24, delta)):
            for part in range(3):
                piece = rest.astype(BF16).astype(F32)
                rest = rest - piece
                for head in range(2):
                    chosen = lane == first + 8 * part + 2 * pair + head
                    stats = jnp.where(chosen, piece[TOK * head : TOK * head + TOK], stats)
    starts = where_ref[5] == 0
    pack_ref[:, D:] = stats.astype(BF16)

    @pl.when(starts)
    def _():
        pack_ref[:, :D] = cot_ref[...]

    @pl.when(jnp.logical_not(starts))
    def _():
        pack_ref[:, :D] = mixed_ref[...]

    put_sides(pack_ref[...].astype(F32), left_ref, right_ref)


def turned_kernel(where_ref, proj_ref, side_ref, far_ref, w_ref, n0, n1, query_ref, nt_ref, full_ref):
    query_ref[:, :TOK] = proj_ref[:, :D].astype(F32).T.astype(BF16)
    query_ref[:, TOK:OWN] = side_ref[:, :D].astype(F32).T.astype(BF16)
    far = nn(far_ref[...], w_ref[:, :D]).astype(BF16)
    query_ref[:, OWN:] = far.astype(F32).T.astype(BF16)
    full_ref[:, :TOK] = n0[...].astype(F32).T
    full_ref[:, TOK:] = n1[...].astype(F32).T
    nt_ref[...] = own_half(where_ref, full_ref).astype(BF16)


def own_half(where_ref, full_ref):
    rows = [
        full_ref[pl.ds(pl.multiple_of((2 * at + where_ref[2]) * BLOCK, BLOCK), BLOCK)]
        for at in range(full_ref.shape[0] // (2 * BLOCK))
    ]
    return jnp.concatenate(rows, axis=0)


def key_probs_kernel(
    where_ref, p0, p1, p2, proj_ref, query_ref, prob_ref, mixed_ref, delta_ref, total_ref
):
    head = lax.broadcasted_iota(jnp.int32, (8, 128), 0)
    lane = lax.broadcasted_iota(jnp.int32, (8, 128), 1)
    stats = jnp.concatenate([p[:, D:] for p in (p0, p1, p2)], axis=0)
    sums = []
    for first in (0, 24):
        chosen = ((lane & 7) == head) & (lane >= first) & (lane < first + 24)
        sums.append(nt(jnp.where(chosen, 1.0, 0.0).astype(BF16), stats))
    log_total, delta_ref[...] = sums

    @pl.when(where_ref[5] != 0)
    def _():
        for piece, p in enumerate((p0, p1, p2)):
            mixed_ref[:, piece * OWN : (piece + 1) * OWN] = p[:, :D].astype(F32).T.astype(BF16)

    total_ref[...] = log_total
    ok = window(where_ref, True)

    def one_pair(pair, carry):
        low = pl.multiple_of(128 * pair, 128)
        key = two_heads(proj_ref[:, pl.ds(low + D, 128)] * 0.125)
        scores = nn(key, query_ref[pl.ds(low, 128)])
        for side in range(2):
            part = scores[TOK * side : TOK * side + TOK] - total_ref[pl.ds(2 * pair + side, 1)]
            probs = jnp.exp(jnp.where(ok, part, -1e30))
            prob_ref[pair, TOK * side : TOK * side + TOK] = probs.astype(BF16)
        return carry

    lax.fori_loop(0, PAIRS, one_pair, 0)


def two_sums(grad, mixed):
    prod = grad.astype(F32) * mixed.astype(F32)
    lane = lax.broadcasted_iota(jnp.int32, prod.shape, 1)
    return jnp.concatenate(
        [
            jnp.sum(jnp.where(lane < 64, prod, 0.0), axis=-1, keepdims=True),
            jnp.sum(jnp.where(lane < 64, 0.0, prod), axis=-1, keepdims=True),
        ],
        axis=0,
    )


def query_kernel(
    where_ref, g_ref, w_ref, mixed_ref, kv_ref, prob_ref, *rest, turn
):
    (dq_ref, dm_ref), prev = rest[-2:], rest[:-2]
    for ref in prev:

        @pl.when(where_ref[5] != turn)
        def _():
            dq_ref[...] = ref[:, :D]

    @pl.when(where_ref[5] == turn)
    def _():
        dm_ref[...] = nt(g_ref[...], w_ref[...]).astype(BF16)

        def one_pair(pair, carry):
            low = pl.multiple_of(128 * pair, 128)
            at = pl.ds(low, 128)
            grad = dm_ref[:, at]
            delta = two_sums(grad, mixed_ref[:, at])
            pressure = nt(two_heads(grad), kv_ref[:, pl.ds(low + D, 128)])
            slopes = (prob_ref[pair].astype(F32) * (pressure - delta)).astype(BF16)
            dq_ref[:, at] = (one_block(nn(slopes, kv_ref[:, at])) * 0.125).astype(BF16)
            return carry

        lax.fori_loop(0, PAIRS, one_pair, 0)


def turned_block(stacked):
    row = lax.broadcasted_iota(jnp.int32, (128, 128), 0)
    return jnp.where(row < 64, stacked[:, :128], stacked[:, 128:]).T


def key_kernel(
    where_ref, g0, g1, g2, wo_ref, delta_ref, proj_ref, query_ref, prob_ref, *rest, turn, last
):
    ins, rest = ((), rest) if last else (rest[:4], rest[4:])
    count = 1 if last else 3
    prev, rest = (rest[:count], rest[count:]) if turn else ((), rest)
    outs, sends, dm_ref = rest[:count], rest[count:-1], rest[-1]
    kv_ref = outs[0] if last else outs[0].at[:, D:]
    active = where_ref[5] == turn

    if prev:

        @pl.when(jnp.logical_not(active))
        def _():
            for new, old in zip(outs, prev):
                new[...] = old[:, D:] if last else old[...]

    @pl.when(active)
    def _():
        for piece, g in enumerate((g0, g1, g2)):
            d_mixed = nt(wo_ref[...], g[:, :D]).astype(BF16)
            dm_ref[:, piece * OWN : (piece + 1) * OWN] = d_mixed

        def one_pair(pair, carry):
            low = pl.multiple_of(128 * pair, 128)
            at = pl.ds(low, 128)
            value = two_heads(proj_ref[:, pl.ds(low + 2 * D, 128)])
            grad = dm_ref[at]
            if turn:
                prod = grad.astype(F32) * delta_ref[at].astype(F32)
                deltas = [jnp.sum(prod[r : r + 64], axis=0, keepdims=True) for r in (0, 64)]
            else:
                deltas = [delta_ref[pl.ds(2 * pair + side, 1)] for side in range(2)]
            pressure = nn(value, grad)
            probs = prob_ref[pair]
            d_value = nt(grad, probs)
            slopes = []
            for side in range(2):
                rows = slice(TOK * side, TOK * side + TOK)
                slopes.append(
                    (probs[rows].astype(F32) * (pressure[rows] - deltas[side])).astype(BF16)
                )
            d_key = nt(query_ref[at], jnp.concatenate(slopes, axis=0))
            kv_ref[:, at] = (turned_block(d_key) * 0.125).astype(BF16)
            kv_ref[:, pl.ds(low + D, 128)] = turned_block(d_value).astype(BF16)
            return carry

        lax.fori_loop(0, PAIRS, one_pair, 0, unroll=2)
        if not last:
            dq_ref, *ins_rest = ins
            outs[0][:, :D] = dq_ref[...]
            outs[1][:TOK] = g0[:TOK, :D]
            outs[1][TOK:] = g1[:TOK, :D]
            out = input_grad(nt(outs[0][...], ins_rest[1][...]), ins_rest[0], ins_rest[2])
            outs[2][...] = out
            low_ref, left_ref, right_ref = sends
            low_ref[...] = out.astype(BF16)
            put_sides(out, left_ref, right_ref)


def input_grad(d_normed, g_ref, x_ref):
    x = x_ref[...].astype(F32)
    inverse = lax.rsqrt(jnp.mean(x * x, axis=-1, keepdims=True) + 1e-06)
    normed = x * inverse
    inner = jnp.mean(d_normed * normed, axis=-1, keepdims=True)
    return g_ref[...].astype(F32) + inverse * (d_normed - normed * inner)


def input_kernel(where_ref, dq_ref, kv_ref, g_ref, wq_ref, x_ref, prev_ref, in_ref, *, turn):
    @pl.when(where_ref[5] == turn)
    def _():
        d_normed = nt(dq_ref[...], wq_ref[:, :D]) + nt(kv_ref[...], wq_ref[:, D:])
        in_ref[...] = input_grad(d_normed, g_ref, x_ref)

    @pl.when(where_ref[5] != turn)
    def _():
        in_ref[...] = prev_ref[...]


def split_rows(where_ref, parts, outs):
    cols = len(outs)
    for distance, out_ref in enumerate(outs):
        col = lax.rem(where_ref[6] + distance, cols)
        for at, ref, step, first in parts:
            rows = [
                ref[pl.ds(pl.multiple_of(step * chip + first + 8 * col, 8), 8)]
                for chip in range(out_ref.shape[0] // 8)
            ]
            out_ref[:, at] = jnp.concatenate(rows, axis=0).astype(BF16)


def early_kernel(where_ref, nt_ref, dq_ref, mixed_ref, g0, g1, m, prev_ref, *refs, turn):
    outs, (left_ref, full_ref, g_ref) = refs[:-3], refs[-3:]

    @pl.when(where_ref[5] == turn)
    def _():
        g_ref[:TOK] = g0[:TOK]
        g_ref[TOK:] = g1[:TOK]

    @pl.when(where_ref[5] != turn)
    def _():
        g_ref[...] = prev_ref[...]

    d_query = jnp.concatenate([dq_ref[...], m[:TOK]], axis=0)
    left_ref[...] = nn(nt_ref[...], d_query)
    mixed = jnp.concatenate([mixed_ref[...], m[TOK:]], axis=0)
    full_ref[...] = tn(mixed, g_ref[...])
    split_rows(
        where_ref,
        [(slice(0, D), left_ref, BLOCK, 0), (slice(D, 2 * D), full_ref, 2 * BLOCK, where_ref[2] * BLOCK)],
        outs,
    )


def late_kernel(where_ref, nt_ref, d0, d1, *refs):
    outs, left_ref = refs[:-1], refs[-1]
    left_ref[...] = nn(nt_ref[...], jnp.concatenate([d0[...], d1[...]], axis=0))
    split_rows(where_ref, [(slice(0, 2 * D), left_ref, BLOCK, 0)], outs)


def col_total_kernel(where_ref, *refs):
    count = (len(refs) - 1) // 2
    for at, parts in ((slice(0, 2 * D), refs[:count]), (slice(2 * D, 4 * D), refs[count:-1])):
        total = parts[0][...].astype(F32)
        for ref in parts[1:]:
            total = total + ref[...].astype(F32)
        refs[-1][:, at] = total.astype(BF16)


def total_kernel(where_ref, part_ref, qkv_ref, out_ref, *, scale):
    total = part_ref[0].astype(F32)
    for source in range(1, part_ref.shape[0]):
        total = total + part_ref[source].astype(F32)
    qkv_ref[:, :D] = total[:, :D] * scale
    qkv_ref[:, D:] = total[:, 2 * D :] * scale
    out_ref[...] = total[:, D : 2 * D] * scale


def call(kernel, outs, *args, scratch=(), flops=0, moved=4 << 20):
    vmem = pl.BlockSpec(memory_space=pltpu.VMEM)
    return pl.pallas_call(
        kernel,
        out_shape=[jax.ShapeDtypeStruct(s, t) for s, t in outs],
        in_specs=[pl.BlockSpec(memory_space=pltpu.SMEM)] + [vmem] * (len(args) - 1),
        out_specs=[vmem] * len(outs),
        scratch_shapes=list(scratch),
        compiler_params=pltpu.CompilerParams(vmem_limit_bytes=VMEM_LIMIT),
        cost_estimate=pl.CostEstimate(flops=flops, bytes_accessed=moved, transcendentals=0),
    )(*args)


def body(sizes, activations, qkv_weight, out_weight, cotangent):
    pipes, chips, cols = sizes

    def routed(block, step):
        pairs = []
        for p in range(pipes):
            for r in range(2 * chips):
                for c in range(cols):
                    p2, r2, c2 = step(p, r, c)
                    target = ((p2 % pipes) * 2 * chips + r2 % (2 * chips)) * cols + c2 % cols
                    pairs.append(((p * 2 * chips + r) * cols + c, target))
        return lax.ppermute(block, AXES, pairs)

    def col_rims(left_half, right_half, down=0):
        left = routed(right_half, lambda p, r, c: (p - down, r, c + 1))
        right = routed(left_half, lambda p, r, c: (p - down, r, c - 1))
        return left, right

    def mate(p, r, c):
        return p, r ^ 1, c

    def row_rims(pieces):
        own = jnp.concatenate(pieces, axis=0)
        beyond = routed(own, lambda p, r, c: (p, r - 1 + 2 * (r & 1), c))
        return own, routed(own, mate), beyond

    pipe, z, core, col = (lax.axis_index(axis) for axis in AXES)
    x = activations.reshape(TOK, D)
    w_qkv, w_out = qkv_weight[0], out_weight[0]
    cot = cotangent.reshape(TOK, D)
    row_total, col_total = 16 * chips, 16 * cols
    where = jnp.stack(
        [8 * (2 * z + core), 16 * col, core, row_total, col_total, pipes - 1 - pipe, col]
    ).astype(jnp.int32)

    x_sides = x.reshape(8, 2, 8, D)
    low_side, high_side = x_sides[:, 0].reshape(64, D), x_sides[:, 1].reshape(64, D)
    base, proj, nlow = call(
        centre_kernel, [((OWN, D), BF16), ((TOK, 3 * D), BF16), ((TOK, D), BF16)],
        where, x, w_qkv, flops=1 << 28,
    )
    left, right = col_rims(low_side, high_side)
    own = lax.dynamic_update_slice(base, left, (TOK, 0))
    own, near, far = row_rims([lax.dynamic_update_slice(own, right, (TOK + 64, 0))])
    side_proj, cot_low, d_mixed = call(
        side_kernel, [((TOK, 3 * D), BF16), ((TOK, D), BF16), ((TOK, D), BF16)],
        where, left, right, w_qkv, w_out, cot, flops=1 << 28,
    )
    wide = D + 128
    kv, q_probs, nlow_mate, low_far, mixed, pack, low_side, high_side = call(
        forward_kernel,
        [((REGION, 2 * D), BF16), ((PAIRS, OWN, REGION), BF16), ((TOK, D), BF16),
         ((2 * OWN, D), BF16), ((TOK, D), BF16), ((TOK, wide), BF16), ((64, wide), BF16),
         ((64, wide), BF16)],
        where, near, far, proj, side_proj, w_qkv, cot_low, d_mixed, flops=2 << 30,
    )
    sides = col_rims(low_side, high_side)
    queries, n_turned = call(
        turned_kernel, [((D, REGION), BF16), ((OWN, OWN), BF16)],
        where, proj, side_proj, low_far, w_qkv, nlow, nlow_mate,
        scratch=[pltpu.VMEM((D, OWN), F32)], flops=1 << 28,
    )

    def query_side(turn, gradient, *prev):
        return call(
            functools.partial(query_kernel, turn=turn), [((TOK, D), BF16)],
            where, gradient, w_out, mixed, kv, q_probs, *prev,
            scratch=[pltpu.VMEM((TOK, D), BF16)], flops=1 << 29,
        )[0]

    d_query = query_side(0, cot_low)
    left, right = sides
    right, queries, d_query = lax.optimization_barrier((right, queries, d_query))
    packs = row_rims([pack, left, right])
    k_probs, mixed_turned, delta = call(
        key_probs_kernel,
        [((PAIRS, OWN, REGION), BF16), ((D, REGION), BF16), ((8, REGION), F32)],
        where, *packs, proj, queries, scratch=[pltpu.VMEM((8, REGION), F32)], flops=1 << 28,
    )
    gradient, gs = cot_low, packs
    def over_cols(parts):
        moved = list(parts)
        for distance in sorted(range(1, cols), key=lambda d: -min(d, cols - d)):
            moved[distance] = routed(parts[distance], lambda p, r, c: (p, r, c + distance))
        return moved

    state = ()
    for turn in range(pipes):
        last = turn == pipes - 1
        if turn > 0:
            low, low_side, high_side = sends
            gradient = routed(low, lambda p, r, c: (p - 1, r, c))
            left, right = col_rims(low_side, high_side, 1)
            left, d_query = lax.optimization_barrier(
                (left, query_side(turn, gradient, *((state[0],) if last else ())))
            )
            gs = row_rims([gradient, left, right])
        fixed = (w_out, mixed_turned if turn else delta, proj, queries, k_probs)
        scratch = [pltpu.VMEM((D, REGION), BF16)]
        if not last:
            outs = call(
                functools.partial(key_kernel, turn=turn, last=False),
                [((TOK, 3 * D), BF16), ((OWN, D), BF16), ((TOK, D), F32), ((TOK, D), BF16),
                 ((64, D), BF16), ((64, D), BF16)],
                where, *gs, *fixed, d_query, gradient if turn else cot, w_qkv, x, *state,
                scratch=scratch, flops=1 << 30,
            )
            state, sends = outs[:3], outs[3:]
    d_proj, g_low, d_in = state
    extra, beyond = lax.optimization_barrier(
        (jnp.concatenate([d_query, mixed], axis=0), gs[2])
    )
    gs = (*gs[:2], beyond)
    early = call(
        functools.partial(early_kernel, turn=turn), [((8 * chips, 2 * D), BF16)] * cols,
        where, n_turned, d_query, mixed, gs[0], gs[1], routed(extra, mate), g_low,
        scratch=[pltpu.VMEM((OWN, D), F32), pltpu.VMEM((D, D), F32), pltpu.VMEM((OWN, D), BF16)],
        flops=1 << 28,
    )
    (d_kv,) = call(
        functools.partial(key_kernel, turn=turn, last=True), [((TOK, 2 * D), BF16)],
        where, *gs, *fixed, d_proj, scratch=scratch, flops=1 << 30,
    )
    early = list(early)
    early[0], d_kv_mate = lax.optimization_barrier((early[0], routed(d_kv, mate)))
    early = over_cols(early)
    late = list(call(
        late_kernel, [((8 * chips, 2 * D), BF16)] * cols, where, n_turned, d_kv, d_kv_mate,
        scratch=[pltpu.VMEM((OWN, 2 * D), F32)], flops=1 << 29,
    ))
    late[1], early[2] = lax.optimization_barrier((late[1], early[2]))
    late = over_cols(late)
    (d_in,) = call(
        functools.partial(input_kernel, turn=turn), [((TOK, D), F32)],
        where, d_query, d_kv, gradient, w_qkv, x, d_in, flops=1 << 28,
    )
    late[-1], d_in = lax.optimization_barrier((late[-1], d_in))
    (part,) = call(col_total_kernel, [((8 * chips, 4 * D), BF16)], where, *early, *late)
    part = part.reshape(chips, 8, 4 * D)
    part = lax.all_to_all(part, "z", 0, 0, tiled=True)
    qkv_part, out_part = call(
        functools.partial(total_kernel, scale=(row_total * col_total) ** (-0.5)),
        [((8, 3 * D), F32), ((8, D), F32)], where, part,
    )
    return d_in.reshape(1, 8, 16, D), qkv_part[None], out_part[None]


def solution(mesh):
    pipes, rows, cols = (mesh.shape[axis] for axis in ("pipe", "row", "col"))
    fine = Mesh(np.asarray(mesh.devices).reshape(pipes, rows // 2, 2, cols), AXES)
    row = ("z", "core")
    return jax.shard_map(
        functools.partial(body, (pipes, rows // 2, cols)),
        mesh=fine,
        in_specs=(
            P("pipe", row, "col", None),
            P("pipe", None, None),
            P("pipe", None, None),
            P(row, "col", None),
        ),
        out_specs=(
            P("pipe", row, "col", None),
            P("pipe", ("z", "core", "col"), None),
            P("pipe", ("z", "core", "col"), None),
        ),
        check_vma=False,
    )
```

```python
import functools

import jax
import jax.numpy as jnp
import numpy as np
from jax import lax
from jax.experimental import pallas as pl
from jax.experimental.pallas import tpu as pltpu
from jax.sharding import Mesh
from jax.sharding import PartitionSpec as P

F32 = jnp.float32
BF16 = jnp.bfloat16
AXES = ("pipe", "z", "core", "col")
D = 512
PAIRS = 4
TOK = 128
OWN = 256
REGION = 768
BLOCK = 32
VMEM_LIMIT = 40 * 1024 * 1024


def nn(a, b):
    return lax.dot_general(a, b, (((1,), (0,)), ((), ())), preferred_element_type=F32)


def nt(a, b):
    return lax.dot_general(a, b, (((1,), (1,)), ((), ())), preferred_element_type=F32)


def tn(a, b):
    return lax.dot_general(a, b, (((0,), (0,)), ((), ())), preferred_element_type=F32)


def two_heads(block):
    lane = lax.broadcasted_iota(jnp.int32, block.shape, 1)
    zero = jnp.zeros_like(block)
    return jnp.concatenate(
        [jnp.where(lane < 64, block, zero), jnp.where(lane < 64, zero, block)], axis=0
    )


def one_block(stacked):
    half = stacked.shape[0] // 2
    lane = lax.broadcasted_iota(jnp.int32, (half, 128), 1)
    return jnp.where(lane < 64, stacked[:half], stacked[half:])


def place(index, core):
    piece = index >> 8
    inner = index & 255
    side = inner - 128
    is_centre = inner < 128
    row = jnp.where(is_centre, inner >> 4, (side & 63) >> 3)
    col = jnp.where(is_centre, inner & 15, jnp.where(side < 64, (side & 7) - 8, (side & 7) + 16))
    mate = jnp.where(core == 0, 8, -8)
    row = row + jnp.where(piece == 1, mate, jnp.where(piece == 2, -mate, 0))
    return row, col


def window(where_ref, keys_own):
    row0, col0, core, rows, cols = (where_ref[i] for i in range(5))
    own = lax.broadcasted_iota(jnp.int32, (TOK, 1), 0)
    reach_row, reach_col = place(lax.broadcasted_iota(jnp.int32, (1, REGION), 1), core)
    grid_row, grid_col = row0 + reach_row, col0 + reach_col
    inside = (grid_row >= 0) & (grid_row < rows) & (grid_col >= 0) & (grid_col < cols)
    reach_row = jnp.where(inside, reach_row, 1 << 20)
    if keys_own:
        step_row, step_col = (own >> 4) - reach_row, (own & 15) - reach_col
    else:
        step_row, step_col = reach_row - (own >> 4), reach_col - (own & 15)
    return (step_row >= -8) & (step_row <= 7) & (step_col >= -8) & (step_col <= 7)


def put_sides(block, left_ref, right_ref):
    sides = block.reshape(8, 2, 8, block.shape[-1])
    left_ref[...] = sides[:, 0].reshape(64, -1).astype(BF16)
    right_ref[...] = sides[:, 1].reshape(64, -1).astype(BF16)


def normed_low(x_ref):
    x = x_ref[...].astype(F32)
    inverse = lax.rsqrt(jnp.mean(x * x, axis=-1, keepdims=True) + 1e-06)
    return (x * inverse).astype(BF16)


def centre_kernel(where_ref, x_ref, w_ref, base_ref, proj_ref, nlow_ref):
    base_ref[:TOK] = x_ref[...]
    base_ref[TOK:] = jnp.zeros((TOK, D), BF16)
    low = normed_low(x_ref)
    nlow_ref[...] = low
    proj_ref[...] = nn(low, w_ref[...]).astype(BF16)


def side_kernel(
    where_ref, left_ref, right_ref, w_ref, wo_ref, cot_ref, proj_ref, cot_low_ref, dm_ref
):
    low = jnp.concatenate([normed_low(left_ref), normed_low(right_ref)], axis=0)
    proj_ref[...] = nn(low, w_ref[...]).astype(BF16)
    grad = cot_ref[...].astype(BF16)
    cot_low_ref[...] = grad
    dm_ref[...] = nt(grad, wo_ref[...]).astype(BF16)


def forward_kernel(
    where_ref, x1, x2, proj_ref, side_ref, w_ref, cot_ref, dm_ref,
    kv_ref, prob_ref, nlow_ref, far_ref, mixed_ref, pack_ref, left_ref, right_ref,
):
    kv_ref[:TOK] = proj_ref[:, D:]
    kv_ref[TOK:OWN] = side_ref[:, D:]
    for piece, x_ref in enumerate((x1, x2)):
        low = normed_low(x_ref)
        far_ref[piece * OWN : (piece + 1) * OWN] = low
        if piece == 0:
            nlow_ref[...] = low[:TOK]
        kv_ref[(piece + 1) * OWN : (piece + 2) * OWN] = nn(low, w_ref[:, D:]).astype(BF16)
    ok = window(where_ref, False)
    ok2 = jnp.concatenate([ok, ok], axis=0)
    lane = lax.broadcasted_iota(jnp.int32, (TOK, 128), 1)
    stats = jnp.zeros((TOK, 128), F32)
    for pair in range(PAIRS):
        at = slice(128 * pair, 128 * pair + 128)
        query = two_heads(proj_ref[:, at] * 0.125)
        scores = nt(query, kv_ref[:, at])
        scores = jnp.where(ok2, scores, -1e30)
        highest = jnp.max(scores, axis=-1, keepdims=True)
        grown = jnp.exp(scores - highest)
        total = jnp.sum(grown, axis=-1, keepdims=True)
        probs = (grown * (1.0 / total)).astype(BF16)
        prob_ref[pair] = probs
        value = kv_ref[:, D + 128 * pair : D + 128 * pair + 128]
        mixed = one_block(nn(probs, value)).astype(BF16)
        mixed_ref[:, at] = mixed
        log_total = highest + jnp.log(total)
        delta = two_sums(dm_ref[:, at], mixed)
        for first, rest in ((0, log_total), (24, delta)):
            for part in range(3):
                piece = rest.astype(BF16).astype(F32)
                rest = rest - piece
                for head in range(2):
                    chosen = lane == first + 8 * part + 2 * pair + head
                    stats = jnp.where(chosen, piece[TOK * head : TOK * head + TOK], stats)
    starts = where_ref[5] == 0
    pack_ref[:, D:] = stats.astype(BF16)

    @pl.when(starts)
    def _():
        pack_ref[:, :D] = cot_ref[...]

    @pl.when(jnp.logical_not(starts))
    def _():
        pack_ref[:, :D] = mixed_ref[...]

    put_sides(pack_ref[...].astype(F32), left_ref, right_ref)


def turned_kernel(where_ref, proj_ref, side_ref, far_ref, w_ref, n0, n1, query_ref, nt_ref, full_ref):
    query_ref[:, :TOK] = proj_ref[:, :D].astype(F32).T.astype(BF16)
    query_ref[:, TOK:OWN] = side_ref[:, :D].astype(F32).T.astype(BF16)
    far = nn(far_ref[...], w_ref[:, :D]).astype(BF16)
    query_ref[:, OWN:] = far.astype(F32).T.astype(BF16)
    full_ref[:, :TOK] = n0[...].astype(F32).T
    full_ref[:, TOK:] = n1[...].astype(F32).T
    nt_ref[...] = own_half(where_ref, full_ref).astype(BF16)


def own_half(where_ref, full_ref):
    rows = [
        full_ref[pl.ds(pl.multiple_of((2 * at + where_ref[2]) * BLOCK, BLOCK), BLOCK)]
        for at in range(full_ref.shape[0] // (2 * BLOCK))
    ]
    return jnp.concatenate(rows, axis=0)


def key_probs_kernel(
    where_ref, p0, p1, p2, proj_ref, query_ref, prob_ref, mixed_ref, delta_ref, total_ref
):
    head = lax.broadcasted_iota(jnp.int32, (8, 128), 0)
    lane = lax.broadcasted_iota(jnp.int32, (8, 128), 1)
    stats = jnp.concatenate([p[:, D:] for p in (p0, p1, p2)], axis=0)
    sums = []
    for first in (0, 24):
        chosen = ((lane & 7) == head) & (lane >= first) & (lane < first + 24)
        sums.append(nt(jnp.where(chosen, 1.0, 0.0).astype(BF16), stats))
    log_total, delta_ref[...] = sums

    @pl.when(where_ref[5] != 0)
    def _():
        for piece, p in enumerate((p0, p1, p2)):
            mixed_ref[:, piece * OWN : (piece + 1) * OWN] = p[:, :D].astype(F32).T.astype(BF16)

    total_ref[...] = log_total
    ok = window(where_ref, True)

    def one_pair(pair, carry):
        low = pl.multiple_of(128 * pair, 128)
        key = two_heads(proj_ref[:, pl.ds(low + D, 128)] * 0.125)
        scores = nn(key, query_ref[pl.ds(low, 128)])
        for side in range(2):
            part = scores[TOK * side : TOK * side + TOK] - total_ref[pl.ds(2 * pair + side, 1)]
            probs = jnp.exp(jnp.where(ok, part, -1e30))
            prob_ref[pair, TOK * side : TOK * side + TOK] = probs.astype(BF16)
        return carry

    lax.fori_loop(0, PAIRS, one_pair, 0)


def two_sums(grad, mixed):
    prod = grad.astype(F32) * mixed.astype(F32)
    lane = lax.broadcasted_iota(jnp.int32, prod.shape, 1)
    return jnp.concatenate(
        [
            jnp.sum(jnp.where(lane < 64, prod, 0.0), axis=-1, keepdims=True),
            jnp.sum(jnp.where(lane < 64, 0.0, prod), axis=-1, keepdims=True),
        ],
        axis=0,
    )


def query_kernel(
    where_ref, g_ref, w_ref, mixed_ref, kv_ref, prob_ref, *rest, turn
):
    (dq_ref, dm_ref), prev = rest[-2:], rest[:-2]
    for ref in prev:

        @pl.when(where_ref[5] != turn)
        def _():
            dq_ref[...] = ref[:, :D]

    @pl.when(where_ref[5] == turn)
    def _():
        dm_ref[...] = nt(g_ref[...], w_ref[...]).astype(BF16)

        def one_pair(pair, carry):
            low = pl.multiple_of(128 * pair, 128)
            at = pl.ds(low, 128)
            grad = dm_ref[:, at]
            delta = two_sums(grad, mixed_ref[:, at])
            pressure = nt(two_heads(grad), kv_ref[:, pl.ds(low + D, 128)])
            slopes = (prob_ref[pair].astype(F32) * (pressure - delta)).astype(BF16)
            dq_ref[:, at] = (one_block(nn(slopes, kv_ref[:, at])) * 0.125).astype(BF16)
            return carry

        lax.fori_loop(0, PAIRS, one_pair, 0)


def turned_block(stacked):
    row = lax.broadcasted_iota(jnp.int32, (128, 128), 0)
    return jnp.where(row < 64, stacked[:, :128], stacked[:, 128:]).T


def key_kernel(
    where_ref, g0, g1, g2, wo_ref, delta_ref, proj_ref, query_ref, prob_ref, *rest, turn, last
):
    ins, rest = ((), rest) if last else (rest[:4], rest[4:])
    count = 1 if last else 3
    prev, rest = (rest[:count], rest[count:]) if turn else ((), rest)
    outs, sends, dm_ref = rest[:count], rest[count:-1], rest[-1]
    kv_ref = outs[0] if last else outs[0].at[:, D:]
    active = where_ref[5] == turn

    if prev:

        @pl.when(jnp.logical_not(active))
        def _():
            for new, old in zip(outs, prev):
                new[...] = old[:, D:] if last else old[...]

    @pl.when(active)
    def _():
        for piece, g in enumerate((g0, g1, g2)):
            d_mixed = nt(wo_ref[...], g[:, :D]).astype(BF16)
            dm_ref[:, piece * OWN : (piece + 1) * OWN] = d_mixed

        def one_pair(pair, carry):
            low = pl.multiple_of(128 * pair, 128)
            at = pl.ds(low, 128)
            value = two_heads(proj_ref[:, pl.ds(low + 2 * D, 128)])
            grad = dm_ref[at]
            if turn:
                prod = grad.astype(F32) * delta_ref[at].astype(F32)
                deltas = [jnp.sum(prod[r : r + 64], axis=0, keepdims=True) for r in (0, 64)]
            else:
                deltas = [delta_ref[pl.ds(2 * pair + side, 1)] for side in range(2)]
            pressure = nn(value, grad)
            probs = prob_ref[pair]
            d_value = nt(grad, probs)
            slopes = []
            for side in range(2):
                rows = slice(TOK * side, TOK * side + TOK)
                slopes.append(
                    (probs[rows].astype(F32) * (pressure[rows] - deltas[side])).astype(BF16)
                )
            d_key = nt(query_ref[at], jnp.concatenate(slopes, axis=0))
            kv_ref[:, at] = (turned_block(d_key) * 0.125).astype(BF16)
            kv_ref[:, pl.ds(low + D, 128)] = turned_block(d_value).astype(BF16)
            return carry

        lax.fori_loop(0, PAIRS, one_pair, 0, unroll=4 if last else 2)
        if not last:
            dq_ref, *ins_rest = ins
            outs[0][:, :D] = dq_ref[...]
            outs[1][:TOK] = g0[:TOK, :D]
            outs[1][TOK:] = g1[:TOK, :D]
            out = input_grad(nt(outs[0][...], ins_rest[1][...]), ins_rest[0], ins_rest[2])
            outs[2][...] = out
            low_ref, left_ref, right_ref = sends
            low_ref[...] = out.astype(BF16)
            put_sides(out, left_ref, right_ref)


def input_grad(d_normed, g_ref, x_ref):
    x = x_ref[...].astype(F32)
    inverse = lax.rsqrt(jnp.mean(x * x, axis=-1, keepdims=True) + 1e-06)
    normed = x * inverse
    inner = jnp.mean(d_normed * normed, axis=-1, keepdims=True)
    return g_ref[...].astype(F32) + inverse * (d_normed - normed * inner)


def input_kernel(where_ref, dq_ref, kv_ref, g_ref, wq_ref, x_ref, prev_ref, in_ref, *, turn):
    @pl.when(where_ref[5] == turn)
    def _():
        d_normed = nt(dq_ref[...], wq_ref[:, :D]) + nt(kv_ref[...], wq_ref[:, D:])
        in_ref[...] = input_grad(d_normed, g_ref, x_ref)

    @pl.when(where_ref[5] != turn)
    def _():
        in_ref[...] = prev_ref[...]


def split_rows(where_ref, parts, outs):
    cols = len(outs)
    for distance, out_ref in enumerate(outs):
        col = lax.rem(where_ref[6] + distance, cols)
        for at, ref, step, first in parts:
            rows = [
                ref[pl.ds(pl.multiple_of(step * chip + first + 8 * col, 8), 8)]
                for chip in range(out_ref.shape[0] // 8)
            ]
            out_ref[:, at] = jnp.concatenate(rows, axis=0).astype(BF16)


def early_kernel(where_ref, nt_ref, dq_ref, mixed_ref, g0, g1, m, prev_ref, *refs, turn):
    outs, (left_ref, full_ref, g_ref) = refs[:-3], refs[-3:]

    @pl.when(where_ref[5] == turn)
    def _():
        g_ref[:TOK] = g0[:TOK]
        g_ref[TOK:] = g1[:TOK]

    @pl.when(where_ref[5] != turn)
    def _():
        g_ref[...] = prev_ref[...]

    d_query = jnp.concatenate([dq_ref[...], m[:TOK]], axis=0)
    left_ref[...] = nn(nt_ref[...], d_query)
    mixed = jnp.concatenate([mixed_ref[...], m[TOK:]], axis=0)
    full_ref[...] = tn(mixed, g_ref[...])
    split_rows(
        where_ref,
        [(slice(0, D), left_ref, BLOCK, 0), (slice(D, 2 * D), full_ref, 2 * BLOCK, where_ref[2] * BLOCK)],
        outs,
    )


def late_kernel(where_ref, nt_ref, d0, d1, *refs):
    outs, left_ref = refs[:-1], refs[-1]
    left_ref[...] = nn(nt_ref[...], jnp.concatenate([d0[...], d1[...]], axis=0))
    split_rows(where_ref, [(slice(0, 2 * D), left_ref, BLOCK, 0)], outs)


def col_total_kernel(where_ref, *refs):
    count = (len(refs) - 1) // 2
    for at, parts in ((slice(0, 2 * D), refs[:count]), (slice(2 * D, 4 * D), refs[count:-1])):
        total = parts[0][...].astype(F32)
        for ref in parts[1:]:
            total = total + ref[...].astype(F32)
        refs[-1][:, at] = total.astype(BF16)


def total_kernel(where_ref, part_ref, qkv_ref, out_ref, *, scale):
    total = part_ref[0].astype(F32)
    for source in range(1, part_ref.shape[0]):
        total = total + part_ref[source].astype(F32)
    qkv_ref[:, :D] = total[:, :D] * scale
    qkv_ref[:, D:] = total[:, 2 * D :] * scale
    out_ref[...] = total[:, D : 2 * D] * scale


def call(kernel, outs, *args, scratch=(), flops=0, moved=4 << 20):
    vmem = pl.BlockSpec(memory_space=pltpu.VMEM)
    return pl.pallas_call(
        kernel,
        out_shape=[jax.ShapeDtypeStruct(s, t) for s, t in outs],
        in_specs=[pl.BlockSpec(memory_space=pltpu.SMEM)] + [vmem] * (len(args) - 1),
        out_specs=[vmem] * len(outs),
        scratch_shapes=list(scratch),
        compiler_params=pltpu.CompilerParams(vmem_limit_bytes=VMEM_LIMIT),
        cost_estimate=pl.CostEstimate(flops=flops, bytes_accessed=moved, transcendentals=0),
    )(*args)


def body(sizes, activations, qkv_weight, out_weight, cotangent):
    pipes, chips, cols = sizes

    def routed(block, step):
        pairs = []
        for p in range(pipes):
            for r in range(2 * chips):
                for c in range(cols):
                    p2, r2, c2 = step(p, r, c)
                    target = ((p2 % pipes) * 2 * chips + r2 % (2 * chips)) * cols + c2 % cols
                    pairs.append(((p * 2 * chips + r) * cols + c, target))
        return lax.ppermute(block, AXES, pairs)

    def col_rims(left_half, right_half, down=0):
        left = routed(right_half, lambda p, r, c: (p - down, r, c + 1))
        right = routed(left_half, lambda p, r, c: (p - down, r, c - 1))
        return left, right

    def mate(p, r, c):
        return p, r ^ 1, c

    def row_rims(pieces):
        own = jnp.concatenate(pieces, axis=0)
        beyond = routed(own, lambda p, r, c: (p, r - 1 + 2 * (r & 1), c))
        return own, routed(own, mate), beyond

    pipe, z, core, col = (lax.axis_index(axis) for axis in AXES)
    x = activations.reshape(TOK, D)
    w_qkv, w_out = qkv_weight[0], out_weight[0]
    cot = cotangent.reshape(TOK, D)
    row_total, col_total = 16 * chips, 16 * cols
    where = jnp.stack(
        [8 * (2 * z + core), 16 * col, core, row_total, col_total, pipes - 1 - pipe, col]
    ).astype(jnp.int32)

    x_sides = x.reshape(8, 2, 8, D)
    low_side, high_side = x_sides[:, 0].reshape(64, D), x_sides[:, 1].reshape(64, D)
    base, proj, nlow = call(
        centre_kernel, [((OWN, D), BF16), ((TOK, 3 * D), BF16), ((TOK, D), BF16)],
        where, x, w_qkv, flops=1 << 28,
    )
    left, right = col_rims(low_side, high_side)
    own = lax.dynamic_update_slice(base, left, (TOK, 0))
    own, near, far = row_rims([lax.dynamic_update_slice(own, right, (TOK + 64, 0))])
    side_proj, cot_low, d_mixed = call(
        side_kernel, [((TOK, 3 * D), BF16), ((TOK, D), BF16), ((TOK, D), BF16)],
        where, left, right, w_qkv, w_out, cot, flops=1 << 28,
    )
    wide = D + 128
    kv, q_probs, nlow_mate, low_far, mixed, pack, low_side, high_side = call(
        forward_kernel,
        [((REGION, 2 * D), BF16), ((PAIRS, OWN, REGION), BF16), ((TOK, D), BF16),
         ((2 * OWN, D), BF16), ((TOK, D), BF16), ((TOK, wide), BF16), ((64, wide), BF16),
         ((64, wide), BF16)],
        where, near, far, proj, side_proj, w_qkv, cot_low, d_mixed, flops=2 << 30,
    )
    sides = col_rims(low_side, high_side)
    queries, n_turned = call(
        turned_kernel, [((D, REGION), BF16), ((OWN, OWN), BF16)],
        where, proj, side_proj, low_far, w_qkv, nlow, nlow_mate,
        scratch=[pltpu.VMEM((D, OWN), F32)], flops=1 << 28,
    )

    def query_side(turn, gradient, *prev):
        return call(
            functools.partial(query_kernel, turn=turn), [((TOK, D), BF16)],
            where, gradient, w_out, mixed, kv, q_probs, *prev,
            scratch=[pltpu.VMEM((TOK, D), BF16)], flops=1 << 29,
        )[0]

    d_query = query_side(0, cot_low)
    left, right = sides
    right, queries, d_query = lax.optimization_barrier((right, queries, d_query))
    packs = row_rims([pack, left, right])
    k_probs, mixed_turned, delta = call(
        key_probs_kernel,
        [((PAIRS, OWN, REGION), BF16), ((D, REGION), BF16), ((8, REGION), F32)],
        where, *packs, proj, queries, scratch=[pltpu.VMEM((8, REGION), F32)], flops=1 << 28,
    )
    gradient, gs = cot_low, packs
    def over_cols(parts):
        moved = list(parts)
        for distance in sorted(range(1, cols), key=lambda d: -min(d, cols - d)):
            moved[distance] = routed(parts[distance], lambda p, r, c: (p, r, c + distance))
        return moved

    state = ()
    for turn in range(pipes):
        last = turn == pipes - 1
        if turn > 0:
            low, low_side, high_side = sends
            gradient = routed(low, lambda p, r, c: (p - 1, r, c))
            left, right = col_rims(low_side, high_side, 1)
            left, d_query = lax.optimization_barrier(
                (left, query_side(turn, gradient, *((state[0],) if last else ())))
            )
            gs = row_rims([gradient, left, right])
        fixed = (w_out, mixed_turned if turn else delta, proj, queries, k_probs)
        scratch = [pltpu.VMEM((D, REGION), BF16)]
        if not last:
            outs = call(
                functools.partial(key_kernel, turn=turn, last=False),
                [((TOK, 3 * D), BF16), ((OWN, D), BF16), ((TOK, D), F32), ((TOK, D), BF16),
                 ((64, D), BF16), ((64, D), BF16)],
                where, *gs, *fixed, d_query, gradient if turn else cot, w_qkv, x, *state,
                scratch=scratch, flops=1 << 30,
            )
            state, sends = outs[:3], outs[3:]
    d_proj, g_low, d_in = state
    extra = jnp.concatenate([d_query, mixed], axis=0)
    early = call(
        functools.partial(early_kernel, turn=turn), [((8 * chips, 2 * D), BF16)] * cols,
        where, n_turned, d_query, mixed, gs[0], gs[1], routed(extra, mate), g_low,
        scratch=[pltpu.VMEM((OWN, D), F32), pltpu.VMEM((D, D), F32), pltpu.VMEM((OWN, D), BF16)],
        flops=1 << 28,
    )
    (d_kv,) = call(
        functools.partial(key_kernel, turn=turn, last=True), [((TOK, 2 * D), BF16)],
        where, *gs, *fixed, d_proj, scratch=scratch, flops=1 << 30,
    )
    early = list(early)
    early[0], d_kv_mate = lax.optimization_barrier((early[0], routed(d_kv, mate)))
    early = over_cols(early)
    late = list(call(
        late_kernel, [((8 * chips, 2 * D), BF16)] * cols, where, n_turned, d_kv, d_kv_mate,
        scratch=[pltpu.VMEM((OWN, 2 * D), F32)], flops=1 << 29,
    ))
    late[1], early[2] = lax.optimization_barrier((late[1], early[2]))
    late = over_cols(late)
    (d_in,) = call(
        functools.partial(input_kernel, turn=turn), [((TOK, D), F32)],
        where, d_query, d_kv, gradient, w_qkv, x, d_in, flops=1 << 28,
    )
    late[-1], d_in = lax.optimization_barrier((late[-1], d_in))
    (part,) = call(col_total_kernel, [((8 * chips, 4 * D), BF16)], where, *early, *late)
    part = part.reshape(chips, 8, 4 * D)
    part = lax.all_to_all(part, "z", 0, 0, tiled=True)
    qkv_part, out_part = call(
        functools.partial(total_kernel, scale=(row_total * col_total) ** (-0.5)),
        [((8, 3 * D), F32), ((8, D), F32)], where, part,
    )
    return d_in.reshape(1, 8, 16, D), qkv_part[None], out_part[None]


def solution(mesh):
    pipes, rows, cols = (mesh.shape[axis] for axis in ("pipe", "row", "col"))
    fine = Mesh(np.asarray(mesh.devices).reshape(pipes, rows // 2, 2, cols), AXES)
    row = ("z", "core")
    return jax.shard_map(
        functools.partial(body, (pipes, rows // 2, cols)),
        mesh=fine,
        in_specs=(
            P("pipe", row, "col", None),
            P("pipe", None, None),
            P("pipe", None, None),
            P(row, "col", None),
        ),
        out_specs=(
            P("pipe", row, "col", None),
            P("pipe", ("z", "core", "col"), None),
            P("pipe", ("z", "core", "col"), None),
        ),
        check_vma=False,
    )
```

```python
import functools

import jax
import jax.numpy as jnp
import numpy as np
from jax import lax
from jax.experimental import pallas as pl
from jax.experimental.pallas import tpu as pltpu
from jax.sharding import Mesh
from jax.sharding import PartitionSpec as P

F32 = jnp.float32
BF16 = jnp.bfloat16
AXES = ("pipe", "z", "core", "col")
D = 512
PAIRS = 4
TOK = 128
OWN = 256
REGION = 768
BLOCK = 32
VMEM_LIMIT = 40 * 1024 * 1024


def nn(a, b):
    return lax.dot_general(a, b, (((1,), (0,)), ((), ())), preferred_element_type=F32)


def nt(a, b):
    return lax.dot_general(a, b, (((1,), (1,)), ((), ())), preferred_element_type=F32)


def tn(a, b):
    return lax.dot_general(a, b, (((0,), (0,)), ((), ())), preferred_element_type=F32)


def two_heads(block):
    lane = lax.broadcasted_iota(jnp.int32, block.shape, 1)
    zero = jnp.zeros_like(block)
    return jnp.concatenate(
        [jnp.where(lane < 64, block, zero), jnp.where(lane < 64, zero, block)], axis=0
    )


def one_block(stacked):
    half = stacked.shape[0] // 2
    lane = lax.broadcasted_iota(jnp.int32, (half, 128), 1)
    return jnp.where(lane < 64, stacked[:half], stacked[half:])


def place(index, core):
    piece = index >> 8
    inner = index & 255
    side = inner - 128
    is_centre = inner < 128
    row = jnp.where(is_centre, inner >> 4, (side & 63) >> 3)
    col = jnp.where(is_centre, inner & 15, jnp.where(side < 64, (side & 7) - 8, (side & 7) + 16))
    mate = jnp.where(core == 0, 8, -8)
    row = row + jnp.where(piece == 1, mate, jnp.where(piece == 2, -mate, 0))
    return row, col


def window(where_ref, keys_own):
    row0, col0, core, rows, cols = (where_ref[i] for i in range(5))
    own = lax.broadcasted_iota(jnp.int32, (TOK, 1), 0)
    reach_row, reach_col = place(lax.broadcasted_iota(jnp.int32, (1, REGION), 1), core)
    grid_row, grid_col = row0 + reach_row, col0 + reach_col
    inside = (grid_row >= 0) & (grid_row < rows) & (grid_col >= 0) & (grid_col < cols)
    reach_row = jnp.where(inside, reach_row, 1 << 20)
    if keys_own:
        step_row, step_col = (own >> 4) - reach_row, (own & 15) - reach_col
    else:
        step_row, step_col = reach_row - (own >> 4), reach_col - (own & 15)
    return (step_row >= -8) & (step_row <= 7) & (step_col >= -8) & (step_col <= 7)


def put_sides(block, left_ref, right_ref):
    sides = block.reshape(8, 2, 8, block.shape[-1])
    left_ref[...] = sides[:, 0].reshape(64, -1).astype(BF16)
    right_ref[...] = sides[:, 1].reshape(64, -1).astype(BF16)


def normed_low(x_ref):
    x = x_ref[...].astype(F32)
    inverse = lax.rsqrt(jnp.mean(x * x, axis=-1, keepdims=True) + 1e-06)
    return (x * inverse).astype(BF16)


def centre_kernel(where_ref, x_ref, w_ref, base_ref, proj_ref, nlow_ref):
    base_ref[:TOK] = x_ref[...]
    base_ref[TOK:] = jnp.zeros((TOK, D), BF16)
    low = normed_low(x_ref)
    nlow_ref[...] = low
    proj_ref[...] = nn(low, w_ref[...]).astype(BF16)


def side_kernel(
    where_ref, left_ref, right_ref, w_ref, wo_ref, cot_ref, proj_ref, cot_low_ref, dm_ref
):
    low = jnp.concatenate([normed_low(left_ref), normed_low(right_ref)], axis=0)
    proj_ref[...] = nn(low, w_ref[...]).astype(BF16)
    grad = cot_ref[...].astype(BF16)
    cot_low_ref[...] = grad
    dm_ref[...] = nt(grad, wo_ref[...]).astype(BF16)


def forward_kernel(
    where_ref, x1, x2, proj_ref, side_ref, w_ref, cot_ref, dm_ref,
    kv_ref, prob_ref, nlow_ref, far_ref, mixed_ref, pack_ref, left_ref, right_ref,
):
    kv_ref[:TOK] = proj_ref[:, D:]
    kv_ref[TOK:OWN] = side_ref[:, D:]
    for piece, x_ref in enumerate((x1, x2)):
        low = normed_low(x_ref)
        far_ref[piece * OWN : (piece + 1) * OWN] = low
        if piece == 0:
            nlow_ref[...] = low[:TOK]
        kv_ref[(piece + 1) * OWN : (piece + 2) * OWN] = nn(low, w_ref[:, D:]).astype(BF16)
    ok = window(where_ref, False)
    ok2 = jnp.concatenate([ok, ok], axis=0)
    lane = lax.broadcasted_iota(jnp.int32, (TOK, 128), 1)
    stats = jnp.zeros((TOK, 128), F32)
    for pair in range(PAIRS):
        at = slice(128 * pair, 128 * pair + 128)
        query = two_heads(proj_ref[:, at] * 0.125)
        scores = nt(query, kv_ref[:, at])
        scores = jnp.where(ok2, scores, -1e30)
        highest = jnp.max(scores, axis=-1, keepdims=True)
        grown = jnp.exp(scores - highest)
        total = jnp.sum(grown, axis=-1, keepdims=True)
        probs = (grown * (1.0 / total)).astype(BF16)
        prob_ref[pair] = probs
        value = kv_ref[:, D + 128 * pair : D + 128 * pair + 128]
        mixed = one_block(nn(probs, value)).astype(BF16)
        mixed_ref[:, at] = mixed
        log_total = highest + jnp.log(total)
        delta = two_sums(dm_ref[:, at], mixed)
        for first, rest in ((0, log_total), (24, delta)):
            for part in range(3):
                piece = rest.astype(BF16).astype(F32)
                rest = rest - piece
                for head in range(2):
                    chosen = lane == first + 8 * part + 2 * pair + head
                    stats = jnp.where(chosen, piece[TOK * head : TOK * head + TOK], stats)
    starts = where_ref[5] == 0
    pack_ref[:, D:] = stats.astype(BF16)

    @pl.when(starts)
    def _():
        pack_ref[:, :D] = cot_ref[...]

    @pl.when(jnp.logical_not(starts))
    def _():
        pack_ref[:, :D] = mixed_ref[...]

    put_sides(pack_ref[...].astype(F32), left_ref, right_ref)


def turned_kernel(where_ref, proj_ref, side_ref, far_ref, w_ref, n0, n1, query_ref, nt_ref, full_ref):
    query_ref[:, :TOK] = proj_ref[:, :D].astype(F32).T.astype(BF16)
    query_ref[:, TOK:OWN] = side_ref[:, :D].astype(F32).T.astype(BF16)
    far = nn(far_ref[...], w_ref[:, :D]).astype(BF16)
    query_ref[:, OWN:] = far.astype(F32).T.astype(BF16)
    full_ref[:, :TOK] = n0[...].astype(F32).T
    full_ref[:, TOK:] = n1[...].astype(F32).T
    nt_ref[...] = own_half(where_ref, full_ref).astype(BF16)


def own_half(where_ref, full_ref):
    rows = [
        full_ref[pl.ds(pl.multiple_of((2 * at + where_ref[2]) * BLOCK, BLOCK), BLOCK)]
        for at in range(full_ref.shape[0] // (2 * BLOCK))
    ]
    return jnp.concatenate(rows, axis=0)


def key_probs_kernel(
    where_ref, p0, p1, p2, proj_ref, query_ref, prob_ref, mixed_ref, delta_ref, total_ref
):
    head = lax.broadcasted_iota(jnp.int32, (8, 128), 0)
    lane = lax.broadcasted_iota(jnp.int32, (8, 128), 1)
    stats = jnp.concatenate([p[:, D:] for p in (p0, p1, p2)], axis=0)
    sums = []
    for first in (0, 24):
        chosen = ((lane & 7) == head) & (lane >= first) & (lane < first + 24)
        sums.append(nt(jnp.where(chosen, 1.0, 0.0).astype(BF16), stats))
    log_total, delta_ref[...] = sums

    @pl.when(where_ref[5] != 0)
    def _():
        for piece, p in enumerate((p0, p1, p2)):
            mixed_ref[:, piece * OWN : (piece + 1) * OWN] = p[:, :D].astype(F32).T.astype(BF16)

    total_ref[...] = log_total
    ok = window(where_ref, True)

    def one_pair(pair, carry):
        low = pl.multiple_of(128 * pair, 128)
        key = two_heads(proj_ref[:, pl.ds(low + D, 128)] * 0.125)
        scores = nn(key, query_ref[pl.ds(low, 128)])
        for side in range(2):
            part = scores[TOK * side : TOK * side + TOK] - total_ref[pl.ds(2 * pair + side, 1)]
            probs = jnp.exp(jnp.where(ok, part, -1e30))
            prob_ref[pair, TOK * side : TOK * side + TOK] = probs.astype(BF16)
        return carry

    lax.fori_loop(0, PAIRS, one_pair, 0)


def two_sums(grad, mixed):
    prod = grad.astype(F32) * mixed.astype(F32)
    lane = lax.broadcasted_iota(jnp.int32, prod.shape, 1)
    return jnp.concatenate(
        [
            jnp.sum(jnp.where(lane < 64, prod, 0.0), axis=-1, keepdims=True),
            jnp.sum(jnp.where(lane < 64, 0.0, prod), axis=-1, keepdims=True),
        ],
        axis=0,
    )


def query_kernel(
    where_ref, g_ref, w_ref, mixed_ref, kv_ref, prob_ref, *rest, turn
):
    (dq_ref, dm_ref), prev = rest[-2:], rest[:-2]
    for ref in prev:

        @pl.when(where_ref[5] != turn)
        def _():
            dq_ref[...] = ref[:, :D]

    @pl.when(where_ref[5] == turn)
    def _():
        dm_ref[...] = nt(g_ref[...], w_ref[...]).astype(BF16)

        def one_pair(pair, carry):
            low = pl.multiple_of(128 * pair, 128)
            at = pl.ds(low, 128)
            grad = dm_ref[:, at]
            delta = two_sums(grad, mixed_ref[:, at])
            pressure = nt(two_heads(grad), kv_ref[:, pl.ds(low + D, 128)])
            slopes = (prob_ref[pair].astype(F32) * (pressure - delta)).astype(BF16)
            dq_ref[:, at] = (one_block(nn(slopes, kv_ref[:, at])) * 0.125).astype(BF16)
            return carry

        lax.fori_loop(0, PAIRS, one_pair, 0)


def turned_block(stacked):
    row = lax.broadcasted_iota(jnp.int32, (128, 128), 0)
    return jnp.where(row < 64, stacked[:, :128], stacked[:, 128:]).T


def key_kernel(
    where_ref, g0, g1, g2, wo_ref, delta_ref, proj_ref, query_ref, prob_ref, *rest, turn, last
):
    ins, rest = ((), rest) if last else (rest[:4], rest[4:])
    count = 1 if last else 3
    prev, rest = (rest[:count], rest[count:]) if turn else ((), rest)
    outs, sends, dm_ref = rest[:count], rest[count:-1], rest[-1]
    kv_ref = outs[0] if last else outs[0].at[:, D:]
    active = where_ref[5] == turn

    if prev:

        @pl.when(jnp.logical_not(active))
        def _():
            for new, old in zip(outs, prev):
                new[...] = old[:, D:] if last else old[...]

    @pl.when(active)
    def _():
        for piece, g in enumerate((g0, g1, g2)):
            d_mixed = nt(wo_ref[...], g[:, :D]).astype(BF16)
            dm_ref[:, piece * OWN : (piece + 1) * OWN] = d_mixed

        def one_pair(pair, carry):
            low = pl.multiple_of(128 * pair, 128)
            at = pl.ds(low, 128)
            value = two_heads(proj_ref[:, pl.ds(low + 2 * D, 128)])
            grad = dm_ref[at]
            if turn:
                prod = grad.astype(F32) * delta_ref[at].astype(F32)
                deltas = [jnp.sum(prod[r : r + 64], axis=0, keepdims=True) for r in (0, 64)]
            else:
                deltas = [delta_ref[pl.ds(2 * pair + side, 1)] for side in range(2)]
            pressure = nn(value, grad)
            probs = prob_ref[pair]
            d_value = nt(grad, probs)
            slopes = []
            for side in range(2):
                rows = slice(TOK * side, TOK * side + TOK)
                slopes.append(
                    (probs[rows].astype(F32) * (pressure[rows] - deltas[side])).astype(BF16)
                )
            d_key = nt(query_ref[at], jnp.concatenate(slopes, axis=0))
            kv_ref[:, at] = (turned_block(d_key) * 0.125).astype(BF16)
            kv_ref[:, pl.ds(low + D, 128)] = turned_block(d_value).astype(BF16)
            return carry

        lax.fori_loop(0, PAIRS, one_pair, 0, unroll=4 if last else 2)
        if not last:
            dq_ref, *ins_rest = ins
            outs[0][:, :D] = dq_ref[...]
            outs[1][:TOK] = g0[:TOK, :D]
            outs[1][TOK:] = g1[:TOK, :D]
            out = input_grad(nt(outs[0][...], ins_rest[1][...]), ins_rest[0], ins_rest[2])
            outs[2][...] = out
            low_ref, left_ref, right_ref = sends
            low_ref[...] = out.astype(BF16)
            put_sides(out, left_ref, right_ref)


def input_grad(d_normed, g_ref, x_ref):
    x = x_ref[...].astype(F32)
    inverse = lax.rsqrt(jnp.mean(x * x, axis=-1, keepdims=True) + 1e-06)
    normed = x * inverse
    inner = jnp.mean(d_normed * normed, axis=-1, keepdims=True)
    return g_ref[...].astype(F32) + inverse * (d_normed - normed * inner)


def input_kernel(where_ref, dq_ref, kv_ref, g_ref, wq_ref, x_ref, prev_ref, in_ref, *, turn):
    @pl.when(where_ref[5] == turn)
    def _():
        d_normed = nt(dq_ref[...], wq_ref[:, :D]) + nt(kv_ref[...], wq_ref[:, D:])
        in_ref[...] = input_grad(d_normed, g_ref, x_ref)

    @pl.when(where_ref[5] != turn)
    def _():
        in_ref[...] = prev_ref[...]


def split_rows(where_ref, parts, outs):
    cols = len(outs)
    for distance, out_ref in enumerate(outs):
        col = lax.rem(where_ref[6] + distance, cols)
        for at, ref, step, first in parts:
            rows = [
                ref[pl.ds(pl.multiple_of(step * chip + first + 8 * col, 8), 8)]
                for chip in range(out_ref.shape[0] // 8)
            ]
            out_ref[:, at] = jnp.concatenate(rows, axis=0).astype(BF16)


def early_kernel(where_ref, nt_ref, dq_ref, mixed_ref, g0, g1, m, prev_ref, *refs, turn):
    outs, (left_ref, full_ref, g_ref) = refs[:-3], refs[-3:]

    @pl.when(where_ref[5] == turn)
    def _():
        g_ref[:TOK] = g0[:TOK]
        g_ref[TOK:] = g1[:TOK]

    @pl.when(where_ref[5] != turn)
    def _():
        g_ref[...] = prev_ref[...]

    d_query = jnp.concatenate([dq_ref[...], m[:TOK]], axis=0)
    left_ref[...] = nn(nt_ref[...], d_query)
    mixed = jnp.concatenate([mixed_ref[...], m[TOK:]], axis=0)
    full_ref[...] = tn(mixed, g_ref[...])
    split_rows(
        where_ref,
        [(slice(0, D), left_ref, BLOCK, 0), (slice(D, 2 * D), full_ref, 2 * BLOCK, where_ref[2] * BLOCK)],
        outs,
    )


def late_kernel(where_ref, nt_ref, d0, d1, *refs):
    outs, left_ref = refs[:-1], refs[-1]
    left_ref[...] = nn(nt_ref[...], jnp.concatenate([d0[...], d1[...]], axis=0))
    split_rows(where_ref, [(slice(0, 2 * D), left_ref, BLOCK, 0)], outs)


def col_total_kernel(where_ref, *refs):
    count = (len(refs) - 1) // 2
    for at, parts in ((slice(0, 2 * D), refs[:count]), (slice(2 * D, 4 * D), refs[count:-1])):
        total = parts[0][...].astype(F32)
        for ref in parts[1:]:
            total = total + ref[...].astype(F32)
        refs[-1][:, at] = total.astype(BF16)


def total_kernel(where_ref, part_ref, qkv_ref, out_ref, *, scale):
    total = part_ref[0].astype(F32)
    for source in range(1, part_ref.shape[0]):
        total = total + part_ref[source].astype(F32)
    qkv_ref[:, :D] = total[:, :D] * scale
    qkv_ref[:, D:] = total[:, 2 * D :] * scale
    out_ref[...] = total[:, D : 2 * D] * scale


def call(kernel, outs, *args, scratch=(), flops=0, moved=4 << 20):
    vmem = pl.BlockSpec(memory_space=pltpu.VMEM)
    return pl.pallas_call(
        kernel,
        out_shape=[jax.ShapeDtypeStruct(s, t) for s, t in outs],
        in_specs=[pl.BlockSpec(memory_space=pltpu.SMEM)] + [vmem] * (len(args) - 1),
        out_specs=[vmem] * len(outs),
        scratch_shapes=list(scratch),
        compiler_params=pltpu.CompilerParams(vmem_limit_bytes=VMEM_LIMIT),
        cost_estimate=pl.CostEstimate(flops=flops, bytes_accessed=moved, transcendentals=0),
    )(*args)


def body(sizes, activations, qkv_weight, out_weight, cotangent):
    pipes, chips, cols = sizes

    def routed(block, step):
        pairs = []
        for p in range(pipes):
            for r in range(2 * chips):
                for c in range(cols):
                    p2, r2, c2 = step(p, r, c)
                    target = ((p2 % pipes) * 2 * chips + r2 % (2 * chips)) * cols + c2 % cols
                    pairs.append(((p * 2 * chips + r) * cols + c, target))
        return lax.ppermute(block, AXES, pairs)

    def col_rims(left_half, right_half, down=0):
        left = routed(right_half, lambda p, r, c: (p - down, r, c + 1))
        right = routed(left_half, lambda p, r, c: (p - down, r, c - 1))
        return left, right

    def mate(p, r, c):
        return p, r ^ 1, c

    def row_rims(pieces):
        own = jnp.concatenate(pieces, axis=0)
        beyond = routed(own, lambda p, r, c: (p, r - 1 + 2 * (r & 1), c))
        return own, routed(own, mate), beyond

    pipe, z, core, col = (lax.axis_index(axis) for axis in AXES)
    x = activations.reshape(TOK, D)
    w_qkv, w_out = qkv_weight[0], out_weight[0]
    cot = cotangent.reshape(TOK, D)
    row_total, col_total = 16 * chips, 16 * cols
    where = jnp.stack(
        [8 * (2 * z + core), 16 * col, core, row_total, col_total, pipes - 1 - pipe, col]
    ).astype(jnp.int32)

    x_sides = x.reshape(8, 2, 8, D)
    low_side, high_side = x_sides[:, 0].reshape(64, D), x_sides[:, 1].reshape(64, D)
    base, proj, nlow = call(
        centre_kernel, [((OWN, D), BF16), ((TOK, 3 * D), BF16), ((TOK, D), BF16)],
        where, x, w_qkv, flops=1 << 28,
    )
    left, right = col_rims(low_side, high_side)
    own = lax.dynamic_update_slice(base, left, (TOK, 0))
    own, near, far = row_rims([lax.dynamic_update_slice(own, right, (TOK + 64, 0))])
    side_proj, cot_low, d_mixed = call(
        side_kernel, [((TOK, 3 * D), BF16), ((TOK, D), BF16), ((TOK, D), BF16)],
        where, left, right, w_qkv, w_out, cot, flops=1 << 28,
    )
    wide = D + 128
    kv, q_probs, nlow_mate, low_far, mixed, pack, low_side, high_side = call(
        forward_kernel,
        [((REGION, 2 * D), BF16), ((PAIRS, OWN, REGION), BF16), ((TOK, D), BF16),
         ((2 * OWN, D), BF16), ((TOK, D), BF16), ((TOK, wide), BF16), ((64, wide), BF16),
         ((64, wide), BF16)],
        where, near, far, proj, side_proj, w_qkv, cot_low, d_mixed, flops=2 << 30,
    )
    sides = col_rims(low_side, high_side)
    queries, n_turned = call(
        turned_kernel, [((D, REGION), BF16), ((OWN, OWN), BF16)],
        where, proj, side_proj, low_far, w_qkv, nlow, nlow_mate,
        scratch=[pltpu.VMEM((D, OWN), F32)], flops=1 << 28,
    )

    def query_side(turn, gradient, *prev):
        return call(
            functools.partial(query_kernel, turn=turn), [((TOK, D), BF16)],
            where, gradient, w_out, mixed, kv, q_probs, *prev,
            scratch=[pltpu.VMEM((TOK, D), BF16)], flops=1 << 29,
        )[0]

    d_query = query_side(0, cot_low)
    left, right = sides
    right, queries, d_query = lax.optimization_barrier((right, queries, d_query))
    packs = row_rims([pack, left, right])
    k_probs, mixed_turned, delta = call(
        key_probs_kernel,
        [((PAIRS, OWN, REGION), BF16), ((D, REGION), BF16), ((8, REGION), F32)],
        where, *packs, proj, queries, scratch=[pltpu.VMEM((8, REGION), F32)], flops=1 << 28,
    )
    gradient, gs = cot_low, packs
    def over_cols(parts):
        moved = list(parts)
        for distance in sorted(range(1, cols), key=lambda d: -min(d, cols - d)):
            moved[distance] = routed(parts[distance], lambda p, r, c: (p, r, c + distance))
        return moved

    state = ()
    for turn in range(pipes):
        last = turn == pipes - 1
        if turn > 0:
            low, low_side, high_side = sends
            gradient = routed(low, lambda p, r, c: (p - 1, r, c))
            left, right = col_rims(low_side, high_side, 1)
            gs = row_rims([gradient, left, right])
            d_query = query_side(turn, gradient, *((state[0],) if last else ()))
        fixed = (w_out, mixed_turned if turn else delta, proj, queries, k_probs)
        scratch = [pltpu.VMEM((D, REGION), BF16)]
        if not last:
            outs = call(
                functools.partial(key_kernel, turn=turn, last=False),
                [((TOK, 3 * D), BF16), ((OWN, D), BF16), ((TOK, D), F32), ((TOK, D), BF16),
                 ((64, D), BF16), ((64, D), BF16)],
                where, *gs, *fixed, d_query, gradient if turn else cot, w_qkv, x, *state,
                scratch=scratch, flops=1 << 30,
            )
            state, sends = outs[:3], outs[3:]
    d_proj, g_low, d_in = state
    extra = jnp.concatenate([d_query, mixed], axis=0)
    early = call(
        functools.partial(early_kernel, turn=turn), [((8 * chips, 2 * D), BF16)] * cols,
        where, n_turned, d_query, mixed, gs[0], gs[1], routed(extra, mate), g_low,
        scratch=[pltpu.VMEM((OWN, D), F32), pltpu.VMEM((D, D), F32), pltpu.VMEM((OWN, D), BF16)],
        flops=1 << 28,
    )
    (d_kv,) = call(
        functools.partial(key_kernel, turn=turn, last=True), [((TOK, 2 * D), BF16)],
        where, *gs, *fixed, d_proj, scratch=scratch, flops=1 << 30,
    )
    early = list(early)
    early[0], d_kv_mate = lax.optimization_barrier((early[0], routed(d_kv, mate)))
    early = over_cols(early)
    late = list(call(
        late_kernel, [((8 * chips, 2 * D), BF16)] * cols, where, n_turned, d_kv, d_kv_mate,
        scratch=[pltpu.VMEM((OWN, 2 * D), F32)], flops=1 << 29,
    ))
    late[1], early[2] = lax.optimization_barrier((late[1], early[2]))
    late = over_cols(late)
    (d_in,) = call(
        functools.partial(input_kernel, turn=turn), [((TOK, D), F32)],
        where, d_query, d_kv, gradient, w_qkv, x, d_in, flops=1 << 28,
    )
    late[-1], d_in = lax.optimization_barrier((late[-1], d_in))
    (part,) = call(col_total_kernel, [((8 * chips, 4 * D), BF16)], where, *early, *late)
    part = part.reshape(chips, 8, 4 * D)
    part = lax.all_to_all(part, "z", 0, 0, tiled=True)
    qkv_part, out_part = call(
        functools.partial(total_kernel, scale=(row_total * col_total) ** (-0.5)),
        [((8, 3 * D), F32), ((8, D), F32)], where, part,
    )
    return d_in.reshape(1, 8, 16, D), qkv_part[None], out_part[None]


def solution(mesh):
    pipes, rows, cols = (mesh.shape[axis] for axis in ("pipe", "row", "col"))
    fine = Mesh(np.asarray(mesh.devices).reshape(pipes, rows // 2, 2, cols), AXES)
    row = ("z", "core")
    return jax.shard_map(
        functools.partial(body, (pipes, rows // 2, cols)),
        mesh=fine,
        in_specs=(
            P("pipe", row, "col", None),
            P("pipe", None, None),
            P("pipe", None, None),
            P(row, "col", None),
        ),
        out_specs=(
            P("pipe", row, "col", None),
            P("pipe", ("z", "core", "col"), None),
            P("pipe", ("z", "core", "col"), None),
        ),
        check_vma=False,
    )
```

```python
import functools

import jax
import jax.numpy as jnp
import numpy as np
from jax import lax
from jax.experimental import pallas as pl
from jax.experimental.pallas import tpu as pltpu
from jax.sharding import Mesh
from jax.sharding import PartitionSpec as P

F32 = jnp.float32
BF16 = jnp.bfloat16
AXES = ("pipe", "z", "core", "col")
D = 512
PAIRS = 4
TOK = 128
OWN = 256
REGION = 768
BLOCK = 32
VMEM_LIMIT = 40 * 1024 * 1024


def nn(a, b):
    return lax.dot_general(a, b, (((1,), (0,)), ((), ())), preferred_element_type=F32)


def nt(a, b):
    return lax.dot_general(a, b, (((1,), (1,)), ((), ())), preferred_element_type=F32)


def tn(a, b):
    return lax.dot_general(a, b, (((0,), (0,)), ((), ())), preferred_element_type=F32)


def two_heads(block):
    lane = lax.broadcasted_iota(jnp.int32, block.shape, 1)
    zero = jnp.zeros_like(block)
    return jnp.concatenate(
        [jnp.where(lane < 64, block, zero), jnp.where(lane < 64, zero, block)], axis=0
    )


def one_block(stacked):
    half = stacked.shape[0] // 2
    lane = lax.broadcasted_iota(jnp.int32, (half, 128), 1)
    return jnp.where(lane < 64, stacked[:half], stacked[half:])


def place(index, core):
    piece = index >> 8
    inner = index & 255
    side = inner - 128
    is_centre = inner < 128
    row = jnp.where(is_centre, inner >> 4, (side & 63) >> 3)
    col = jnp.where(is_centre, inner & 15, jnp.where(side < 64, (side & 7) - 8, (side & 7) + 16))
    mate = jnp.where(core == 0, 8, -8)
    row = row + jnp.where(piece == 1, mate, jnp.where(piece == 2, -mate, 0))
    return row, col


def window(where_ref, keys_own):
    row0, col0, core, rows, cols = (where_ref[i] for i in range(5))
    own = lax.broadcasted_iota(jnp.int32, (TOK, 1), 0)
    reach_row, reach_col = place(lax.broadcasted_iota(jnp.int32, (1, REGION), 1), core)
    grid_row, grid_col = row0 + reach_row, col0 + reach_col
    inside = (grid_row >= 0) & (grid_row < rows) & (grid_col >= 0) & (grid_col < cols)
    reach_row = jnp.where(inside, reach_row, 1 << 20)
    if keys_own:
        step_row, step_col = (own >> 4) - reach_row, (own & 15) - reach_col
    else:
        step_row, step_col = reach_row - (own >> 4), reach_col - (own & 15)
    return (step_row >= -8) & (step_row <= 7) & (step_col >= -8) & (step_col <= 7)


def put_sides(block, left_ref, right_ref):
    sides = block.reshape(8, 2, 8, block.shape[-1])
    left_ref[...] = sides[:, 0].reshape(64, -1).astype(BF16)
    right_ref[...] = sides[:, 1].reshape(64, -1).astype(BF16)


def normed_low(x_ref):
    x = x_ref[...].astype(F32)
    inverse = lax.rsqrt(jnp.mean(x * x, axis=-1, keepdims=True) + 1e-06)
    return (x * inverse).astype(BF16)


def centre_kernel(where_ref, x_ref, w_ref, base_ref, proj_ref, nlow_ref):
    base_ref[:TOK] = x_ref[...]
    base_ref[TOK:] = jnp.zeros((TOK, D), BF16)
    low = normed_low(x_ref)
    nlow_ref[...] = low
    proj_ref[...] = nn(low, w_ref[...]).astype(BF16)


def side_kernel(
    where_ref, left_ref, right_ref, w_ref, wo_ref, cot_ref, proj_ref, cot_low_ref, dm_ref
):
    low = jnp.concatenate([normed_low(left_ref), normed_low(right_ref)], axis=0)
    proj_ref[...] = nn(low, w_ref[...]).astype(BF16)
    grad = cot_ref[...].astype(BF16)
    cot_low_ref[...] = grad
    dm_ref[...] = nt(grad, wo_ref[...]).astype(BF16)


def forward_kernel(
    where_ref, x1, x2, proj_ref, side_ref, w_ref, cot_ref, dm_ref,
    kv_ref, prob_ref, nlow_ref, far_ref, mixed_ref, pack_ref, left_ref, right_ref,
):
    kv_ref[:TOK] = proj_ref[:, D:]
    kv_ref[TOK:OWN] = side_ref[:, D:]
    for piece, x_ref in enumerate((x1, x2)):
        low = normed_low(x_ref)
        far_ref[piece * OWN : (piece + 1) * OWN] = low
        if piece == 0:
            nlow_ref[...] = low[:TOK]
        kv_ref[(piece + 1) * OWN : (piece + 2) * OWN] = nn(low, w_ref[:, D:]).astype(BF16)
    ok = window(where_ref, False)
    ok2 = jnp.concatenate([ok, ok], axis=0)
    lane = lax.broadcasted_iota(jnp.int32, (TOK, 128), 1)

    def one_pair(pair, stats):
        low = pl.multiple_of(128 * pair, 128)
        at = pl.ds(low, 128)
        query = two_heads(proj_ref[:, at] * 0.125)
        scores = jnp.where(ok2, nt(query, kv_ref[:, at]), -1e30)
        highest = jnp.max(scores, axis=-1, keepdims=True)
        grown = jnp.exp(scores - highest)
        total = jnp.sum(grown, axis=-1, keepdims=True)
        probs = (grown * (1.0 / total)).astype(BF16)
        prob_ref[pair] = probs
        mixed = one_block(nn(probs, kv_ref[:, pl.ds(low + D, 128)])).astype(BF16)
        mixed_ref[:, at] = mixed
        log_total = highest + jnp.log(total)
        delta = two_sums(dm_ref[:, at], mixed)
        for first, rest in ((0, log_total), (24, delta)):
            for part in range(3):
                piece = rest.astype(BF16).astype(F32)
                rest = rest - piece
                for head in range(2):
                    chosen = lane == first + 8 * part + 2 * pair + head
                    stats = jnp.where(chosen, piece[TOK * head : TOK * head + TOK], stats)
        return stats

    stats = lax.fori_loop(0, PAIRS, one_pair, jnp.zeros((TOK, 128), F32), unroll=2)
    starts = where_ref[5] == 0
    pack_ref[:, D:] = stats.astype(BF16)

    @pl.when(starts)
    def _():
        pack_ref[:, :D] = cot_ref[...]

    @pl.when(jnp.logical_not(starts))
    def _():
        pack_ref[:, :D] = mixed_ref[...]

    put_sides(pack_ref[...].astype(F32), left_ref, right_ref)


def turned_kernel(where_ref, proj_ref, side_ref, far_ref, w_ref, n0, n1, query_ref, nt_ref, full_ref):
    query_ref[:, :TOK] = proj_ref[:, :D].astype(F32).T.astype(BF16)
    query_ref[:, TOK:OWN] = side_ref[:, :D].astype(F32).T.astype(BF16)
    far = nn(far_ref[...], w_ref[:, :D]).astype(BF16)
    query_ref[:, OWN:] = far.astype(F32).T.astype(BF16)
    full_ref[:, :TOK] = n0[...].astype(F32).T
    full_ref[:, TOK:] = n1[...].astype(F32).T
    nt_ref[...] = own_half(where_ref, full_ref).astype(BF16)


def own_half(where_ref, full_ref):
    rows = [
        full_ref[pl.ds(pl.multiple_of((2 * at + where_ref[2]) * BLOCK, BLOCK), BLOCK)]
        for at in range(full_ref.shape[0] // (2 * BLOCK))
    ]
    return jnp.concatenate(rows, axis=0)


def key_probs_kernel(
    where_ref, p0, p1, p2, proj_ref, query_ref, prob_ref, mixed_ref, delta_ref, total_ref
):
    head = lax.broadcasted_iota(jnp.int32, (8, 128), 0)
    lane = lax.broadcasted_iota(jnp.int32, (8, 128), 1)
    stats = jnp.concatenate([p[:, D:] for p in (p0, p1, p2)], axis=0)
    sums = []
    for first in (0, 24):
        chosen = ((lane & 7) == head) & (lane >= first) & (lane < first + 24)
        sums.append(nt(jnp.where(chosen, 1.0, 0.0).astype(BF16), stats))
    log_total, delta_ref[...] = sums

    @pl.when(where_ref[5] != 0)
    def _():
        for piece, p in enumerate((p0, p1, p2)):
            mixed_ref[:, piece * OWN : (piece + 1) * OWN] = p[:, :D].astype(F32).T.astype(BF16)

    total_ref[...] = log_total
    ok = window(where_ref, True)

    def one_pair(pair, carry):
        low = pl.multiple_of(128 * pair, 128)
        key = two_heads(proj_ref[:, pl.ds(low + D, 128)] * 0.125)
        scores = nn(key, query_ref[pl.ds(low, 128)])
        for side in range(2):
            part = scores[TOK * side : TOK * side + TOK] - total_ref[pl.ds(2 * pair + side, 1)]
            probs = jnp.exp(jnp.where(ok, part, -1e30))
            prob_ref[pair, TOK * side : TOK * side + TOK] = probs.astype(BF16)
        return carry

    lax.fori_loop(0, PAIRS, one_pair, 0)


def two_sums(grad, mixed):
    prod = grad.astype(F32) * mixed.astype(F32)
    lane = lax.broadcasted_iota(jnp.int32, prod.shape, 1)
    return jnp.concatenate(
        [
            jnp.sum(jnp.where(lane < 64, prod, 0.0), axis=-1, keepdims=True),
            jnp.sum(jnp.where(lane < 64, 0.0, prod), axis=-1, keepdims=True),
        ],
        axis=0,
    )


def query_kernel(
    where_ref, g_ref, w_ref, mixed_ref, kv_ref, prob_ref, *rest, turn
):
    (dq_ref, dm_ref), prev = rest[-2:], rest[:-2]
    for ref in prev:

        @pl.when(where_ref[5] != turn)
        def _():
            dq_ref[...] = ref[:, :D]

    @pl.when(where_ref[5] == turn)
    def _():
        dm_ref[...] = nt(g_ref[...], w_ref[...]).astype(BF16)

        def one_pair(pair, carry):
            low = pl.multiple_of(128 * pair, 128)
            at = pl.ds(low, 128)
            grad = dm_ref[:, at]
            delta = two_sums(grad, mixed_ref[:, at])
            pressure = nt(two_heads(grad), kv_ref[:, pl.ds(low + D, 128)])
            slopes = (prob_ref[pair].astype(F32) * (pressure - delta)).astype(BF16)
            dq_ref[:, at] = (one_block(nn(slopes, kv_ref[:, at])) * 0.125).astype(BF16)
            return carry

        lax.fori_loop(0, PAIRS, one_pair, 0, unroll=2)


def turned_block(stacked):
    row = lax.broadcasted_iota(jnp.int32, (128, 128), 0)
    return jnp.where(row < 64, stacked[:, :128], stacked[:, 128:]).T


def key_kernel(
    where_ref, g0, g1, g2, wo_ref, delta_ref, proj_ref, query_ref, prob_ref, *rest, turn, last
):
    ins, rest = ((), rest) if last else (rest[:4], rest[4:])
    count = 1 if last else 3
    prev, rest = (rest[:count], rest[count:]) if turn else ((), rest)
    outs, sends, dm_ref = rest[:count], rest[count:-1], rest[-1]
    kv_ref = outs[0] if last else outs[0].at[:, D:]
    active = where_ref[5] == turn

    if prev:

        @pl.when(jnp.logical_not(active))
        def _():
            for new, old in zip(outs, prev):
                new[...] = old[:, D:] if last else old[...]

    @pl.when(active)
    def _():
        for piece, g in enumerate((g0, g1, g2)):
            d_mixed = nt(wo_ref[...], g[:, :D]).astype(BF16)
            dm_ref[:, piece * OWN : (piece + 1) * OWN] = d_mixed

        def one_pair(pair, carry):
            low = pl.multiple_of(128 * pair, 128)
            at = pl.ds(low, 128)
            value = two_heads(proj_ref[:, pl.ds(low + 2 * D, 128)])
            grad = dm_ref[at]
            if turn:
                prod = grad.astype(F32) * delta_ref[at].astype(F32)
                deltas = [jnp.sum(prod[r : r + 64], axis=0, keepdims=True) for r in (0, 64)]
            else:
                deltas = [delta_ref[pl.ds(2 * pair + side, 1)] for side in range(2)]
            pressure = nn(value, grad)
            probs = prob_ref[pair]
            d_value = nt(grad, probs)
            slopes = []
            for side in range(2):
                rows = slice(TOK * side, TOK * side + TOK)
                slopes.append(
                    (probs[rows].astype(F32) * (pressure[rows] - deltas[side])).astype(BF16)
                )
            d_key = nt(query_ref[at], jnp.concatenate(slopes, axis=0))
            kv_ref[:, at] = (turned_block(d_key) * 0.125).astype(BF16)
            kv_ref[:, pl.ds(low + D, 128)] = turned_block(d_value).astype(BF16)
            return carry

        lax.fori_loop(0, PAIRS, one_pair, 0, unroll=4 if last else 2)
        if not last:
            dq_ref, *ins_rest = ins
            outs[0][:, :D] = dq_ref[...]
            outs[1][:TOK] = g0[:TOK, :D]
            outs[1][TOK:] = g1[:TOK, :D]
            out = input_grad(nt(outs[0][...], ins_rest[1][...]), ins_rest[0], ins_rest[2])
            outs[2][...] = out
            low_ref, left_ref, right_ref = sends
            low_ref[...] = out.astype(BF16)
            put_sides(out, left_ref, right_ref)


def input_grad(d_normed, g_ref, x_ref):
    x = x_ref[...].astype(F32)
    inverse = lax.rsqrt(jnp.mean(x * x, axis=-1, keepdims=True) + 1e-06)
    normed = x * inverse
    inner = jnp.mean(d_normed * normed, axis=-1, keepdims=True)
    return g_ref[...].astype(F32) + inverse * (d_normed - normed * inner)


def input_kernel(where_ref, dq_ref, kv_ref, g_ref, wq_ref, x_ref, prev_ref, in_ref, *, turn):
    @pl.when(where_ref[5] == turn)
    def _():
        d_normed = nt(dq_ref[...], wq_ref[:, :D]) + nt(kv_ref[...], wq_ref[:, D:])
        in_ref[...] = input_grad(d_normed, g_ref, x_ref)

    @pl.when(where_ref[5] != turn)
    def _():
        in_ref[...] = prev_ref[...]


def split_rows(where_ref, parts, outs):
    cols = len(outs)
    for distance, out_ref in enumerate(outs):
        col = lax.rem(where_ref[6] + distance, cols)
        for at, ref, step, first in parts:
            rows = [
                ref[pl.ds(pl.multiple_of(step * chip + first + 8 * col, 8), 8)]
                for chip in range(out_ref.shape[0] // 8)
            ]
            out_ref[:, at] = jnp.concatenate(rows, axis=0).astype(BF16)


def early_kernel(where_ref, nt_ref, dq_ref, mixed_ref, g0, g1, m, prev_ref, *refs, turn):
    outs, (left_ref, full_ref, g_ref) = refs[:-3], refs[-3:]

    @pl.when(where_ref[5] == turn)
    def _():
        g_ref[:TOK] = g0[:TOK]
        g_ref[TOK:] = g1[:TOK]

    @pl.when(where_ref[5] != turn)
    def _():
        g_ref[...] = prev_ref[...]

    d_query = jnp.concatenate([dq_ref[...], m[:TOK]], axis=0)
    left_ref[...] = nn(nt_ref[...], d_query)
    mixed = jnp.concatenate([mixed_ref[...], m[TOK:]], axis=0)
    full_ref[...] = tn(mixed, g_ref[...])
    split_rows(
        where_ref,
        [(slice(0, D), left_ref, BLOCK, 0), (slice(D, 2 * D), full_ref, 2 * BLOCK, where_ref[2] * BLOCK)],
        outs,
    )


def late_kernel(where_ref, nt_ref, d0, d1, *refs):
    outs, left_ref = refs[:-1], refs[-1]
    left_ref[...] = nn(nt_ref[...], jnp.concatenate([d0[...], d1[...]], axis=0))
    split_rows(where_ref, [(slice(0, 2 * D), left_ref, BLOCK, 0)], outs)


def col_total_kernel(where_ref, *refs):
    count = (len(refs) - 1) // 2
    for at, parts in ((slice(0, 2 * D), refs[:count]), (slice(2 * D, 4 * D), refs[count:-1])):
        total = parts[0][...].astype(F32)
        for ref in parts[1:]:
            total = total + ref[...].astype(F32)
        refs[-1][:, at] = total.astype(BF16)


def total_kernel(where_ref, part_ref, qkv_ref, out_ref, *, scale):
    total = part_ref[0].astype(F32)
    for source in range(1, part_ref.shape[0]):
        total = total + part_ref[source].astype(F32)
    qkv_ref[:, :D] = total[:, :D] * scale
    qkv_ref[:, D:] = total[:, 2 * D :] * scale
    out_ref[...] = total[:, D : 2 * D] * scale


def call(kernel, outs, *args, scratch=(), flops=0, moved=4 << 20):
    vmem = pl.BlockSpec(memory_space=pltpu.VMEM)
    return pl.pallas_call(
        kernel,
        out_shape=[jax.ShapeDtypeStruct(s, t) for s, t in outs],
        in_specs=[pl.BlockSpec(memory_space=pltpu.SMEM)] + [vmem] * (len(args) - 1),
        out_specs=[vmem] * len(outs),
        scratch_shapes=list(scratch),
        compiler_params=pltpu.CompilerParams(vmem_limit_bytes=VMEM_LIMIT),
        cost_estimate=pl.CostEstimate(flops=flops, bytes_accessed=moved, transcendentals=0),
    )(*args)


def body(sizes, activations, qkv_weight, out_weight, cotangent):
    pipes, chips, cols = sizes

    def routed(block, step):
        pairs = []
        for p in range(pipes):
            for r in range(2 * chips):
                for c in range(cols):
                    p2, r2, c2 = step(p, r, c)
                    target = ((p2 % pipes) * 2 * chips + r2 % (2 * chips)) * cols + c2 % cols
                    pairs.append(((p * 2 * chips + r) * cols + c, target))
        return lax.ppermute(block, AXES, pairs)

    def col_rims(left_half, right_half, down=0):
        left = routed(right_half, lambda p, r, c: (p - down, r, c + 1))
        right = routed(left_half, lambda p, r, c: (p - down, r, c - 1))
        return left, right

    def mate(p, r, c):
        return p, r ^ 1, c

    def row_rims(pieces):
        own = jnp.concatenate(pieces, axis=0)
        beyond = routed(own, lambda p, r, c: (p, r - 1 + 2 * (r & 1), c))
        return own, routed(own, mate), beyond

    pipe, z, core, col = (lax.axis_index(axis) for axis in AXES)
    x = activations.reshape(TOK, D)
    w_qkv, w_out = qkv_weight[0], out_weight[0]
    cot = cotangent.reshape(TOK, D)
    row_total, col_total = 16 * chips, 16 * cols
    where = jnp.stack(
        [8 * (2 * z + core), 16 * col, core, row_total, col_total, pipes - 1 - pipe, col]
    ).astype(jnp.int32)

    x_sides = x.reshape(8, 2, 8, D)
    low_side, high_side = x_sides[:, 0].reshape(64, D), x_sides[:, 1].reshape(64, D)
    base, proj, nlow = call(
        centre_kernel, [((OWN, D), BF16), ((TOK, 3 * D), BF16), ((TOK, D), BF16)],
        where, x, w_qkv, flops=1 << 28,
    )
    left, right = col_rims(low_side, high_side)
    own = lax.dynamic_update_slice(base, left, (TOK, 0))
    own, near, far = row_rims([lax.dynamic_update_slice(own, right, (TOK + 64, 0))])
    side_proj, cot_low, d_mixed = call(
        side_kernel, [((TOK, 3 * D), BF16), ((TOK, D), BF16), ((TOK, D), BF16)],
        where, left, right, w_qkv, w_out, cot, flops=1 << 28,
    )
    wide = D + 128
    kv, q_probs, nlow_mate, low_far, mixed, pack, low_side, high_side = call(
        forward_kernel,
        [((REGION, 2 * D), BF16), ((PAIRS, OWN, REGION), BF16), ((TOK, D), BF16),
         ((2 * OWN, D), BF16), ((TOK, D), BF16), ((TOK, wide), BF16), ((64, wide), BF16),
         ((64, wide), BF16)],
        where, near, far, proj, side_proj, w_qkv, cot_low, d_mixed, flops=2 << 30,
    )
    sides = col_rims(low_side, high_side)
    queries, n_turned = call(
        turned_kernel, [((D, REGION), BF16), ((OWN, OWN), BF16)],
        where, proj, side_proj, low_far, w_qkv, nlow, nlow_mate,
        scratch=[pltpu.VMEM((D, OWN), F32)], flops=1 << 28,
    )

    def query_side(turn, gradient, *prev):
        return call(
            functools.partial(query_kernel, turn=turn), [((TOK, D), BF16)],
            where, gradient, w_out, mixed, kv, q_probs, *prev,
            scratch=[pltpu.VMEM((TOK, D), BF16)], flops=1 << 29,
        )[0]

    d_query = query_side(0, cot_low)
    left, right = sides
    right, queries, d_query = lax.optimization_barrier((right, queries, d_query))
    packs = row_rims([pack, left, right])
    k_probs, mixed_turned, delta = call(
        key_probs_kernel,
        [((PAIRS, OWN, REGION), BF16), ((D, REGION), BF16), ((8, REGION), F32)],
        where, *packs, proj, queries, scratch=[pltpu.VMEM((8, REGION), F32)], flops=1 << 28,
    )
    gradient, gs = cot_low, packs
    def over_cols(parts):
        moved = list(parts)
        for distance in sorted(range(1, cols), key=lambda d: -min(d, cols - d)):
            moved[distance] = routed(parts[distance], lambda p, r, c: (p, r, c + distance))
        return moved

    state = ()
    for turn in range(pipes):
        last = turn == pipes - 1
        if turn > 0:
            low, low_side, high_side = sends
            gradient = routed(low, lambda p, r, c: (p - 1, r, c))
            left, right = col_rims(low_side, high_side, 1)
            gs = row_rims([gradient, left, right])
            d_query = query_side(turn, gradient, *((state[0],) if last else ()))
        fixed = (w_out, mixed_turned if turn else delta, proj, queries, k_probs)
        scratch = [pltpu.VMEM((D, REGION), BF16)]
        if not last:
            outs = call(
                functools.partial(key_kernel, turn=turn, last=False),
                [((TOK, 3 * D), BF16), ((OWN, D), BF16), ((TOK, D), F32), ((TOK, D), BF16),
                 ((64, D), BF16), ((64, D), BF16)],
                where, *gs, *fixed, d_query, gradient if turn else cot, w_qkv, x, *state,
                scratch=scratch, flops=1 << 30,
            )
            state, sends = outs[:3], outs[3:]
    d_proj, g_low, d_in = state
    extra = jnp.concatenate([d_query, mixed], axis=0)
    early = call(
        functools.partial(early_kernel, turn=turn), [((8 * chips, 2 * D), BF16)] * cols,
        where, n_turned, d_query, mixed, gs[0], gs[1], routed(extra, mate), g_low,
        scratch=[pltpu.VMEM((OWN, D), F32), pltpu.VMEM((D, D), F32), pltpu.VMEM((OWN, D), BF16)],
        flops=1 << 28,
    )
    (d_kv,) = call(
        functools.partial(key_kernel, turn=turn, last=True), [((TOK, 2 * D), BF16)],
        where, *gs, *fixed, d_proj, scratch=scratch, flops=1 << 30,
    )
    early = list(early)
    early[0], d_kv_mate = lax.optimization_barrier((early[0], routed(d_kv, mate)))
    early = over_cols(early)
    late = list(call(
        late_kernel, [((8 * chips, 2 * D), BF16)] * cols, where, n_turned, d_kv, d_kv_mate,
        scratch=[pltpu.VMEM((OWN, 2 * D), F32)], flops=1 << 29,
    ))
    late[1], early[2] = lax.optimization_barrier((late[1], early[2]))
    late = over_cols(late)
    (d_in,) = call(
        functools.partial(input_kernel, turn=turn), [((TOK, D), F32)],
        where, d_query, d_kv, gradient, w_qkv, x, d_in, flops=1 << 28,
    )
    late[-1], d_in = lax.optimization_barrier((late[-1], d_in))
    (part,) = call(col_total_kernel, [((8 * chips, 4 * D), BF16)], where, *early, *late)
    part = part.reshape(chips, 8, 4 * D)
    part = lax.all_to_all(part, "z", 0, 0, tiled=True)
    qkv_part, out_part = call(
        functools.partial(total_kernel, scale=(row_total * col_total) ** (-0.5)),
        [((8, 3 * D), F32), ((8, D), F32)], where, part,
    )
    return d_in.reshape(1, 8, 16, D), qkv_part[None], out_part[None]


def solution(mesh):
    pipes, rows, cols = (mesh.shape[axis] for axis in ("pipe", "row", "col"))
    fine = Mesh(np.asarray(mesh.devices).reshape(pipes, rows // 2, 2, cols), AXES)
    row = ("z", "core")
    return jax.shard_map(
        functools.partial(body, (pipes, rows // 2, cols)),
        mesh=fine,
        in_specs=(
            P("pipe", row, "col", None),
            P("pipe", None, None),
            P("pipe", None, None),
            P(row, "col", None),
        ),
        out_specs=(
            P("pipe", row, "col", None),
            P("pipe", ("z", "core", "col"), None),
            P("pipe", ("z", "core", "col"), None),
        ),
        check_vma=False,
    )
```

```python
import functools

import jax
import jax.numpy as jnp
import numpy as np
from jax import lax
from jax.experimental import pallas as pl
from jax.experimental.pallas import tpu as pltpu
from jax.sharding import Mesh
from jax.sharding import PartitionSpec as P

F32 = jnp.float32
BF16 = jnp.bfloat16
AXES = ("pipe", "z", "core", "col")
D = 512
PAIRS = 4
TOK = 128
OWN = 256
REGION = 768
BLOCK = 32
VMEM_LIMIT = 40 * 1024 * 1024


def nn(a, b):
    return lax.dot_general(a, b, (((1,), (0,)), ((), ())), preferred_element_type=F32)


def nt(a, b):
    return lax.dot_general(a, b, (((1,), (1,)), ((), ())), preferred_element_type=F32)


def tn(a, b):
    return lax.dot_general(a, b, (((0,), (0,)), ((), ())), preferred_element_type=F32)


def two_heads(block):
    lane = lax.broadcasted_iota(jnp.int32, block.shape, 1)
    zero = jnp.zeros_like(block)
    return jnp.concatenate(
        [jnp.where(lane < 64, block, zero), jnp.where(lane < 64, zero, block)], axis=0
    )


def one_block(stacked):
    half = stacked.shape[0] // 2
    lane = lax.broadcasted_iota(jnp.int32, (half, 128), 1)
    return jnp.where(lane < 64, stacked[:half], stacked[half:])


def place(index, core):
    piece = index >> 8
    inner = index & 255
    side = inner - 128
    is_centre = inner < 128
    row = jnp.where(is_centre, inner >> 4, (side & 63) >> 3)
    col = jnp.where(is_centre, inner & 15, jnp.where(side < 64, (side & 7) - 8, (side & 7) + 16))
    mate = jnp.where(core == 0, 8, -8)
    row = row + jnp.where(piece == 1, mate, jnp.where(piece == 2, -mate, 0))
    return row, col


def window(where_ref, keys_own):
    row0, col0, core, rows, cols = (where_ref[i] for i in range(5))
    own = lax.broadcasted_iota(jnp.int32, (TOK, 1), 0)
    reach_row, reach_col = place(lax.broadcasted_iota(jnp.int32, (1, REGION), 1), core)
    grid_row, grid_col = row0 + reach_row, col0 + reach_col
    inside = (grid_row >= 0) & (grid_row < rows) & (grid_col >= 0) & (grid_col < cols)
    reach_row = jnp.where(inside, reach_row, 1 << 20)
    if keys_own:
        step_row, step_col = (own >> 4) - reach_row, (own & 15) - reach_col
    else:
        step_row, step_col = reach_row - (own >> 4), reach_col - (own & 15)
    return (step_row >= -8) & (step_row <= 7) & (step_col >= -8) & (step_col <= 7)


def put_sides(block, left_ref, right_ref):
    sides = block.reshape(8, 2, 8, block.shape[-1])
    left_ref[...] = sides[:, 0].reshape(64, -1).astype(BF16)
    right_ref[...] = sides[:, 1].reshape(64, -1).astype(BF16)


def normed_low(x_ref):
    x = x_ref[...].astype(F32)
    inverse = lax.rsqrt(jnp.mean(x * x, axis=-1, keepdims=True) + 1e-06)
    return (x * inverse).astype(BF16)


def centre_kernel(where_ref, x_ref, w_ref, base_ref, proj_ref, nlow_ref):
    base_ref[:TOK] = x_ref[...]
    base_ref[TOK:] = jnp.zeros((TOK, D), BF16)
    low = normed_low(x_ref)
    nlow_ref[...] = low
    proj_ref[...] = nn(low, w_ref[...]).astype(BF16)


def side_kernel(
    where_ref, left_ref, right_ref, w_ref, wo_ref, cot_ref, proj_ref, cot_low_ref, dm_ref
):
    low = jnp.concatenate([normed_low(left_ref), normed_low(right_ref)], axis=0)
    proj_ref[...] = nn(low, w_ref[...]).astype(BF16)
    grad = cot_ref[...].astype(BF16)
    cot_low_ref[...] = grad
    dm_ref[...] = nt(grad, wo_ref[...]).astype(BF16)


def forward_kernel(
    where_ref, x1, x2, proj_ref, side_ref, w_ref, cot_ref, dm_ref,
    kv_ref, prob_ref, nlow_ref, far_ref, mixed_ref, pack_ref, left_ref, right_ref,
):
    kv_ref[:TOK] = proj_ref[:, D:]
    kv_ref[TOK:OWN] = side_ref[:, D:]
    for piece, x_ref in enumerate((x1, x2)):
        low = normed_low(x_ref)
        far_ref[piece * OWN : (piece + 1) * OWN] = low
        if piece == 0:
            nlow_ref[...] = low[:TOK]
        kv_ref[(piece + 1) * OWN : (piece + 2) * OWN] = nn(low, w_ref[:, D:]).astype(BF16)
    ok = window(where_ref, False)
    ok2 = jnp.concatenate([ok, ok], axis=0)
    lane = lax.broadcasted_iota(jnp.int32, (TOK, 128), 1)
    stats = jnp.zeros((TOK, 128), F32)
    for pair in range(PAIRS):
        at = slice(128 * pair, 128 * pair + 128)
        query = two_heads(proj_ref[:, at] * 0.125)
        scores = nt(query, kv_ref[:, at])
        scores = jnp.where(ok2, scores, -1e30)
        highest = jnp.max(scores, axis=-1, keepdims=True)
        grown = jnp.exp(scores - highest)
        total = jnp.sum(grown, axis=-1, keepdims=True)
        probs = (grown * (1.0 / total)).astype(BF16)
        prob_ref[pair] = probs
        value = kv_ref[:, D + 128 * pair : D + 128 * pair + 128]
        mixed = one_block(nn(probs, value)).astype(BF16)
        mixed_ref[:, at] = mixed
        log_total = highest + jnp.log(total)
        delta = two_sums(dm_ref[:, at], mixed)
        for first, rest in ((0, log_total), (24, delta)):
            for part in range(3):
                piece = rest.astype(BF16).astype(F32)
                rest = rest - piece
                for head in range(2):
                    chosen = lane == first + 8 * part + 2 * pair + head
                    stats = jnp.where(chosen, piece[TOK * head : TOK * head + TOK], stats)
    starts = where_ref[5] == 0
    pack_ref[:, D:] = stats.astype(BF16)

    @pl.when(starts)
    def _():
        pack_ref[:, :D] = cot_ref[...]

    @pl.when(jnp.logical_not(starts))
    def _():
        pack_ref[:, :D] = mixed_ref[...]

    put_sides(pack_ref[...].astype(F32), left_ref, right_ref)


def turned_kernel(where_ref, proj_ref, side_ref, far_ref, w_ref, n0, n1, query_ref, nt_ref, full_ref):
    query_ref[:, :TOK] = proj_ref[:, :D].astype(F32).T.astype(BF16)
    query_ref[:, TOK:OWN] = side_ref[:, :D].astype(F32).T.astype(BF16)
    far = nn(far_ref[...], w_ref[:, :D]).astype(BF16)
    query_ref[:, OWN:] = far.astype(F32).T.astype(BF16)
    full_ref[:, :TOK] = n0[...].astype(F32).T
    full_ref[:, TOK:] = n1[...].astype(F32).T
    nt_ref[...] = own_half(where_ref, full_ref).astype(BF16)


def own_half(where_ref, full_ref):
    rows = [
        full_ref[pl.ds(pl.multiple_of((2 * at + where_ref[2]) * BLOCK, BLOCK), BLOCK)]
        for at in range(full_ref.shape[0] // (2 * BLOCK))
    ]
    return jnp.concatenate(rows, axis=0)


def key_probs_kernel(
    where_ref, p0, p1, p2, proj_ref, query_ref, prob_ref, mixed_ref, delta_ref, total_ref
):
    head = lax.broadcasted_iota(jnp.int32, (8, 128), 0)
    lane = lax.broadcasted_iota(jnp.int32, (8, 128), 1)
    stats = jnp.concatenate([p[:, D:] for p in (p0, p1, p2)], axis=0)
    sums = []
    for first in (0, 24):
        chosen = ((lane & 7) == head) & (lane >= first) & (lane < first + 24)
        sums.append(nt(jnp.where(chosen, 1.0, 0.0).astype(BF16), stats))
    log_total, delta_ref[...] = sums

    @pl.when(where_ref[5] != 0)
    def _():
        for piece, p in enumerate((p0, p1, p2)):
            mixed_ref[:, piece * OWN : (piece + 1) * OWN] = p[:, :D].astype(F32).T.astype(BF16)

    total_ref[...] = log_total
    ok = window(where_ref, True)

    def one_pair(pair, carry):
        low = pl.multiple_of(128 * pair, 128)
        key = two_heads(proj_ref[:, pl.ds(low + D, 128)] * 0.125)
        scores = nn(key, query_ref[pl.ds(low, 128)])
        for side in range(2):
            part = scores[TOK * side : TOK * side + TOK] - total_ref[pl.ds(2 * pair + side, 1)]
            probs = jnp.exp(jnp.where(ok, part, -1e30))
            prob_ref[pair, TOK * side : TOK * side + TOK] = probs.astype(BF16)
        return carry

    lax.fori_loop(0, PAIRS, one_pair, 0)


def two_sums(grad, mixed):
    prod = grad.astype(F32) * mixed.astype(F32)
    lane = lax.broadcasted_iota(jnp.int32, prod.shape, 1)
    return jnp.concatenate(
        [
            jnp.sum(jnp.where(lane < 64, prod, 0.0), axis=-1, keepdims=True),
            jnp.sum(jnp.where(lane < 64, 0.0, prod), axis=-1, keepdims=True),
        ],
        axis=0,
    )


def query_kernel(
    where_ref, g_ref, w_ref, mixed_ref, kv_ref, prob_ref, *rest, turn
):
    (dq_ref, dm_ref), prev = rest[-2:], rest[:-2]
    for ref in prev:

        @pl.when(where_ref[5] != turn)
        def _():
            dq_ref[...] = ref[:, :D]

    @pl.when(where_ref[5] == turn)
    def _():
        dm_ref[...] = nt(g_ref[...], w_ref[...]).astype(BF16)

        def one_pair(pair, carry):
            low = pl.multiple_of(128 * pair, 128)
            at = pl.ds(low, 128)
            grad = dm_ref[:, at]
            delta = two_sums(grad, mixed_ref[:, at])
            pressure = nt(two_heads(grad), kv_ref[:, pl.ds(low + D, 128)])
            slopes = (prob_ref[pair].astype(F32) * (pressure - delta)).astype(BF16)
            dq_ref[:, at] = (one_block(nn(slopes, kv_ref[:, at])) * 0.125).astype(BF16)
            return carry

        lax.fori_loop(0, PAIRS, one_pair, 0, unroll=2 if turn else 1)


def turned_block(stacked):
    row = lax.broadcasted_iota(jnp.int32, (128, 128), 0)
    return jnp.where(row < 64, stacked[:, :128], stacked[:, 128:]).T


def key_kernel(
    where_ref, g0, g1, g2, wo_ref, delta_ref, proj_ref, query_ref, prob_ref, *rest, turn, last
):
    ins, rest = ((), rest) if last else (rest[:4], rest[4:])
    count = 1 if last else 3
    prev, rest = (rest[:count], rest[count:]) if turn else ((), rest)
    outs, sends, dm_ref = rest[:count], rest[count:-1], rest[-1]
    kv_ref = outs[0] if last else outs[0].at[:, D:]
    active = where_ref[5] == turn

    if prev:

        @pl.when(jnp.logical_not(active))
        def _():
            for new, old in zip(outs, prev):
                new[...] = old[:, D:] if last else old[...]

    @pl.when(active)
    def _():
        for piece, g in enumerate((g0, g1, g2)):
            d_mixed = nt(wo_ref[...], g[:, :D]).astype(BF16)
            dm_ref[:, piece * OWN : (piece + 1) * OWN] = d_mixed

        def one_pair(pair, carry):
            low = pl.multiple_of(128 * pair, 128)
            at = pl.ds(low, 128)
            value = two_heads(proj_ref[:, pl.ds(low + 2 * D, 128)])
            grad = dm_ref[at]
            if turn:
                prod = grad.astype(F32) * delta_ref[at].astype(F32)
                deltas = [jnp.sum(prod[r : r + 64], axis=0, keepdims=True) for r in (0, 64)]
            else:
                deltas = [delta_ref[pl.ds(2 * pair + side, 1)] for side in range(2)]
            pressure = nn(value, grad)
            probs = prob_ref[pair]
            d_value = nt(grad, probs)
            slopes = []
            for side in range(2):
                rows = slice(TOK * side, TOK * side + TOK)
                slopes.append(
                    (probs[rows].astype(F32) * (pressure[rows] - deltas[side])).astype(BF16)
                )
            d_key = nt(query_ref[at], jnp.concatenate(slopes, axis=0))
            kv_ref[:, at] = (turned_block(d_key) * 0.125).astype(BF16)
            kv_ref[:, pl.ds(low + D, 128)] = turned_block(d_value).astype(BF16)
            return carry

        lax.fori_loop(0, PAIRS, one_pair, 0, unroll=2)
        if not last:
            dq_ref, *ins_rest = ins
            outs[0][:, :D] = dq_ref[...]
            outs[1][:TOK] = g0[:TOK, :D]
            outs[1][TOK:] = g1[:TOK, :D]
            out = input_grad(nt(outs[0][...], ins_rest[1][...]), ins_rest[0], ins_rest[2])
            outs[2][...] = out
            low_ref, left_ref, right_ref = sends
            low_ref[...] = out.astype(BF16)
            put_sides(out, left_ref, right_ref)


def input_grad(d_normed, g_ref, x_ref):
    x = x_ref[...].astype(F32)
    inverse = lax.rsqrt(jnp.mean(x * x, axis=-1, keepdims=True) + 1e-06)
    normed = x * inverse
    inner = jnp.mean(d_normed * normed, axis=-1, keepdims=True)
    return g_ref[...].astype(F32) + inverse * (d_normed - normed * inner)


def input_kernel(where_ref, dq_ref, kv_ref, g_ref, wq_ref, x_ref, prev_ref, in_ref, *, turn):
    @pl.when(where_ref[5] == turn)
    def _():
        d_normed = nt(dq_ref[...], wq_ref[:, :D]) + nt(kv_ref[...], wq_ref[:, D:])
        in_ref[...] = input_grad(d_normed, g_ref, x_ref)

    @pl.when(where_ref[5] != turn)
    def _():
        in_ref[...] = prev_ref[...]


def split_rows(where_ref, parts, outs):
    cols = len(outs)
    for distance, out_ref in enumerate(outs):
        col = lax.rem(where_ref[6] + distance, cols)
        for at, ref, step, first in parts:
            rows = [
                ref[pl.ds(pl.multiple_of(step * chip + first + 8 * col, 8), 8)]
                for chip in range(out_ref.shape[0] // 8)
            ]
            out_ref[:, at] = jnp.concatenate(rows, axis=0).astype(BF16)


def early_kernel(where_ref, nt_ref, dq_ref, mixed_ref, g0, g1, m, prev_ref, *refs, turn):
    outs, (left_ref, full_ref, g_ref) = refs[:-3], refs[-3:]

    @pl.when(where_ref[5] == turn)
    def _():
        g_ref[:TOK] = g0[:TOK]
        g_ref[TOK:] = g1[:TOK]

    @pl.when(where_ref[5] != turn)
    def _():
        g_ref[...] = prev_ref[...]

    d_query = jnp.concatenate([dq_ref[...], m[:TOK]], axis=0)
    left_ref[...] = nn(nt_ref[...], d_query)
    mixed = jnp.concatenate([mixed_ref[...], m[TOK:]], axis=0)
    full_ref[...] = tn(mixed, g_ref[...])
    split_rows(
        where_ref,
        [(slice(0, D), left_ref, BLOCK, 0), (slice(D, 2 * D), full_ref, 2 * BLOCK, where_ref[2] * BLOCK)],
        outs,
    )


def late_kernel(where_ref, nt_ref, d0, d1, *refs):
    outs, left_ref = refs[:-1], refs[-1]
    left_ref[...] = nn(nt_ref[...], jnp.concatenate([d0[...], d1[...]], axis=0))
    split_rows(where_ref, [(slice(0, 2 * D), left_ref, BLOCK, 0)], outs)


def col_total_kernel(where_ref, *refs):
    count = (len(refs) - 1) // 2
    for at, parts in ((slice(0, 2 * D), refs[:count]), (slice(2 * D, 4 * D), refs[count:-1])):
        total = parts[0][...].astype(F32)
        for ref in parts[1:]:
            total = total + ref[...].astype(F32)
        refs[-1][:, at] = total.astype(BF16)


def total_kernel(where_ref, part_ref, qkv_ref, out_ref, *, scale):
    total = part_ref[0].astype(F32)
    for source in range(1, part_ref.shape[0]):
        total = total + part_ref[source].astype(F32)
    qkv_ref[:, :D] = total[:, :D] * scale
    qkv_ref[:, D:] = total[:, 2 * D :] * scale
    out_ref[...] = total[:, D : 2 * D] * scale


def call(kernel, outs, *args, scratch=(), flops=0, moved=4 << 20):
    vmem = pl.BlockSpec(memory_space=pltpu.VMEM)
    return pl.pallas_call(
        kernel,
        out_shape=[jax.ShapeDtypeStruct(s, t) for s, t in outs],
        in_specs=[pl.BlockSpec(memory_space=pltpu.SMEM)] + [vmem] * (len(args) - 1),
        out_specs=[vmem] * len(outs),
        scratch_shapes=list(scratch),
        compiler_params=pltpu.CompilerParams(vmem_limit_bytes=VMEM_LIMIT),
        cost_estimate=pl.CostEstimate(flops=flops, bytes_accessed=moved, transcendentals=0),
    )(*args)


def body(sizes, activations, qkv_weight, out_weight, cotangent):
    pipes, chips, cols = sizes

    def routed(block, step):
        pairs = []
        for p in range(pipes):
            for r in range(2 * chips):
                for c in range(cols):
                    p2, r2, c2 = step(p, r, c)
                    target = ((p2 % pipes) * 2 * chips + r2 % (2 * chips)) * cols + c2 % cols
                    pairs.append(((p * 2 * chips + r) * cols + c, target))
        return lax.ppermute(block, AXES, pairs)

    def col_rims(left_half, right_half, down=0):
        left = routed(right_half, lambda p, r, c: (p - down, r, c + 1))
        right = routed(left_half, lambda p, r, c: (p - down, r, c - 1))
        return left, right

    def mate(p, r, c):
        return p, r ^ 1, c

    def row_rims(pieces):
        own = jnp.concatenate(pieces, axis=0)
        beyond = routed(own, lambda p, r, c: (p, r - 1 + 2 * (r & 1), c))
        return own, routed(own, mate), beyond

    pipe, z, core, col = (lax.axis_index(axis) for axis in AXES)
    x = activations.reshape(TOK, D)
    w_qkv, w_out = qkv_weight[0], out_weight[0]
    cot = cotangent.reshape(TOK, D)
    row_total, col_total = 16 * chips, 16 * cols
    where = jnp.stack(
        [8 * (2 * z + core), 16 * col, core, row_total, col_total, pipes - 1 - pipe, col]
    ).astype(jnp.int32)

    x_sides = x.reshape(8, 2, 8, D)
    low_side, high_side = x_sides[:, 0].reshape(64, D), x_sides[:, 1].reshape(64, D)
    base, proj, nlow = call(
        centre_kernel, [((OWN, D), BF16), ((TOK, 3 * D), BF16), ((TOK, D), BF16)],
        where, x, w_qkv, flops=1 << 28,
    )
    left, right = col_rims(low_side, high_side)
    own = lax.dynamic_update_slice(base, left, (TOK, 0))
    own, near, far = row_rims([lax.dynamic_update_slice(own, right, (TOK + 64, 0))])
    side_proj, cot_low, d_mixed = call(
        side_kernel, [((TOK, 3 * D), BF16), ((TOK, D), BF16), ((TOK, D), BF16)],
        where, left, right, w_qkv, w_out, cot, flops=1 << 28,
    )
    wide = D + 128
    kv, q_probs, nlow_mate, low_far, mixed, pack, low_side, high_side = call(
        forward_kernel,
        [((REGION, 2 * D), BF16), ((PAIRS, OWN, REGION), BF16), ((TOK, D), BF16),
         ((2 * OWN, D), BF16), ((TOK, D), BF16), ((TOK, wide), BF16), ((64, wide), BF16),
         ((64, wide), BF16)],
        where, near, far, proj, side_proj, w_qkv, cot_low, d_mixed, flops=2 << 30,
    )
    sides = col_rims(low_side, high_side)
    queries, n_turned = call(
        turned_kernel, [((D, REGION), BF16), ((OWN, OWN), BF16)],
        where, proj, side_proj, low_far, w_qkv, nlow, nlow_mate,
        scratch=[pltpu.VMEM((D, OWN), F32)], flops=1 << 28,
    )

    def query_side(turn, gradient, *prev):
        return call(
            functools.partial(query_kernel, turn=turn), [((TOK, D), BF16)],
            where, gradient, w_out, mixed, kv, q_probs, *prev,
            scratch=[pltpu.VMEM((TOK, D), BF16)], flops=1 << 29,
        )[0]

    d_query = query_side(0, cot_low)
    left, right = sides
    right, queries, d_query = lax.optimization_barrier((right, queries, d_query))
    packs = row_rims([pack, left, right])
    k_probs, mixed_turned, delta = call(
        key_probs_kernel,
        [((PAIRS, OWN, REGION), BF16), ((D, REGION), BF16), ((8, REGION), F32)],
        where, *packs, proj, queries, scratch=[pltpu.VMEM((8, REGION), F32)], flops=1 << 28,
    )
    gradient, gs = cot_low, packs
    def over_cols(parts):
        moved = list(parts)
        for distance in sorted(range(1, cols), key=lambda d: -min(d, cols - d)):
            moved[distance] = routed(parts[distance], lambda p, r, c: (p, r, c + distance))
        return moved

    state = ()
    for turn in range(pipes):
        last = turn == pipes - 1
        if turn > 0:
            low, low_side, high_side = sends
            gradient = routed(low, lambda p, r, c: (p - 1, r, c))
            left, right = col_rims(low_side, high_side, 1)
            gs = row_rims([gradient, left, right])
            d_query = query_side(turn, gradient, *((state[0],) if last else ()))
        fixed = (w_out, mixed_turned if turn else delta, proj, queries, k_probs)
        scratch = [pltpu.VMEM((D, REGION), BF16)]
        if not last:
            outs = call(
                functools.partial(key_kernel, turn=turn, last=False),
                [((TOK, 3 * D), BF16), ((OWN, D), BF16), ((TOK, D), F32), ((TOK, D), BF16),
                 ((64, D), BF16), ((64, D), BF16)],
                where, *gs, *fixed, d_query, gradient if turn else cot, w_qkv, x, *state,
                scratch=scratch, flops=1 << 30,
            )
            state, sends = outs[:3], outs[3:]
    d_proj, g_low, d_in = state
    extra = jnp.concatenate([d_query, mixed], axis=0)
    early = call(
        functools.partial(early_kernel, turn=turn), [((8 * chips, 2 * D), BF16)] * cols,
        where, n_turned, d_query, mixed, gs[0], gs[1], routed(extra, mate), g_low,
        scratch=[pltpu.VMEM((OWN, D), F32), pltpu.VMEM((D, D), F32), pltpu.VMEM((OWN, D), BF16)],
        flops=1 << 28,
    )
    (d_kv,) = call(
        functools.partial(key_kernel, turn=turn, last=True), [((TOK, 2 * D), BF16)],
        where, *gs, *fixed, d_proj, scratch=scratch, flops=1 << 30,
    )
    early = list(early)
    early[0], d_kv_mate = lax.optimization_barrier((early[0], routed(d_kv, mate)))
    early = over_cols(early)
    late = list(call(
        late_kernel, [((8 * chips, 2 * D), BF16)] * cols, where, n_turned, d_kv, d_kv_mate,
        scratch=[pltpu.VMEM((OWN, 2 * D), F32)], flops=1 << 29,
    ))
    late[1], early[2] = lax.optimization_barrier((late[1], early[2]))
    late = over_cols(late)
    (d_in,) = call(
        functools.partial(input_kernel, turn=turn), [((TOK, D), F32)],
        where, d_query, d_kv, gradient, w_qkv, x, d_in, flops=1 << 28,
    )
    late[-1], d_in = lax.optimization_barrier((late[-1], d_in))
    (part,) = call(col_total_kernel, [((8 * chips, 4 * D), BF16)], where, *early, *late)
    part = part.reshape(chips, 8, 4 * D)
    part = lax.all_to_all(part, "z", 0, 0, tiled=True)
    qkv_part, out_part = call(
        functools.partial(total_kernel, scale=(row_total * col_total) ** (-0.5)),
        [((8, 3 * D), F32), ((8, D), F32)], where, part,
    )
    return d_in.reshape(1, 8, 16, D), qkv_part[None], out_part[None]


def solution(mesh):
    pipes, rows, cols = (mesh.shape[axis] for axis in ("pipe", "row", "col"))
    fine = Mesh(np.asarray(mesh.devices).reshape(pipes, rows // 2, 2, cols), AXES)
    row = ("z", "core")
    return jax.shard_map(
        functools.partial(body, (pipes, rows // 2, cols)),
        mesh=fine,
        in_specs=(
            P("pipe", row, "col", None),
            P("pipe", None, None),
            P("pipe", None, None),
            P(row, "col", None),
        ),
        out_specs=(
            P("pipe", row, "col", None),
            P("pipe", ("z", "core", "col"), None),
            P("pipe", ("z", "core", "col"), None),
        ),
        check_vma=False,
    )
```
